256 devices in a mesh: gx: 4 (over x), gy: 8 (over z), gz: 8 (over y, core).
Axes of the slice: x: 4, y: 4, z: 8, core: 2. Of those that a mesh axis runs over, the one named last changes fastest.
Arguments:
- right_side: float32 [64, 128, 1024], P('gx', 'gy', 'gz'), may hold values from -8 to 8
- classes: int32 [64, 128, 1024], P('gx', 'gy', 'gz'), may hold values from 0 to 15
- table: float32 [16], replicated, may hold values from 0.001 to 0.5
Outputs:
- solution_field: float32 [64, 128, 1024], P('gx', 'gy', 'gz')
- residual: float32 [64, 128, 1024], P('gx', 'gy', 'gz')
The draws below stay inside these ranges and needn't reach their ends.
All inputs are finite; a program needn't handle non-finite values.
Results may differ from the reference program's by a relative error of at most 0.0003.
Values sent between devices are 32-bit elements; how exact they have to be, the bound alone decides.
No kernel may reach another device: no remote copies, remote signals or barrier semaphores. Data moves between devices by JAX's collectives and lax.ppermute only.
A program may use at most 64 MiB of HBM per device.

```python
import math
import jax
import jax.numpy as jnp

CLASSES = 16
ITERS = 3
COARSE_SWEEPS = 6
NX = 64
NY = 128
NZ = 1024


def draw_right_side(key, part):
    key = jax.random.fold_in(key, 11)
    first, second = jax.random.split(key, 2)
    ramp_x = jnp.arange(NX, dtype=jnp.float32)[:, None, None] / NX
    ramp_y = jnp.arange(NY, dtype=jnp.float32)[None, :, None] / NY
    ramp_z = jnp.arange(NZ, dtype=jnp.float32)[None, None, :] / NZ
    ramp = 1.0 + (ramp_x + ramp_y + ramp_z) * (2.0 / 3.0)
    noise = jax.random.normal(first, (NX, NY, NZ), jnp.float32)
    spread = jnp.exp(jax.random.uniform(second, (NX, NY, NZ), jnp.float32) * math.log(3.0))
    values = noise * spread * 0.6 * ramp
    return jnp.clip(values, -8.0, 8.0).astype(jnp.float32)


def place_ends(entries, stream_key, low, high):
    extent = entries.shape
    place = [jax.random.randint(jax.random.fold_in(stream_key, axis), (), 0, extent[axis]) for axis in range(len(extent))]
    entries = entries.at[tuple(place)].set(low)
    longest = extent.index(max(extent))
    place[longest] = (place[longest] + 1) % extent[longest]
    return entries.at[tuple(place)].set(high)


def setup_inputs(seed: int = 0) -> dict:
    arg_keys = jax.random.split(jax.random.key(seed), 4)
    return {
        "right_side": draw_right_side(jax.random.fold_in(arg_keys[3], 71), 0),
        "classes": place_ends(jax.random.randint(arg_keys[1], (NX, NY, NZ), 0, CLASSES), jax.random.fold_in(arg_keys[1], 1), 0, CLASSES - 1).astype(jnp.int32),
        "table": jnp.clip(jnp.exp(jax.random.uniform(arg_keys[2], (CLASSES,), jnp.float32, math.log(0.001), math.log(0.5))), 0.001, 0.5),
    }


OMEGA = 0.8


def lookup(classes, table):
    kap = jnp.zeros(classes.shape, jnp.float32)
    for index in range(CLASSES):
        kap = kap + jnp.where(classes == index, table[index], jnp.float32(0.0))
    return kap


def restrict(v):
    a, b, c = v.shape
    return jnp.mean(v.reshape(a // 2, 2, b // 2, 2, c // 2, 2), axis=(1, 3, 5))


def prolong(v):
    return jnp.repeat(jnp.repeat(jnp.repeat(v, 2, axis=0), 2, axis=1), 2, axis=2)


def neighbours(padded):
    beside = padded[2:, 1:-1, 1:-1] + padded[:-2, 1:-1, 1:-1]
    beside = beside + padded[1:-1, 2:, 1:-1] + padded[1:-1, :-2, 1:-1]
    beside = beside + padded[1:-1, 1:-1, 2:] + padded[1:-1, 1:-1, :-2]
    return beside


def operate(u, kap, scale):
    return (kap + 6.0 * scale) * u - scale * neighbours(jnp.pad(u, 1))


def vcycle(r, kaps, diags):
    x0 = OMEGA * r / diags[0]
    r1 = restrict(r - operate(x0, kaps[0], 1.0))
    x1 = OMEGA * r1 / diags[1]
    r2 = restrict(r1 - operate(x1, kaps[1], 0.25))
    x2 = OMEGA * r2 / diags[2]
    for sweep in range(COARSE_SWEEPS - 1):
        x2 = x2 + OMEGA * (r2 - operate(x2, kaps[2], 0.0625)) / diags[2]
    x1 = x1 + prolong(x2)
    x1 = x1 + OMEGA * (r1 - operate(x1, kaps[1], 0.25)) / diags[1]
    x0 = x0 + prolong(x1)
    return x0 + OMEGA * (r - operate(x0, kaps[0], 1.0)) / diags[0]


def reference(right_side, classes, table):
    kap0 = lookup(classes, table)
    kap1 = restrict(kap0)
    kap2 = restrict(kap1)
    kaps = (kap0, kap1, kap2)
    diags = (kap0 + 6.0, kap1 + 6.0 * 0.25, kap2 + 6.0 * 0.0625)
    solution_field = jnp.zeros_like(right_side)
    residual = right_side
    precond = vcycle(residual, kaps, diags)
    direction = precond
    rz_now = jnp.sum(residual * precond)
    for step in range(ITERS):
        image = operate(direction, kap0, 1.0)
        alpha = rz_now / jnp.sum(direction * image)
        solution_field = solution_field + alpha * direction
        residual = residual - alpha * image
        if step + 1 < ITERS:
            precond = vcycle(residual, kaps, diags)
            rz_next = jnp.sum(residual * precond)
            direction = precond + (rz_next / rz_now) * direction
            rz_now = rz_next
    return solution_field, residual
```

```python
import jax
import jax.numpy as jnp
from jax import lax
from jax.experimental import pallas as pl
from jax.experimental.pallas import tpu as pltpu
from jax.sharding import PartitionSpec as P

CLASSES = 16
COARSE_SWEEPS = 6
OMEGA = 0.8
KEEP = 1.0 - OMEGA
F32 = jnp.float32
SLABS, MIDS = 26, 12
VMEM = pl.BlockSpec(memory_space=pltpu.VMEM)
SMEM = pl.BlockSpec(memory_space=pltpu.SMEM)


def iota(shape, dim):
    return lax.broadcasted_iota(jnp.int32, shape, dim)


def roll(v, shift, axis):
    shift = shift % v.shape[axis]
    return v if shift == 0 else pltpu.roll(v, shift, axis)


def around(v, rows, lanes):
    return (roll(v, rows, 0) + roll(v, -rows, 0)) + (roll(v, lanes, 1) + roll(v, -lanes, 1))


def pair_mean(v, step):
    rows = (iota(v.shape, 0) // step) % 2 == 0
    v = v + jnp.where(rows, roll(v, -step, 0), roll(v, step, 0))
    lanes = (iota(v.shape, 1) // step) % 2 == 0
    v = v + jnp.where(lanes, roll(v, -step, 1), roll(v, step, 1))
    return v * 0.125


def pack_fine(read, low_ref, high_ref):
    chunk = iota((16, 128), 1) // 8
    low = high = jnp.zeros((16, 128), F32)
    for k in range(16):
        v = read(k)
        low = jnp.where(chunk == k, roll(v, 8 * k, 1), low)
        high = jnp.where(chunk == k, roll(v, 8 * k + 8, 1), high)
    low_ref[...] = low
    high_ref[...] = high


def prepare_kernel(rhs, classes, table, kap, low, high):
    for k in range(16):
        c = classes[k]
        v = jnp.zeros((16, 128), F32)
        for index in range(CLASSES):
            v = jnp.where(c == index, table[index], v)
        kap[k] = v
    pack_fine(lambda k: rhs[k], low.at[0], high.at[0])
    pack_fine(lambda k: kap[k], low.at[1], high.at[1])


def slab_sources(i):
    x = i - 5
    if x < 0:
        return 18 + x + 5, 23, 24, 16 + x
    if x < 16:
        return x, 16, 17, x
    return 25 + x - 16, 30, 31, x - 16


def assemble_fine(body, upper, lower, i):
    def unit(u):
        return jnp.concatenate([body[u], upper[u], lower[u]], axis=0)

    main, above, below, k = slab_sources(i)
    lane = iota((32, 128), 1)
    side = jnp.where(lane >= 120, roll(unit(below), 120 - 8 * k, 1), 0.0)
    side = jnp.where(lane < 8, roll(unit(above), -8 * k, 1), side)
    return jnp.concatenate([unit(main), side], axis=1)


def inside_fine(place, sizes):
    row, lane = iota((32, 256), 0), iota((32, 256), 1)
    y = jnp.where(row < 24, row, row - 32) + 16 * place[1]
    z = jnp.where(lane < 192, lane, lane - 256) + 128 * place[2]
    near = (lane < 136) | (lane >= 248)
    return near & (y >= 0) & (y < 16 * sizes[1]) & (z >= 0) & (z < 128 * sizes[2])


def fine_weights(place, sizes, body, upper, lower, weight0, weight1, middle, quads, weight2):
    inside = inside_fine(place, sizes)
    for m in range(MIDS):
        pair = None
        for i in (2 * m + 1, 2 * m + 2):
            kap = assemble_fine(body, upper, lower, i)
            x = 16 * place[0] + (i - 5)
            weight0[i] = jnp.where(inside & (x >= 0) & (x < 16 * sizes[0]), OMEGA / (kap + 6.0), 0.0)
            pair = kap if pair is None else pair + kap
        kap1 = pair_mean(pair, 1)
        middle[m] = kap1
        x = 8 * place[0] + (m - 2)
        weight1[m] = jnp.where(inside & (x >= 0) & (x < 8 * sizes[0]), OMEGA / (kap1 + 1.5), 0.0)
    for i in (0, SLABS - 1):
        kap = assemble_fine(body, upper, lower, i)
        x = 16 * place[0] + (i - 5)
        weight0[i] = jnp.where(inside & (x >= 0) & (x < 16 * sizes[0]), OMEGA / (kap + 6.0), 0.0)
    for c in range(4):
        kap2 = pair_mean(middle[2 + 2 * c] + middle[3 + 2 * c], 2)[:16, :128]
        quads[c] = OMEGA / (kap2 + 0.375)
    pack_coarse(quads, weight2, 0)


def pack_coarse(quads, out, base):
    row, chunk = iota((8, 128), 0), iota((8, 128), 1) // 32
    ends = jnp.zeros((8, 128), F32)
    rows = [quads[c, pl.ds(0, 4, stride=4), :] for c in range(4)]
    for c in range(4):
        both = jnp.concatenate([rows[c], rows[c]], axis=0)
        both = jnp.where(row < 4, roll(both, 32 * c, 1), roll(both, 32 * c + 32, 1))
        ends = jnp.where(chunk == c, both, ends)
    out[base] = jnp.concatenate(rows[:2], axis=0)
    out[base + 1] = jnp.concatenate(rows[2:], axis=0)
    out[base + 2] = ends


def down_sweep(body, upper, lower, weight0, weight1, x0, x1, unit, r, r1, quads):
    for i in range(SLABS):
        v = assemble_fine(body, upper, lower, i)
        r[i] = v
        x0[i] = weight0[i] * v
    for m in range(MIDS):
        i = 2 * m + 1
        two = x0[i] + x0[i + 1]
        left = KEEP * (r[i] + r[i + 1]) + ((x0[i - 1] + x0[i + 2]) + two) + around(two, 1, 1)
        v = pair_mean(left, 1)
        r1[m] = v
        x1[m] = weight1[m] * v
    for c in range(4):
        m = 2 + 2 * c
        two = x1[m] + x1[m + 1]
        left = KEEP * (r1[m] + r1[m + 1]) + 0.25 * (((x1[m - 1] + x1[m + 2]) + two) + around(two, 2, 2))
        quads[c] = pair_mean(left, 2)[:16, :128]
    pack_coarse(quads, unit, 0)


def first_down_kernel(sizes, place, body, upper, lower, kbody, kupper, klower, weight0, weight1, x0, x1, unit, r, r1, quads):
    fine_weights(place, sizes, kbody, kupper, klower, weight0, weight1, r1, quads, unit.at[pl.ds(3, 3)])
    down_sweep(body, upper, lower, weight0, weight1, x0, x1, unit, r, r1, quads)


def down_kernel(body, upper, lower, weight0, weight1, x0, x1, unit, r, r1, quads):
    down_sweep(body, upper, lower, weight0, weight1, x0, x1, unit, r, r1, quads)


def assemble_coarse(place, blocks, base, out, first, change):
    own, up1, down1, up2, down2 = blocks
    lane = iota((16, 128), 1)
    for k in range(4):
        def rows(t, s):
            parts = [own[k, t, s:s + 4], up1[k, t, s:s + 4], up2[k, t, s:s + 2], down2[k, t, s + 2:s + 4], down1[k, t, s:s + 4]]
            return jnp.concatenate(parts, axis=0)

        above, below = rows(base + 2, 0), rows(base + 2, 4)
        start = 4 * lax.rem(place[0] + k, 4) + first
        for s in range(4):
            side = jnp.where(lane >= 96, roll(below, 96 - 32 * s, 1), 0.0)
            side = jnp.where(lane < 32, roll(above, -32 * s, 1), side)
            v = jnp.concatenate([rows(base + s // 2, 4 * (s % 2)), side], axis=1)
            out[start + s] = change(start + s, v)


def up_sweep(place, blocks, weight2, weight1, weight0, x0, x1, kap, u, w, low, high, a, b, rhs2, spread, middle, t1, t0):
    zero = jnp.zeros((16, 256), F32)
    for ref in (a, b):
        ref[0] = zero
        ref[17] = zero
    assemble_coarse(place, blocks, 0, rhs2, 1, lambda s, v: weight2[s] * v)
    for s in range(1, 17):
        a[s] = rhs2[s]
    for sweep in range(COARSE_SWEEPS - 1):
        old, new = (a, b) if sweep % 2 == 0 else (b, a)

        def step(s, carry, old=old, new=new):
            v = old[s]
            beside = (old[s - 1] + old[s + 1]) + around(v, 1, 4)
            new[s] = (KEEP * v + rhs2[s]) + weight2[s] * (0.0625 * beside)
            return carry

        lax.fori_loop(1, 17, step, 0, unroll=4)
    last = b if COARSE_SWEEPS % 2 == 0 else a
    half = iota((8, 256), 0) < 4
    for c in range(6):
        v = last[4 * place[0] + c]
        spread[c] = jnp.concatenate(
            [
                jnp.where(half, jnp.broadcast_to(v[j:j + 1], (8, 256)), jnp.broadcast_to(v[j + 1:j + 2], (8, 256)))
                for j in (0, 2, 4, 14)
            ],
            axis=0,
        )
    for m in range(MIDS):
        t1[m] = x1[m] + spread[m // 2]
    for m in range(1, MIDS - 1):
        v = t1[m]
        beside = (t1[m - 1] + t1[m + 1]) + around(v, 2, 2)
        middle[m] = (KEEP * v + x1[m]) + weight1[m] * (0.25 * beside)
    for i in range(3, SLABS - 3):
        t0[i] = x0[i] + middle[(i - 1) // 2]
    for i in range(4, SLABS - 4):
        v = t0[i]
        beside = (t0[i - 1] + t0[i + 1]) + around(v, 1, 1)
        middle_v = (KEEP * v + x0[i]) + weight0[i] * beside
        u[i] = middle_v
    for i in range(5, SLABS - 5):
        v = u[i]
        beside = (u[i - 1] + u[i + 1]) + around(v, 1, 1)
        w[i - 5] = (kap[i - 5] + 6.0) * v[:16, :128] - beside[:16, :128]
    pack_fine(lambda k: w[k], low, high)


def lanes_of(values, shape=(8, 128)):
    lane = iota(shape, 1)
    out = jnp.zeros(shape, F32)
    for k, v in enumerate(values):
        out = jnp.where(lane == k, jnp.sum(v), out)
    return out


def first_up_kernel(place, sizes, *refs):
    (own, up1, down1, up2, down2, weight1, weight0, x0, x1, kap, rhs,
     weight2, u, w, low, high, dots, a, b, rhs2, spread, middle, t1, t0, full) = refs
    blocks = (own, up1, down1, up2, down2)
    row, lane = iota((16, 256), 0), iota((16, 256), 1)
    y = jnp.where(row < 10, row, row - 16) + 4 * place[1]
    z = jnp.where(lane < 192, lane, lane - 256) + 128 * place[2]
    near = (lane < 160) | (lane >= 224)
    inside = near & (y >= 0) & (y < 4 * sizes[1]) & (z >= 0) & (z < 128 * sizes[2])
    assemble_coarse(place, blocks, 3, weight2, 1, lambda s, v: jnp.where(inside, v, 0.0))
    up_sweep(place, blocks, weight2, weight1, weight0, x0, x1, kap, full, w, low, high, a, b, rhs2, spread, middle, t1, t0)
    rz = curve = jnp.zeros((16, 128), F32)
    for k in range(16):
        v = full[k + 5][:16, :128]
        u[k] = v
        rz = rz + rhs[k] * v
        curve = curve + w[k] * v
    dots[...] = lanes_of([rz, curve])


def up_kernel(place, *refs):
    (own, up1, down1, up2, down2, weight2, weight1, weight0, x0, x1, kap,
     u, w, low, high, a, b, rhs2, spread, middle, t1, t0, full) = refs
    blocks = (own, up1, down1, up2, down2)
    up_sweep(place, blocks, weight2, weight1, weight0, x0, x1, kap, full, w, low, high, a, b, rhs2, spread, middle, t1, t0)
    for k in range(16):
        u[k] = full[k + 5][:16, :128]


def dots_kernel(first, r0, u0, w0, m0, n0, p, q, r1, u1, w1, m1, n1, dots):
    alpha = first[0:1, 0:1] / first[0:1, 1:2]
    sums = [jnp.zeros((16, 128), F32)] * 12
    for k in range(16):
        vw0, vm0, vn0 = w0[k], m0[k], n0[k]
        vr1 = r0[k] - alpha * vw0
        vu1 = u0[k] - alpha * vm0
        vw1 = vw0 - alpha * vn0
        vm1 = vm0 - alpha * p[k]
        vn1 = vn0 - alpha * q[k]
        r1[k], u1[k], w1[k], m1[k], n1[k] = vr1, vu1, vw1, vm1, vn1
        terms = [vr1 * vu1, vr1 * vm1, vr1 * vm0, vw1 * vu1, vw1 * vm1, vw1 * vm0,
                 vw0 * vu1, vw0 * vm1, vw0 * vm0, vn1 * vm1, vn1 * vm0, vn0 * vm0]
        sums = [s + t for s, t in zip(sums, terms)]
    dots[...] = lanes_of(sums)


def finish_kernel(first, second, u0, w0, m0, n0, r1, u1, w1, m1, n1, field, residual):
    g0, d0 = first[0:1, 0:1], first[0:1, 1:2]
    r1u1, r1m1, r1m0, w1u1, w1m1, w1m0, w0u1, w0m1, w0m0, n1m1, n1m0, n0m0 = [second[0:1, k:k + 1] for k in range(12)]
    alpha0 = g0 / d0
    beta1 = r1u1 / g0
    curve1 = w1u1 + 2.0 * beta1 * w0u1 + beta1 * beta1 * d0
    alpha1 = r1u1 / curve1
    ab = alpha1 * beta1
    su = w1u1 + beta1 * w0u1 - alpha1 * (w1m1 + beta1 * w0m1) - ab * (w1m0 + beta1 * w0m0)
    g2 = (r1u1 - alpha1 * r1m1 - ab * r1m0) - alpha1 * su
    beta2 = g2 / r1u1
    uw = (w1u1 - 2.0 * alpha1 * w1m1 - 2.0 * ab * w1m0) + (alpha1 * alpha1 * n1m1 + 2.0 * alpha1 * ab * n1m0 + ab * ab * n0m0)
    curve2 = uw + 2.0 * beta2 * su + beta2 * beta2 * curve1
    alpha2 = g2 / curve2
    mix = alpha1 + alpha2 * beta2
    cu0, cu1, cm1, cm0 = alpha0 + mix * beta1, mix + alpha2, alpha2 * alpha1, alpha2 * ab
    cw0 = mix * beta1
    for k in range(16):
        field[k] = (cu0 * u0[k] + cu1 * u1[k]) - (cm1 * m1[k] + cm0 * m0[k])
        residual[k] = r1[k] - (cw0 * w0[k] + cu1 * w1[k]) + (cm1 * n1[k] + cm0 * n0[k])


def shape(*dims):
    return jax.ShapeDtypeStruct(dims, F32)


def call(kernel, outs, scratch=(), scalars=0, count=0, smem=()):
    specs = [SMEM if (k < scalars or k in smem) else VMEM for k in range(count)]
    return pl.pallas_call(
        kernel,
        out_shape=outs,
        in_specs=specs,
        out_specs=[VMEM] * len(outs),
        scratch_shapes=[pltpu.VMEM(s, F32) for s in scratch],
        compiler_params=pltpu.CompilerParams(vmem_limit_bytes=40 * 1024 * 1024),
    )


def ring(axis, distance):
    count = lax.axis_size(axis)
    return [(i, (i + distance) % count) for i in range(count)]


def shift(v, axis, distance):
    return lax.ppermute(v, axis, ring(axis, -distance))


def fine_exchange(own, low, high):
    above, below = shift(low, "gz", 1), shift(high, "gz", -1)
    packs = [above[..., None, :, :], below[..., None, :, :]]
    first = jnp.concatenate([own[..., :5, :, :]] + packs, axis=-3)
    last = jnp.concatenate([own[..., 11:, :, :]] + packs, axis=-3)
    before, after = shift(last, "gx", -1), shift(first, "gx", 1)
    body = jnp.concatenate([own] + packs + [before, after], axis=-3)
    upper, lower = shift(body[..., :8, :], "gy", 1), shift(body[..., 8:, :], "gy", -1)
    return body, upper, lower


def coarse_exchange(unit):
    groups = []
    ends = unit[2::3]
    above, below = shift(ends, "gz", 1), shift(ends, "gz", -1)
    tiles = []
    for k in range(unit.shape[0] // 3):
        tiles += [unit[3 * k], unit[3 * k + 1], jnp.concatenate([above[k, :4], below[k, 4:]], axis=0)]
    unit = jnp.stack(tiles)
    groups = jnp.stack([unit] + [shift(unit, "gx", k) for k in (1, 2, 3)])
    return [groups] + [shift(groups, "gy", k) for k in (1, -1, 2, -2)]


def total(v):
    row = v[:1]
    for axes, count in ((("gx", "gy"), lax.axis_size("gx") * lax.axis_size("gy")), (("gz",), lax.axis_size("gz"))):
        parts = lax.all_to_all(jnp.broadcast_to(row[None], (count, 1, 128)), axes, 0, 0, tiled=True)
        row = parts.sum(0)
    return jnp.broadcast_to(row, (8, 128))


def local(right_side, classes, table):
    place = jnp.stack([lax.axis_index(axis) for axis in ("gx", "gy", "gz")]).astype(jnp.int32)
    sizes = jnp.array([lax.axis_size(axis) for axis in ("gx", "gy", "gz")], jnp.int32)
    block, halo = (16, 16, 128), (SLABS, 32, 256)
    mids = (MIDS, 32, 256)
    down_scratch = [halo, mids, (4, 16, 128)]
    up_scratch = [(18, 16, 256), (18, 16, 256), (18, 16, 256), (6, 32, 256), mids, mids, halo, halo]

    kap, low, high = call(
        prepare_kernel, [shape(*block), shape(2, 16, 128), shape(2, 16, 128)], count=3, smem=(2,)
    )(right_side, classes, table)
    body, upper, lower = fine_exchange(jnp.stack([right_side, kap]), low, high)
    weight0, weight1, x0, x1, unit = call(
        first_down_kernel, [shape(*halo), shape(*mids), shape(*halo), shape(*mids), shape(6, 8, 128)],
        down_scratch, scalars=2, count=8,
    )(sizes, place, body[0], upper[0], lower[0], body[1], upper[1], lower[1])
    blocks = coarse_exchange(unit)
    weight2, u0, w0, low, high, dots = call(
        first_up_kernel,
        [shape(18, 16, 256), shape(*block), shape(*block), shape(16, 128), shape(16, 128), shape(8, 128)],
        up_scratch, scalars=2, count=13,
    )(place, sizes, *blocks, weight1, weight0, x0, x1, kap, right_side)
    first = total(dots)

    def apply(v, low, high):
        body, upper, lower = fine_exchange(v, low, high)
        x0, x1, unit = call(
            down_kernel, [shape(*halo), shape(*mids), shape(3, 8, 128)], down_scratch, count=5
        )(body, upper, lower, weight0, weight1)
        blocks = coarse_exchange(unit)
        return call(
            up_kernel, [shape(*block), shape(*block), shape(16, 128), shape(16, 128)],
            up_scratch, scalars=1, count=12,
        )(place, *blocks, weight2, weight1, weight0, x0, x1, kap)

    m0, n0, low, high = apply(w0, low, high)
    p, q, _, _ = apply(n0, low, high)
    r1, u1, w1, m1, n1, dots = call(
        dots_kernel, [shape(*block)] * 5 + [shape(8, 128)], count=8
    )(first, right_side, u0, w0, m0, n0, p, q)
    second = total(dots)
    field, residual = call(finish_kernel, [shape(*block)] * 2, count=11)(
        first, second, u0, w0, m0, n0, r1, u1, w1, m1, n1
    )
    return field, residual


def solution(mesh):
    in_specs = (P("gx", "gy", "gz"), P("gx", "gy", "gz"), P())
    out_specs = (P("gx", "gy", "gz"), P("gx", "gy", "gz"))
    return jax.shard_map(local, mesh=mesh, in_specs=in_specs, out_specs=out_specs, check_vma=False)
```

```python
import jax
import jax.numpy as jnp
from jax import lax
from jax.experimental import pallas as pl
from jax.experimental.pallas import tpu as pltpu
from jax.sharding import PartitionSpec as P

CLASSES = 16
COARSE_SWEEPS = 6
OMEGA = 0.8
KEEP = 1.0 - OMEGA
F32 = jnp.float32
SLABS, MIDS = 26, 12
MARK = 64
BLOCK, HALO, MID = (16, 16, 128), (SLABS, 32, 256), (MIDS, 32, 256)
VMEM = pl.BlockSpec(memory_space=pltpu.VMEM)
ANY = pl.BlockSpec(memory_space=pl.ANY)


def iota(shape, dim):
    return lax.broadcasted_iota(jnp.int32, shape, dim)


def roll(v, shift, axis):
    shift = shift % v.shape[axis]
    return v if shift == 0 else pltpu.roll(v, shift, axis)


def around(v, rows, lanes):
    return (roll(v, rows, 0) + roll(v, -rows, 0)) + (roll(v, lanes, 1) + roll(v, -lanes, 1))


def pair_mean(v, step):
    rows = (iota(v.shape, 0) // step) % 2 == 0
    v = v + jnp.where(rows, roll(v, -step, 0), roll(v, step, 0))
    lanes = (iota(v.shape, 1) // step) % 2 == 0
    v = v + jnp.where(lanes, roll(v, -step, 1), roll(v, step, 1))
    return v * 0.125


def place():
    return tuple(lax.axis_index(axis) for axis in ("gx", "gy", "gz"))


def sizes():
    return tuple(lax.axis_size(axis) for axis in ("gx", "gy", "gz"))


def pack_fine(read, low_ref, high_ref):
    chunk = iota((16, 128), 1) // 32
    for g in range(4):
        low = high = None
        for j in range(4):
            v = read(4 * g + j)
            first, last = roll(v, 32 * j, 1), roll(v, 32 * j + 32, 1)
            low = first if j == 0 else jnp.where(chunk == j, first, low)
            high = last if j == 0 else jnp.where(chunk == j, last, high)
        low_ref[g] = low
        high_ref[g] = high


def prepare_kernel(rhs_in, classes_in, table_in, both, low, high, classes, table, sems):
    copies = [
        pltpu.make_async_copy(rhs_in, both.at[0], sems.at[0]),
        pltpu.make_async_copy(classes_in, classes, sems.at[1]),
        pltpu.make_async_copy(table_in, table, sems.at[2]),
    ]
    for copy in copies:
        copy.start()
    for copy in copies:
        copy.wait()
    for k in range(16):
        c = classes[k]
        v = jnp.zeros((16, 128), F32)
        for index in range(CLASSES):
            v = jnp.where(c == index, table[index], v)
        both[1, k] = v
    for t in range(2):
        pack_fine(lambda k, t=t: both[t, k], low.at[t], high.at[t])


def slab_sources(i):
    x = i - 5
    if x < 0:
        k = 16 + x
        return 24 + x + 5, 29 + k // 4 - 2, 31 + k // 4 - 2, k % 4
    if x < 16:
        return x, 16 + x // 4, 20 + x // 4, x % 4
    k = x - 16
    return 33 + k, 38 + k // 4, 40 + k // 4, k % 4


def assemble_fine(body, upper, lower, i):
    def unit(u):
        return jnp.concatenate([body[u], upper[u], lower[u]], axis=0)

    main, above, below, j = slab_sources(i)
    lane = iota((32, 128), 1)
    side = jnp.where(lane < 64, roll(unit(above), -32 * j, 1), roll(unit(below), 96 - 32 * j, 1))
    return jnp.concatenate([unit(main), side], axis=1)


def near(lane):
    return (lane < 160) | (lane >= 224)


def inside_lanes(lane):
    z = jnp.where(lane < 192, lane, lane - 256) + 128 * place()[2]
    return near(lane) & (z >= 0) & (z < 128 * sizes()[2])


def inside_fine():
    row, lane = iota((32, 256), 0), iota((32, 256), 1)
    y = jnp.where(row < 24, row, row - 32) + 16 * place()[1]
    return inside_lanes(lane) & (y >= 0) & (y < 16 * sizes()[1])


def fine_weights(body, upper, lower, weight0, weight1, middle, quads, unit):
    inside, gx, nx = inside_fine(), place()[0], sizes()[0]

    def weigh(i):
        kap = assemble_fine(body, upper, lower, i)
        x = 16 * gx + (i - 5)
        weight0[i] = jnp.where(inside & (x >= 0) & (x < 16 * nx), OMEGA / (kap + 6.0), 0.0)
        return kap

    weigh(0)
    weigh(SLABS - 1)
    for m in range(MIDS):
        kap1 = pair_mean(weigh(2 * m + 1) + weigh(2 * m + 2), 1)
        middle[m] = kap1
        x = 8 * gx + (m - 2)
        weight1[m] = jnp.where(inside & (x >= 0) & (x < 8 * nx), OMEGA / (kap1 + 1.5), 0.0)
    for c in range(4):
        kap2 = pair_mean(middle[2 + 2 * c] + middle[3 + 2 * c], 2)[:16]
        weight2 = OMEGA / (kap2 + 0.375)
        quads[0, c], quads[1, c] = weight2[:, :128], weight2[:, 128:]
    pack_coarse(quads, unit)


def pack_coarse(quads, unit):
    turn = iota((4, 128), 1) % 4
    for half in range(2):
        v = quads[half, 0, pl.ds(0, 4, stride=4), :]
        for c in range(1, 4):
            v = jnp.where(turn == c, quads[half, c, pl.ds(0, 4, stride=4), :], v)
        unit[4 * half:4 * half + 4] = v


def down_sweep(body, upper, lower, weight0, weight1, x0, x1, unit, r, r1, quads):
    for i in range(SLABS):
        v = assemble_fine(body, upper, lower, i)
        r[i] = v
        x0[i] = weight0[i] * v
    for m in range(MIDS):
        i = 2 * m + 1
        two = x0[i] + x0[i + 1]
        left = KEEP * (r[i] + r[i + 1]) + ((x0[i - 1] + x0[i + 2]) + two) + around(two, 1, 1)
        v = pair_mean(left, 1)
        r1[m] = v
        x1[m] = weight1[m] * v
    for c in range(4):
        m = 2 + 2 * c
        two = x1[m] + x1[m + 1]
        left = KEEP * (r1[m] + r1[m + 1]) + 0.25 * (((x1[m - 1] + x1[m + 2]) + two) + around(two, 2, 2))
        v = pair_mean(left, 2)[:16]
        quads[0, c], quads[1, c] = v[:, :128], v[:, 128:]
    pack_coarse(quads, unit)


def first_down_kernel(body, upper, lower, weight0, weight1, x0, x1, unit, r, r1, quads):
    fine_weights(body.at[1], upper.at[1], lower.at[1], weight0, weight1, r1, quads, unit.at[1])
    down_sweep(body.at[0], upper.at[0], lower.at[0], weight0, weight1, x0, x1, unit.at[0], r, r1, quads)


def down_kernel(body, upper, lower, weight0, weight1, x0, x1, unit, r, r1, quads):
    down_sweep(body, upper, lower, weight0, weight1, x0, x1, unit, r, r1, quads)


def assemble_coarse(gather, t, out, change):
    gy, ny = place()[1], sizes()[1]
    turn = iota((16, 256), 1) % 4
    for k in range(4):
        own, up1, up2, down2, down1 = [ny * k + lax.rem(gy + d + ny, ny) for d in (0, 1, 2, -2, -1)]
        v = jnp.concatenate(
            [
                jnp.concatenate([
                    gather[own, t, s:s + 4], gather[up1, t, s:s + 4], gather[up2, t, s:s + 2],
                    gather[down2, t, s + 2:s + 4], gather[down1, t, s:s + 4],
                ], axis=0)
                for s in (0, 4)
            ],
            axis=1,
        )
        moved = {d: roll(v, d, 1) for d in range(-3, 4)}
        for c in range(4):
            slab = moved[-c]
            for j in range(1, 4):
                slab = jnp.where(turn == j, moved[j - c], slab)
            out[4 * k + c + 1] = change(4 * k + c + 1, slab)


def up_sweep(gather, weight2, weight1, weight0, x0, x1, kap, u, w, a, b, rhs2, spread, middle, t1, t0):
    zero = jnp.zeros((16, 256), F32)
    for ref in (a, b):
        ref[0] = zero
        ref[17] = zero
    assemble_coarse(gather, 0, rhs2, lambda s, v: weight2[s] * v)
    for s in range(1, 17):
        a[s] = rhs2[s]
    for sweep in range(COARSE_SWEEPS - 1):
        old, new = (a, b) if sweep % 2 == 0 else (b, a)

        def step(s, carry, old=old, new=new):
            v = old[s]
            beside = (old[s - 1] + old[s + 1]) + around(v, 1, 4)
            new[s] = (KEEP * v + rhs2[s]) + weight2[s] * (0.0625 * beside)
            return carry

        lax.fori_loop(1, 17, step, 0, unroll=4)
    last = b if COARSE_SWEEPS % 2 == 0 else a
    half = iota((8, 256), 0) < 4
    for c in range(6):
        v = last[4 * place()[0] + c]
        spread[c] = jnp.concatenate(
            [
                jnp.where(half, jnp.broadcast_to(v[j:j + 1], (8, 256)), jnp.broadcast_to(v[j + 1:j + 2], (8, 256)))
                for j in (0, 2, 4, 14)
            ],
            axis=0,
        )
    for m in range(MIDS):
        t1[m] = x1[m] + spread[m // 2]
    for m in range(1, MIDS - 1):
        v = t1[m]
        beside = (t1[m - 1] + t1[m + 1]) + around(v, 2, 2)
        middle[m] = (KEEP * v + x1[m]) + weight1[m] * (0.25 * beside)
    for i in range(3, SLABS - 3):
        t0[i] = x0[i] + middle[(i - 1) // 2]
    for i in range(4, SLABS - 4):
        v = t0[i]
        beside = (t0[i - 1] + t0[i + 1]) + around(v, 1, 1)
        u[i] = (KEEP * v + x0[i]) + weight0[i] * beside
    for i in range(5, SLABS - 5):
        v = u[i]
        beside = (u[i - 1] + u[i + 1]) + around(v, 1, 1)
        w[i - 5] = (kap[i - 5] + 6.0) * v[:16, :128] - beside[:16, :128]


def lanes_of(values):
    lane = iota((8, 128), 1)
    out = jnp.zeros((8, 128), F32)
    for k, v in enumerate(values):
        out = jnp.where(lane == MARK + k, jnp.sum(v), out)
    return out


def first_up_kernel(gather, weight1, weight0, x0, x1, both, weight2, u, w, low, high, dots, *scratch):
    (*scratch, full) = scratch
    row, lane = iota((16, 256), 0), iota((16, 256), 1)
    y = jnp.where(row < 10, row, row - 16) + 4 * place()[1]
    inside = inside_lanes(lane) & (y >= 0) & (y < 4 * sizes()[1])
    assemble_coarse(gather, 1, weight2, lambda s, v: jnp.where(inside, v, 0.0))
    up_sweep(gather, weight2, weight1, weight0, x0, x1, both.at[1], full, w, *scratch)
    rz = curve = jnp.zeros((16, 128), F32)
    for k in range(16):
        v = full[k + 5][:16, :128]
        u[k] = v
        rz = rz + both[0, k] * v
        curve = curve + w[k] * v
    dots[...] = lanes_of([rz, curve])
    pack_fine(lambda k: w[k], low, high)


def second_up_kernel(gather, weight2, weight1, weight0, x0, x1, both, u0, w0,
                     m0, n0, r1, u1, w1, low, high, first, *scratch):
    (*scratch, full) = scratch
    sums = gather[0, 0]
    for k in range(1, gather.shape[0]):
        sums = sums + gather[k, 0]
    first[...] = sums
    alpha = sums[4:5, MARK:MARK + 1] / sums[4:5, MARK + 1:MARK + 2]
    up_sweep(gather, weight2, weight1, weight0, x0, x1, both.at[1], full, n0, *scratch)
    for k in range(16):
        v = full[k + 5][:16, :128]
        m0[k] = v
        r1[k] = both[0, k] - alpha * w0[k]
        u1[k] = u0[k] - alpha * v
        w1[k] = w0[k] - alpha * n0[k]
    pack_fine(lambda k: w1[k], low, high)


def third_up_kernel(gather, weight2, weight1, weight0, x0, x1, both, w0, m0, n0, r1, u1, w1, m1, n1, dots, *scratch):
    (*scratch, full) = scratch
    up_sweep(gather, weight2, weight1, weight0, x0, x1, both.at[1], full, n1, *scratch)
    sums = [jnp.zeros((16, 128), F32)] * 12
    for k in range(16):
        vm1 = full[k + 5][:16, :128]
        m1[k] = vm1
        vw0, vm0, vn0, vr1, vu1, vw1, vn1 = w0[k], m0[k], n0[k], r1[k], u1[k], w1[k], n1[k]
        terms = [vr1 * vu1, vr1 * vm1, vr1 * vm0, vw1 * vu1, vw1 * vm1, vw1 * vm0,
                 vw0 * vu1, vw0 * vm1, vw0 * vm0, vn1 * vm1, vn1 * vm0, vn0 * vm0]
        sums = [s + t for s, t in zip(sums, terms)]
    dots[...] = lanes_of(sums)


def finish_kernel(first, second, u0, w0, m0, n0, r1, u1, w1, m1, n1, field, residual):
    g0, d0 = first[4:5, MARK:MARK + 1], first[4:5, MARK + 1:MARK + 2]
    (r1u1, r1m1, r1m0, w1u1, w1m1, w1m0, w0u1, w0m1, w0m0, n1m1, n1m0, n0m0) = [
        second[0:1, MARK + k:MARK + k + 1] for k in range(12)
    ]
    alpha0 = g0 / d0
    beta1 = r1u1 / g0
    curve1 = w1u1 + 2.0 * beta1 * w0u1 + beta1 * beta1 * d0
    alpha1 = r1u1 / curve1
    ab = alpha1 * beta1
    su = w1u1 + beta1 * w0u1 - alpha1 * (w1m1 + beta1 * w0m1) - ab * (w1m0 + beta1 * w0m0)
    g2 = (r1u1 - alpha1 * r1m1 - ab * r1m0) - alpha1 * su
    beta2 = g2 / r1u1
    uw = (w1u1 - 2.0 * alpha1 * w1m1 - 2.0 * ab * w1m0) + (alpha1 * alpha1 * n1m1 + 2.0 * alpha1 * ab * n1m0 + ab * ab * n0m0)
    curve2 = uw + 2.0 * beta2 * su + beta2 * beta2 * curve1
    alpha2 = g2 / curve2
    mix = alpha1 + alpha2 * beta2
    cu0, cu1, cm1, cm0 = alpha0 + mix * beta1, mix + alpha2, alpha2 * alpha1, alpha2 * ab
    cw0 = mix * beta1
    for k in range(16):
        field[k] = (cu0 * u0[k] + cu1 * u1[k]) - (cm1 * m1[k] + cm0 * m0[k])
        residual[k] = r1[k] - (cw0 * w0[k] + cu1 * w1[k]) + (cm1 * n1[k] + cm0 * n0[k])


def shape(*dims):
    return jax.ShapeDtypeStruct(dims, F32)


def call(kernel, outs, scratch=(), specs=None, count=0):
    return pl.pallas_call(
        kernel,
        out_shape=outs,
        in_specs=specs or [VMEM] * count,
        out_specs=[VMEM] * len(outs),
        scratch_shapes=list(scratch),
        compiler_params=pltpu.CompilerParams(vmem_limit_bytes=40 * 1024 * 1024),
    )


def shift(v, axis, distance):
    count = lax.axis_size(axis)
    return lax.ppermute(v, axis, [((i + distance) % count, i) for i in range(count)])


def fine_exchange(own, low, high, scalars=None):
    if scalars is None:
        above, below = shift(low, "gz", 1), shift(high, "gz", -1)
    else:
        above = shift(jnp.concatenate([low.reshape(8, 8, 128), scalars[None]]), "gz", 1)
        below = shift(high, "gz", -1)
        scalars = scalars + above[8]
        above = above[:8].reshape(4, 16, 128)
    first = jnp.concatenate([own[..., :5, :, :], above[..., :2, :, :], below[..., :2, :, :]], axis=-3)
    last = jnp.concatenate([own[..., 11:, :, :], above[..., 2:, :, :], below[..., 2:, :, :]], axis=-3)
    if scalars is not None:
        first, last, scalars = lax.optimization_barrier((first, last, scalars))
        scalars = scalars + shift(scalars, "gz", 2)
    before, after = shift(last, "gx", -1), shift(first, "gx", 1)
    body = jnp.concatenate([own, above, below, before, after], axis=-3)
    if scalars is not None:
        body, scalars = lax.optimization_barrier((body, scalars))
        scalars = scalars + shift(scalars, "gz", 4)
    upper, lower = shift(body[..., :8, :], "gy", 1), shift(body[..., 8:, :], "gy", -1)
    return (body, upper, lower), scalars


def gather(unit):
    count = lax.axis_size("gx") * lax.axis_size("gy")
    return lax.all_to_all(jnp.broadcast_to(unit[None], (count,) + unit.shape), ("gx", "gy"), 0, 0, tiled=True)


def total(v):
    axes = ("gx", "gy", "gz")
    count = lax.axis_size("gx") * lax.axis_size("gy") * lax.axis_size("gz")
    parts = lax.all_to_all(jnp.broadcast_to(v[None, :1], (count, 1, 128)), axes, 0, 0, tiled=True)
    return jnp.broadcast_to(parts.sum(0), (8, 128))


def local(right_side, classes, table):
    def scratch(*shapes):
        return [pltpu.VMEM(s, F32) for s in shapes]

    block, halo, mids = shape(*BLOCK), shape(*HALO), shape(*MID)
    packs, tile = shape(4, 16, 128), shape(8, 128)
    down_scratch = scratch(HALO, MID, (2, 4, 16, 128))
    up_scratch = scratch((18, 16, 256), (18, 16, 256), (18, 16, 256), (6, 32, 256), MID, MID, HALO, HALO)

    both, low, high = call(
        prepare_kernel, [shape(2, *BLOCK), shape(2, 4, 16, 128), shape(2, 4, 16, 128)],
        [pltpu.VMEM(BLOCK, jnp.int32), pltpu.SMEM((CLASSES,), F32), pltpu.SemaphoreType.DMA((3,))], specs=[ANY] * 3,
    )(right_side, classes, table)
    halos, _ = fine_exchange(both, low, high)
    weight0, weight1, x0, x1, unit = call(
        first_down_kernel, [halo, mids, halo, mids, shape(2, 8, 128)], down_scratch, count=3
    )(*halos)
    weight2, u0, w0, low, high, dots = call(
        first_up_kernel, [shape(18, 16, 256), block, block, packs, packs, tile], up_scratch, count=6
    )(gather(unit), weight1, weight0, x0, x1, both)

    down = call(down_kernel, [halo, mids, tile], down_scratch, count=5)
    halos, scalars = fine_exchange(w0, low, high, dots)
    x0, x1, unit = down(*halos, weight0, weight1)
    free = (iota((8, 128), 0) >= 4) & (iota((8, 128), 1) >= 32) & (iota((8, 128), 1) < 96)
    unit = jnp.where(free, scalars, unit)
    m0, n0, r1, u1, w1, low, high, first = call(
        second_up_kernel, [block] * 5 + [packs, packs, tile], up_scratch, count=9
    )(gather(unit[None]), weight2, weight1, weight0, x0, x1, both, u0, w0)

    halos, _ = fine_exchange(w1, low, high)
    x0, x1, unit = down(*halos, weight0, weight1)
    m1, n1, dots = call(third_up_kernel, [block] * 2 + [tile], up_scratch, count=13)(
        gather(unit[None]), weight2, weight1, weight0, x0, x1, both, w0, m0, n0, r1, u1, w1
    )
    field, residual = call(finish_kernel, [block] * 2, count=11)(
        first, total(dots), u0, w0, m0, n0, r1, u1, w1, m1, n1
    )
    return field, residual


def solution(mesh):
    in_specs = (P("gx", "gy", "gz"), P("gx", "gy", "gz"), P())
    out_specs = (P("gx", "gy", "gz"), P("gx", "gy", "gz"))
    return jax.shard_map(local, mesh=mesh, in_specs=in_specs, out_specs=out_specs, check_vma=False)
```

```python
import jax
import jax.numpy as jnp
from jax import lax
from jax.experimental import pallas as pl
from jax.experimental.pallas import tpu as pltpu
from jax.sharding import PartitionSpec as P

CLASSES = 16
COARSE_SWEEPS = 6
OMEGA = 0.8
KEEP = 1.0 - OMEGA
F32 = jnp.float32
SLABS, MIDS, UNITS = 26, 12, 40
MARK = 64
BLOCK, HALO, MID = (16, 16, 128), (SLABS, 32, 256), (MIDS, 32, 256)
VMEM = pl.BlockSpec(memory_space=pltpu.VMEM)
ANY = pl.BlockSpec(memory_space=pl.ANY)


def iota(shape, dim):
    return lax.broadcasted_iota(jnp.int32, shape, dim)


def roll(v, shift, axis):
    shift = shift % v.shape[axis]
    return v if shift == 0 else pltpu.roll(v, shift, axis)


def around(v, rows, lanes):
    return (roll(v, rows, 0) + roll(v, -rows, 0)) + (roll(v, lanes, 1) + roll(v, -lanes, 1))


def pair_mean(v, step):
    rows = (iota(v.shape, 0) // step) % 2 == 0
    v = v + jnp.where(rows, roll(v, -step, 0), roll(v, step, 0))
    lanes = (iota(v.shape, 1) // step) % 2 == 0
    v = v + jnp.where(lanes, roll(v, -step, 1), roll(v, step, 1))
    return v * 0.125


def place():
    return tuple(lax.axis_index(axis) for axis in ("gx", "gy", "gz"))


def sizes():
    return tuple(lax.axis_size(axis) for axis in ("gx", "gy", "gz"))


def pack_fine(read, low_ref, high_ref):
    lane = iota((16, 128), 1)
    chunk = lane // 32
    for g in range(4):
        low = high = None
        for j in range(4):
            v = read(4 * g + j)
            first, last = roll(v, 32 * j, 1), roll(v, 32 * j + 32, 1)
            low = first if j == 0 else jnp.where(chunk == j, first, low)
            high = last if j == 0 else jnp.where(chunk == j, last, high)
        low_ref[g] = low
        high_ref[g] = high
    for g, slabs in ((4, (0, 1, 2, 3, 4)), (5, (15, 14, 13, 12, 11))):
        low, high = read(slabs[0]), roll(read(slabs[0]), 32, 1)
        for j in range(1, 5):
            v, here = read(slabs[j]), (lane >= 112 if j == 4 else chunk == j)
            low = jnp.where(here, roll(v, 112 if j == 4 else 32 * j, 1), low)
            high = jnp.where(here, roll(v, (32, 64, 96, 112, 0)[j], 1), high)
        low_ref[g] = low
        high_ref[g] = high


def prepare_kernel(rhs_in, classes_in, table_in, both, low, high, classes, table, sems):
    copies = [
        pltpu.make_async_copy(rhs_in, both.at[0], sems.at[0]),
        pltpu.make_async_copy(classes_in, classes, sems.at[1]),
        pltpu.make_async_copy(table_in, table, sems.at[2]),
    ]
    for copy in copies:
        copy.start()
    for copy in copies:
        copy.wait()
    for k in range(16):
        c = classes[k]
        v = jnp.zeros((16, 128), F32)
        for index in range(CLASSES):
            v = jnp.where(c == index, table[index], v)
        both[1, k] = v
    for t in range(2):
        pack_fine(lambda k, t=t: both[t, k], low.at[t], high.at[t])


def slab_sources(i):
    x = i - 5
    if 0 <= x < 16:
        return x, 16 + x // 4, 20 + x // 4, -32 * (x % 4), 96 - 32 * (x % 4)
    base, far = (24, -1 - x) if x < 0 else (31, x - 16)
    return base + (x + 5 if x < 0 else far), base + 5, base + 6, (0, -32, -64, -96, -112)[far], (96, 64, 32, 16, 0)[far]


def assemble_fine(body, sides, i):
    def unit(u):
        return jnp.concatenate([body[u][...], sides[u][...]], axis=0)

    main, above, below, up, down = slab_sources(i)
    lane = iota((32, 128), 1)
    side = jnp.where(lane < 64, roll(unit(above), up, 1), roll(unit(below), down, 1))
    return jnp.concatenate([unit(main), side], axis=1)


def pack_rows_kernel(body, upper, lower):
    for g in range(body.shape[0] // 128):
        for t in range(5):
            upper[5 * g + t] = body[pl.ds(128 * g + t, 8, stride=16), :]
            lower[5 * g + t] = body[pl.ds(128 * g + 11 + t, 8, stride=16), :]


def unpack_rows(upper, lower, first, sides):
    sides[...] = jnp.zeros(sides.shape, F32)
    for g in range(UNITS // 8):
        for t in range(5):
            sides[pl.ds(128 * g + t, 8, stride=16), :] = upper[first + 5 * g + t]
            sides[pl.ds(128 * g + 11 + t, 8, stride=16), :] = lower[first + 5 * g + t]
    return [sides.at[pl.ds(16 * u, 16)] for u in range(UNITS)]


def near(lane):
    return (lane < 160) | (lane >= 224)


def inside_lanes(lane):
    z = jnp.where(lane < 192, lane, lane - 256) + 128 * place()[2]
    return near(lane) & (z >= 0) & (z < 128 * sizes()[2])


def inside_fine():
    row, lane = iota((32, 256), 0), iota((32, 256), 1)
    y = jnp.where(row < 24, row, row - 32) + 16 * place()[1]
    return inside_lanes(lane) & (y >= 0) & (y < 16 * sizes()[1])


def fine_weights(body, sides, weight0, weight1, middle, quads, unit):
    inside, gx, nx = inside_fine(), place()[0], sizes()[0]

    def weigh(i):
        kap = assemble_fine(body, sides, i)
        x = 16 * gx + (i - 5)
        weight0[i] = jnp.where(inside & (x >= 0) & (x < 16 * nx), OMEGA / (kap + 6.0), 0.0)
        return kap

    weigh(0)
    weigh(SLABS - 1)
    for m in range(MIDS):
        kap1 = pair_mean(weigh(2 * m + 1) + weigh(2 * m + 2), 1)
        middle[m] = kap1
        x = 8 * gx + (m - 2)
        weight1[m] = jnp.where(inside & (x >= 0) & (x < 8 * nx), OMEGA / (kap1 + 1.5), 0.0)
    for c in range(4):
        kap2 = pair_mean(middle[2 + 2 * c] + middle[3 + 2 * c], 2)[:16]
        weight2 = OMEGA / (kap2 + 0.375)
        quads[0, c], quads[1, c] = weight2[:, :128], weight2[:, 128:]
    pack_coarse(quads, unit)


def pack_coarse(quads, unit):
    turn = iota((4, 128), 1) % 4
    for half in range(2):
        v = quads[half, 0, pl.ds(0, 4, stride=4), :]
        for c in range(1, 4):
            v = jnp.where(turn == c, quads[half, c, pl.ds(0, 4, stride=4), :], v)
        unit[4 * half:4 * half + 4] = v


def down_sweep(body, sides, weight0, weight1, x0, x1, unit, r, r1, quads):
    for i in range(SLABS):
        v = assemble_fine(body, sides, i)
        r[i] = v
        x0[i] = weight0[i] * v
    for m in range(MIDS):
        i = 2 * m + 1
        two = x0[i] + x0[i + 1]
        left = KEEP * (r[i] + r[i + 1]) + ((x0[i - 1] + x0[i + 2]) + two) + around(two, 1, 1)
        v = pair_mean(left, 1)
        r1[m] = v
        x1[m] = weight1[m] * v
    for c in range(4):
        m = 2 + 2 * c
        two = x1[m] + x1[m + 1]
        left = KEEP * (r1[m] + r1[m + 1]) + 0.25 * (((x1[m - 1] + x1[m + 2]) + two) + around(two, 2, 2))
        v = pair_mean(left, 2)[:16]
        quads[0, c], quads[1, c] = v[:, :128], v[:, 128:]
    pack_coarse(quads, unit)


def units(body, first):
    return [body.at[pl.ds(first + 16 * u, 16)] for u in range(UNITS)]


def first_down_kernel(body, upper, lower, weight0, weight1, x0, x1, unit, r, r1, quads, sides, more):
    kap_sides = unpack_rows(upper, lower, 5 * UNITS // 8, more)
    fine_weights(units(body, 16 * UNITS), kap_sides, weight0, weight1, r1, quads, unit.at[1])
    r_sides = unpack_rows(upper, lower, 0, sides)
    down_sweep(units(body, 0), r_sides, weight0, weight1, x0, x1, unit.at[0], r, r1, quads)


def down_kernel(body, upper, lower, weight0, weight1, x0, x1, unit, r, r1, quads, sides):
    r_sides = unpack_rows(upper, lower, 0, sides)
    down_sweep(units(body, 0), r_sides, weight0, weight1, x0, x1, unit, r, r1, quads)


def assemble_coarse(gather, t, out, change):
    gy, ny = place()[1], sizes()[1]
    turn = iota((16, 256), 1) % 4
    for k in range(4):
        own, up1, up2, down2, down1 = [ny * k + lax.rem(gy + d + ny, ny) for d in (0, 1, 2, -2, -1)]
        v = jnp.concatenate(
            [
                jnp.concatenate([
                    gather[own, t, s:s + 4], gather[up1, t, s:s + 4], gather[up2, t, s:s + 2],
                    gather[down2, t, s + 2:s + 4], gather[down1, t, s:s + 4],
                ], axis=0)
                for s in (0, 4)
            ],
            axis=1,
        )
        moved = {d: roll(v, d, 1) for d in range(-3, 4)}
        for c in range(4):
            slab = moved[-c]
            for j in range(1, 4):
                slab = jnp.where(turn == j, moved[j - c], slab)
            out[4 * k + c + 1] = change(4 * k + c + 1, slab)


def up_sweep(gather, weight2, weight1, weight0, x0, x1, kap, u, w, a, b, rhs2, spread, middle, t1, t0):
    zero = jnp.zeros((16, 256), F32)
    for ref in (a, b):
        ref[0] = zero
        ref[17] = zero
    assemble_coarse(gather, 0, rhs2, lambda s, v: weight2[s] * v)
    for s in range(1, 17):
        a[s] = rhs2[s]
    for sweep in range(COARSE_SWEEPS - 1):
        old, new = (a, b) if sweep % 2 == 0 else (b, a)

        for s in range(1, 17):
            v = old[s]
            beside = (old[s - 1] + old[s + 1]) + around(v, 1, 4)
            new[s] = (KEEP * v + rhs2[s]) + weight2[s] * (0.0625 * beside)
    last = b if COARSE_SWEEPS % 2 == 0 else a
    half = iota((8, 256), 0) < 4
    for c in range(6):
        v = last[4 * place()[0] + c]
        spread[c] = jnp.concatenate(
            [
                jnp.where(half, jnp.broadcast_to(v[j:j + 1], (8, 256)), jnp.broadcast_to(v[j + 1:j + 2], (8, 256)))
                for j in (0, 2, 4, 14)
            ],
            axis=0,
        )
    for m in range(MIDS):
        t1[m] = x1[m] + spread[m // 2]
    for m in range(1, MIDS - 1):
        v = t1[m]
        beside = (t1[m - 1] + t1[m + 1]) + around(v, 2, 2)
        middle[m] = (KEEP * v + x1[m]) + weight1[m] * (0.25 * beside)
    for i in range(3, SLABS - 3):
        t0[i] = x0[i] + middle[(i - 1) // 2]
    for i in range(4, SLABS - 4):
        v = t0[i]
        beside = (t0[i - 1] + t0[i + 1]) + around(v, 1, 1)
        u[i] = (KEEP * v + x0[i]) + weight0[i] * beside
    for i in range(5, SLABS - 5):
        v = u[i]
        beside = (u[i - 1] + u[i + 1]) + around(v, 1, 1)
        w[i - 5] = (kap[i - 5] + 6.0) * v[:16, :128] - beside[:16, :128]


def lanes_of(values):
    lane = iota((8, 128), 1)
    out = jnp.zeros((8, 128), F32)
    for k, v in enumerate(values):
        out = jnp.where(lane == MARK + k, jnp.sum(v), out)
    return out


def first_up_kernel(gather, weight1, weight0, x0, x1, both, weight2, u, w, low, high, dots, *scratch):
    (*scratch, full) = scratch
    row, lane = iota((16, 256), 0), iota((16, 256), 1)
    y = jnp.where(row < 10, row, row - 16) + 4 * place()[1]
    inside = inside_lanes(lane) & (y >= 0) & (y < 4 * sizes()[1])
    assemble_coarse(gather, 1, weight2, lambda s, v: jnp.where(inside, v, 0.0))
    up_sweep(gather, weight2, weight1, weight0, x0, x1, both.at[1], full, w, *scratch)
    rz = curve = jnp.zeros((16, 128), F32)
    for k in range(16):
        v = full[k + 5][:16, :128]
        u[k] = v
        rz = rz + both[0, k] * v
        curve = curve + w[k] * v
    dots[...] = lanes_of([rz, curve])
    pack_fine(lambda k: w[k], low, high)


def second_up_kernel(gather, weight2, weight1, weight0, x0, x1, both, u0, w0,
                     m0, n0, r1, u1, w1, low, high, first, *scratch):
    (*scratch, full) = scratch
    sums = gather[0, 0]
    for k in range(1, gather.shape[0]):
        sums = sums + gather[k, 0]
    first[...] = sums
    alpha = sums[4:5, MARK:MARK + 1] / sums[4:5, MARK + 1:MARK + 2]
    up_sweep(gather, weight2, weight1, weight0, x0, x1, both.at[1], full, n0, *scratch)
    for k in range(16):
        v = full[k + 5][:16, :128]
        m0[k] = v
        r1[k] = both[0, k] - alpha * w0[k]
        u1[k] = u0[k] - alpha * v
        w1[k] = w0[k] - alpha * n0[k]
    pack_fine(lambda k: w1[k], low, high)


def third_up_kernel(gather, weight2, weight1, weight0, x0, x1, both, w0, m0, n0, r1, u1, w1, m1, n1, dots, *scratch):
    (*scratch, full) = scratch
    up_sweep(gather, weight2, weight1, weight0, x0, x1, both.at[1], full, n1, *scratch)
    sums = [jnp.zeros((16, 128), F32)] * 12
    for k in range(16):
        vm1 = full[k + 5][:16, :128]
        m1[k] = vm1
        vw0, vm0, vn0, vr1, vu1, vw1, vn1 = w0[k], m0[k], n0[k], r1[k], u1[k], w1[k], n1[k]
        terms = [vr1 * vu1, vr1 * vm1, vr1 * vm0, vw1 * vu1, vw1 * vm1, vw1 * vm0,
                 vw0 * vu1, vw0 * vm1, vw0 * vm0, vn1 * vm1, vn1 * vm0, vn0 * vm0]
        sums = [s + t for s, t in zip(sums, terms)]
    dots[...] = lanes_of(sums)


def finish_kernel(first, second, u0, w0, m0, n0, r1, u1, w1, m1, n1, field, residual):
    g0, d0 = first[4:5, MARK:MARK + 1], first[4:5, MARK + 1:MARK + 2]
    (r1u1, r1m1, r1m0, w1u1, w1m1, w1m0, w0u1, w0m1, w0m0, n1m1, n1m0, n0m0) = [
        second[0:1, MARK + k:MARK + k + 1] for k in range(12)
    ]
    alpha0 = g0 / d0
    beta1 = r1u1 / g0
    curve1 = w1u1 + 2.0 * beta1 * w0u1 + beta1 * beta1 * d0
    alpha1 = r1u1 / curve1
    ab = alpha1 * beta1
    su = w1u1 + beta1 * w0u1 - alpha1 * (w1m1 + beta1 * w0m1) - ab * (w1m0 + beta1 * w0m0)
    g2 = (r1u1 - alpha1 * r1m1 - ab * r1m0) - alpha1 * su
    beta2 = g2 / r1u1
    uw = (w1u1 - 2.0 * alpha1 * w1m1 - 2.0 * ab * w1m0) + (alpha1 * alpha1 * n1m1 + 2.0 * alpha1 * ab * n1m0 + ab * ab * n0m0)
    curve2 = uw + 2.0 * beta2 * su + beta2 * beta2 * curve1
    alpha2 = g2 / curve2
    mix = alpha1 + alpha2 * beta2
    cu0, cu1, cm1, cm0 = alpha0 + mix * beta1, mix + alpha2, alpha2 * alpha1, alpha2 * ab
    cw0 = mix * beta1
    for k in range(16):
        field[k] = (cu0 * u0[k] + cu1 * u1[k]) - (cm1 * m1[k] + cm0 * m0[k])
        residual[k] = r1[k] - (cw0 * w0[k] + cu1 * w1[k]) + (cm1 * n1[k] + cm0 * n0[k])


def shape(*dims):
    return jax.ShapeDtypeStruct(dims, F32)


def call(kernel, outs, scratch=(), specs=None, count=0, grant=40):
    return pl.pallas_call(
        kernel,
        out_shape=outs,
        in_specs=specs or [VMEM] * count,
        out_specs=[VMEM] * len(outs),
        scratch_shapes=list(scratch),
        compiler_params=pltpu.CompilerParams(vmem_limit_bytes=grant * 1024 * 1024),
    )


def shift(v, axis, distance):
    count = lax.axis_size(axis)
    return lax.ppermute(v, axis, [((i + distance) % count, i) for i in range(count)])


def fine_exchange(own, low, high, scalars=None):
    if scalars is None:
        above, below = shift(low, "gz", 1), shift(high, "gz", -1)
    else:
        above = shift(jnp.concatenate([low.reshape(12, 8, 128), scalars[None]]), "gz", 1)
        below = shift(jnp.concatenate([high.reshape(12, 8, 128), scalars[None]]), "gz", -1)
        two = scalars + below[12]
        three = two + above[12]
        above, below = above[:12].reshape(6, 16, 128), below[:12].reshape(6, 16, 128)
    first = jnp.concatenate([own[..., :5, :, :], above[..., 4:5, :, :], below[..., 4:5, :, :]], axis=-3)
    last = jnp.concatenate([own[..., 11:, :, :], above[..., 5:6, :, :], below[..., 5:6, :, :]], axis=-3)
    before, after = shift(last, "gx", -1), shift(first, "gx", 1)
    parts = [own, above[..., :4, :, :], below[..., :4, :, :], before, after, own[..., :2, :, :]]
    body = jnp.concatenate(parts, axis=-3).reshape(-1, 128)
    tiles = body.shape[0] // 16 // 8 * 5
    upper, lower = call(pack_rows_kernel, [shape(tiles, 8, 128)] * 2, count=1)(body)
    if scalars is not None:
        upper, lower, two, three = lax.optimization_barrier((upper, lower, two, three))
    upper, lower = shift(upper, "gy", 1), shift(lower, "gy", -1)
    if scalars is not None:
        scalars = (three + shift(three, "gz", 3)) + shift(two, "gz", -2)
    return (body, upper, lower), scalars


def gather(unit):
    count = lax.axis_size("gx") * lax.axis_size("gy")
    return lax.all_to_all(jnp.broadcast_to(unit[None], (count,) + unit.shape), ("gx", "gy"), 0, 0, tiled=True)


def total(v):
    axes = ("gx", "gy", "gz")
    count = lax.axis_size("gx") * lax.axis_size("gy") * lax.axis_size("gz")
    parts = lax.all_to_all(jnp.broadcast_to(v[None, :1], (count, 1, 128)), axes, 0, 0, tiled=True)
    return jnp.broadcast_to(parts.sum(0), (8, 128))


def local(right_side, classes, table):
    def scratch(*shapes):
        return [pltpu.VMEM(s, F32) for s in shapes]

    block, halo, mids = shape(*BLOCK), shape(*HALO), shape(*MID)
    packs, tile = shape(6, 16, 128), shape(8, 128)
    down_scratch = scratch(HALO, MID, (2, 4, 16, 128), (16 * UNITS, 128))
    up_scratch = scratch((18, 16, 256), (18, 16, 256), (18, 16, 256), (6, 32, 256), MID, MID, HALO, HALO)

    both, low, high = call(
        prepare_kernel, [shape(2, *BLOCK), shape(2, 6, 16, 128), shape(2, 6, 16, 128)],
        [pltpu.VMEM(BLOCK, jnp.int32), pltpu.SMEM((CLASSES,), F32), pltpu.SemaphoreType.DMA((3,))], specs=[ANY] * 3, grant=60,
    )(right_side, classes, table)
    halos, _ = fine_exchange(both, low, high)
    weight0, weight1, x0, x1, unit = call(
        first_down_kernel, [halo, mids, halo, mids, shape(2, 8, 128)], down_scratch + scratch((16 * UNITS, 128)), count=3
    )(*halos)
    weight2, u0, w0, low, high, dots = call(
        first_up_kernel, [shape(18, 16, 256), block, block, packs, packs, tile], up_scratch, count=6
    )(gather(unit), weight1, weight0, x0, x1, both)

    down = call(down_kernel, [halo, mids, tile], down_scratch, count=5)
    halos, scalars = fine_exchange(w0, low, high, dots)
    x0, x1, unit = down(*halos, weight0, weight1)
    free = (iota((8, 128), 0) >= 4) & (iota((8, 128), 1) >= 32) & (iota((8, 128), 1) < 96)
    unit = jnp.where(free, scalars, unit)
    m0, n0, r1, u1, w1, low, high, first = call(
        second_up_kernel, [block] * 5 + [packs, packs, tile], up_scratch, count=9
    )(gather(unit[None]), weight2, weight1, weight0, x0, x1, both, u0, w0)

    halos, _ = fine_exchange(w1, low, high)
    x0, x1, unit = down(*halos, weight0, weight1)
    m1, n1, dots = call(third_up_kernel, [block] * 2 + [tile], up_scratch, count=13)(
        gather(unit[None]), weight2, weight1, weight0, x0, x1, both, w0, m0, n0, r1, u1, w1
    )
    field, residual = call(finish_kernel, [block] * 2, count=11)(
        first, total(dots), u0, w0, m0, n0, r1, u1, w1, m1, n1
    )
    return field, residual


def solution(mesh):
    in_specs = (P("gx", "gy", "gz"), P("gx", "gy", "gz"), P())
    out_specs = (P("gx", "gy", "gz"), P("gx", "gy", "gz"))
    return jax.shard_map(local, mesh=mesh, in_specs=in_specs, out_specs=out_specs, check_vma=False)
```

```python
import jax
import jax.numpy as jnp
from jax import lax
from jax.experimental import pallas as pl
from jax.experimental.pallas import tpu as pltpu
from jax.sharding import PartitionSpec as P

CLASSES = 16
COARSE_SWEEPS = 6
OMEGA = 0.8
KEEP = 1.0 - OMEGA
F32 = jnp.float32
SLABS, MIDS, UNITS = 26, 12, 40
MARK = 64
BLOCK, HALO, MID = (16, 16, 128), (SLABS, 32, 256), (MIDS, 32, 256)
VMEM = pl.BlockSpec(memory_space=pltpu.VMEM)
ANY = pl.BlockSpec(memory_space=pl.ANY)


def iota(shape, dim):
    return lax.broadcasted_iota(jnp.int32, shape, dim)


def roll(v, shift, axis):
    shift = shift % v.shape[axis]
    return v if shift == 0 else pltpu.roll(v, shift, axis)


def around(v, rows, lanes):
    return (roll(v, rows, 0) + roll(v, -rows, 0)) + (roll(v, lanes, 1) + roll(v, -lanes, 1))


def pair_mean(v, step):
    rows = (iota(v.shape, 0) // step) % 2 == 0
    v = v + jnp.where(rows, roll(v, -step, 0), roll(v, step, 0))
    lanes = (iota(v.shape, 1) // step) % 2 == 0
    v = v + jnp.where(lanes, roll(v, -step, 1), roll(v, step, 1))
    return v * 0.125


def place():
    return tuple(lax.axis_index(axis) for axis in ("gx", "gy", "gz"))


def sizes():
    return tuple(lax.axis_size(axis) for axis in ("gx", "gy", "gz"))


def pack_fine(read, low_ref, high_ref):
    lane = iota((16, 128), 1)
    chunk = lane // 32
    for g in range(4):
        low = high = None
        for j in range(4):
            v = read(4 * g + j)
            first, last = roll(v, 32 * j, 1), roll(v, 32 * j + 32, 1)
            low = first if j == 0 else jnp.where(chunk == j, first, low)
            high = last if j == 0 else jnp.where(chunk == j, last, high)
        low_ref[g] = low
        high_ref[g] = high
    for g, slabs in ((4, (0, 1, 2, 3, 4)), (5, (15, 14, 13, 12, 11))):
        low, high = read(slabs[0]), roll(read(slabs[0]), 32, 1)
        for j in range(1, 5):
            v, here = read(slabs[j]), (lane >= 112 if j == 4 else chunk == j)
            low = jnp.where(here, roll(v, 112 if j == 4 else 32 * j, 1), low)
            high = jnp.where(here, roll(v, (32, 64, 96, 112, 0)[j], 1), high)
        low_ref[g] = low
        high_ref[g] = high


def pack_near(read, low_ref, high_ref):
    lane = iota((16, 128), 1)
    near_low = near_high = None
    for g in range(4):
        low = high = None
        for j in range(4):
            k = 4 * g + j
            v = read(k)
            first, last = roll(v, 32 * j, 1), roll(v, 32 * j + 32, 1)
            low = first if j == 0 else jnp.where(lane // 32 == j, first, low)
            high = last if j == 0 else jnp.where(lane // 32 == j, last, high)
            first, last = roll(v, 8 * k, 1), roll(v, 8 * k + 8, 1)
            near_low = first if k == 0 else jnp.where(lane // 8 == k, first, near_low)
            near_high = last if k == 0 else jnp.where(lane // 8 == k, last, near_high)
        low_ref[g] = low
        high_ref[g] = high
    low_ref[4] = near_low
    high_ref[4] = near_high


def prepare_kernel(rhs_in, classes_in, table_in, both, low, high, classes, table, sems):
    copies = [
        pltpu.make_async_copy(rhs_in, both.at[0], sems.at[0]),
        pltpu.make_async_copy(classes_in, classes, sems.at[1]),
        pltpu.make_async_copy(table_in, table, sems.at[2]),
    ]
    for copy in copies:
        copy.start()
    for copy in copies:
        copy.wait()
    for k in range(16):
        c = classes[k]
        v = jnp.zeros((16, 128), F32)
        for index in range(CLASSES):
            v = jnp.where(c == index, table[index], v)
        both[1, k] = v
    for t in range(2):
        pack_fine(lambda k, t=t: both[t, k], low.at[t], high.at[t])


def slab_sources(i):
    x = i - 5
    if 0 <= x < 16:
        return x, 16 + x // 4, 20 + x // 4, -32 * (x % 4), 96 - 32 * (x % 4)
    base, far = (24, -1 - x) if x < 0 else (31, x - 16)
    return base + (x + 5 if x < 0 else far), base + 5, base + 6, (0, -32, -64, -96, -112)[far], (96, 64, 32, 16, 0)[far]


def near_sources(i):
    x = i - 5
    base, above, k = (x, 16, x) if 0 <= x < 16 else ((23 + x, 23, 16 + x) if x < 0 else (x + 9, 30, x - 16))
    return base, above, above + 1, -8 * k, 120 - 8 * k


def assemble_fine(body, sides, i, sources=slab_sources):
    def unit(u):
        return jnp.concatenate([body[u][...], sides[u][...]], axis=0)

    main, above, below, up, down = sources(i)
    lane = iota((32, 128), 1)
    side = jnp.where(lane < 64, roll(unit(above), up, 1), roll(unit(below), down, 1))
    return jnp.concatenate([unit(main), side], axis=1)


def pack_rows_kernel(body, upper, lower):
    for g in range(body.shape[0] // 128):
        for t in range(5):
            upper[5 * g + t] = body[pl.ds(128 * g + t, 8, stride=16), :]
            lower[5 * g + t] = body[pl.ds(128 * g + 11 + t, 8, stride=16), :]


def units(body, first, count):
    return [body.at[pl.ds(first + 16 * u, 16)] for u in range(count)]


def unpack_rows(upper, lower, first, sides):
    sides[...] = jnp.zeros(sides.shape, F32)
    for g in range(sides.shape[0] // 128):
        for t in range(5):
            sides[pl.ds(128 * g + t, 8, stride=16), :] = upper[first + 5 * g + t]
            sides[pl.ds(128 * g + 11 + t, 8, stride=16), :] = lower[first + 5 * g + t]
    return units(sides, 0, sides.shape[0] // 16)


def near(lane):
    return (lane < 160) | (lane >= 224)


def inside_lanes(lane):
    z = jnp.where(lane < 192, lane, lane - 256) + 128 * place()[2]
    return near(lane) & (z >= 0) & (z < 128 * sizes()[2])


def inside_fine():
    row, lane = iota((32, 256), 0), iota((32, 256), 1)
    y = jnp.where(row < 24, row, row - 32) + 16 * place()[1]
    return inside_lanes(lane) & (y >= 0) & (y < 16 * sizes()[1])


def fine_weights(body, sides, weight0, weight1, middle, quads, unit):
    inside, gx, nx = inside_fine(), place()[0], sizes()[0]

    def weigh(i):
        kap = assemble_fine(body, sides, i)
        x = 16 * gx + (i - 5)
        weight0[i] = jnp.where(inside & (x >= 0) & (x < 16 * nx), OMEGA / (kap + 6.0), 0.0)
        return kap

    weigh(0)
    weigh(SLABS - 1)
    for m in range(MIDS):
        kap1 = pair_mean(weigh(2 * m + 1) + weigh(2 * m + 2), 1)
        middle[m] = kap1
        x = 8 * gx + (m - 2)
        weight1[m] = jnp.where(inside & (x >= 0) & (x < 8 * nx), OMEGA / (kap1 + 1.5), 0.0)
    for c in range(4):
        kap2 = pair_mean(middle[2 + 2 * c] + middle[3 + 2 * c], 2)[:16]
        weight2 = OMEGA / (kap2 + 0.375)
        quads[0, c], quads[1, c] = weight2[:, :128], weight2[:, 128:]
    pack_coarse(quads, unit)


def pack_coarse(quads, unit):
    turn = iota((4, 128), 1) % 4
    for half in range(2):
        v = quads[half, 0, pl.ds(0, 4, stride=4), :]
        for c in range(1, 4):
            v = jnp.where(turn == c, quads[half, c, pl.ds(0, 4, stride=4), :], v)
        unit[4 * half:4 * half + 4] = v


def down_sweep(body, sides, weight0, weight1, x0, x1, unit, r, r1, quads):
    for i in range(SLABS):
        v = assemble_fine(body, sides, i)
        r[i] = v
        x0[i] = weight0[i] * v
    for m in range(MIDS):
        i = 2 * m + 1
        two = x0[i] + x0[i + 1]
        left = KEEP * (r[i] + r[i + 1]) + ((x0[i - 1] + x0[i + 2]) + two) + around(two, 1, 1)
        v = pair_mean(left, 1)
        r1[m] = v
        x1[m] = weight1[m] * v
    for c in range(4):
        m = 2 + 2 * c
        two = x1[m] + x1[m + 1]
        left = KEEP * (r1[m] + r1[m + 1]) + 0.25 * (((x1[m - 1] + x1[m + 2]) + two) + around(two, 2, 2))
        v = pair_mean(left, 2)[:16]
        quads[0, c], quads[1, c] = v[:, :128], v[:, 128:]
    pack_coarse(quads, unit)


def first_down_kernel(body, upper, lower, weight0, weight1, x0, x1, unit, r, r1, quads, sides, more):
    kap_sides = unpack_rows(upper, lower, 5 * UNITS // 8, more)
    fine_weights(units(body, 16 * UNITS, UNITS), kap_sides, weight0, weight1, r1, quads, unit.at[1])
    r_sides = unpack_rows(upper, lower, 0, sides)
    down_sweep(units(body, 0, UNITS), r_sides, weight0, weight1, x0, x1, unit.at[0], r, r1, quads)


def share_kernel(own, above, below, weight0, weight1, share, r, x0, r1, x1, quads):
    lane = iota((16, 128), 1)
    for k in range(16):
        up, down = above[k // 4], below[k // 4]
        side = jnp.where(lane < 64, roll(up, -32 * (k % 4), 1), roll(down, 96 - 32 * (k % 4), 1))
        v = jnp.concatenate([own[k], side], axis=1)
        r[k] = v
        x0[k] = weight0[k + 5, :16] * v
    zero = jnp.zeros((16, 256), F32)

    def tall(v):
        return jnp.concatenate([v, zero], axis=0)

    for m in range(10):
        x = 2 * (m - 1)
        if m == 0:
            left = tall(x0[0])
        elif m == 9:
            left = tall(x0[15])
        else:
            two = x0[x] + x0[x + 1]
            flat = KEEP * (r[x] + r[x + 1]) + two
            flat = flat + x0[x - 1] if x > 0 else flat
            flat = flat + x0[x + 2] if x < 14 else flat
            left = tall(flat) + around(tall(two), 1, 1)
        v = pair_mean(left, 1)
        r1[m] = v
        x1[m] = weight1[m + 1] * v
    for c in range(6):
        pair = [m for m in (2 * c - 1, 2 * c) if 0 <= m < 10]
        two = sum(x1[m] for m in pair)
        left = KEEP * sum(r1[m] for m in pair)
        beside = two + around(two, 2, 2)
        for m in (2 * c - 2, 2 * c + 1):
            beside = beside + x1[m] if 0 <= m < 10 else beside
        v = pair_mean(left + 0.25 * beside, 2)
        quads[0, c], quads[1, c] = v[:, :128], v[:, 128:]
    gy = place()[1]
    for half in range(2):
        for start, count, first in ((28, 1, 0), (0, 5, 1)):
            turn = iota((count, 128), 1) % 4
            inside = gy > 0 if count == 1 else (iota((count, 128), 0) < 4) | (gy < sizes()[1] - 1)

            def rows(c):
                v = quads[half, c, pl.ds(start, count, stride=4), :] if count > 1 else quads[half, c, pl.ds(start, 1), :]
                return jnp.where(inside, v, 0.0)

            v = rows(1)
            for c in range(1, 4):
                v = jnp.where(turn == c, rows(c + 1), v)
            share[pl.ds(6 * half + first, count)] = v
            v = jnp.where(turn == 3, rows(0), jnp.where(turn == 0, rows(5), 0.0))
            share[pl.ds(12 + 6 * half + first, count)] = v


def pack_both_kernel(body, own, next1, next2, next3, upper, lower, coarse, stage):
    pack_rows_kernel(body, upper, lower)
    gx = place()[0]
    for k, share in enumerate((own, next1, next2, next3)):
        stage[lax.rem(gx + k, 4)] = share[...]
    turn = iota((12, 128), 1) % 4
    for b in range(4):
        v = stage[b, :12]
        if b < 3:
            v = v + jnp.where(turn == 3, stage[b + 1, 12:], 0.0)
        if b > 0:
            v = v + jnp.where(turn == 0, stage[b - 1, 12:], 0.0)
        coarse[pl.ds(12 * b, 12)] = v


def near_sweep(body, upper, lower, weight0, weight1, x0, x1, r, sides):
    here, there = units(body, 0, 32), unpack_rows(upper, lower, 0, sides)
    for i in range(SLABS):
        v = assemble_fine(here, there, i, near_sources)
        r[i] = v
        x0[i] = weight0[i] * v
    for m in range(MIDS):
        i = 2 * m + 1
        two = x0[i] + x0[i + 1]
        left = KEEP * (r[i] + r[i + 1]) + ((x0[i - 1] + x0[i + 2]) + two) + around(two, 1, 1)
        x1[m] = weight1[m] * pair_mean(left, 1)


def unfold(v, k, out, change):
    turn = iota((16, 256), 1) % 4
    moved = {d: roll(v, d, 1) for d in range(-3, 4)}
    for c in range(4):
        slab = moved[-c]
        for j in range(1, 4):
            slab = jnp.where(turn == j, moved[j - c], slab)
        out[4 * k + c + 1] = change(4 * k + c + 1, slab)


def assemble_shares(own, up1, down1, up2, down2, out, change):
    def zeros(n):
        return jnp.zeros((n, 128), F32)

    for k in range(4):
        halves = []
        for s in (12 * k, 12 * k + 6):
            v = jnp.concatenate([own[s + 1:s + 6], zeros(10), own[s:s + 1]], axis=0)
            v = v + jnp.concatenate([zeros(3), up1[s:s + 6], zeros(7)], axis=0)
            v = v + jnp.concatenate([zeros(7), up2[s:s + 3], zeros(6)], axis=0)
            v = v + jnp.concatenate([down1[s + 5:s + 6], zeros(10), down1[s:s + 5]], axis=0)
            v = v + jnp.concatenate([zeros(10), down2[s + 3:s + 6], zeros(3)], axis=0)
            halves.append(v)
        unfold(jnp.concatenate(halves, axis=1), k, out, change)


def assemble_coarse(gather, t, out, change):
    gy, ny = place()[1], sizes()[1]
    for k in range(4):
        own, up1, up2, down2, down1 = [ny * k + lax.rem(gy + d + ny, ny) for d in (0, 1, 2, -2, -1)]
        v = jnp.concatenate(
            [
                jnp.concatenate([
                    gather[own, t, s:s + 4], gather[up1, t, s:s + 4], gather[up2, t, s:s + 2],
                    gather[down2, t, s + 2:s + 4], gather[down1, t, s:s + 4],
                ], axis=0)
                for s in (0, 4)
            ],
            axis=1,
        )
        unfold(v, k, out, change)


def up_sweep(assemble, weight2, weight1, weight0, x0, x1, kap, u, w, a, b, rhs2, spread, middle, t1, t0):
    zero = jnp.zeros((16, 256), F32)
    for ref in (a, b):
        ref[0] = zero
        ref[17] = zero
    assemble(rhs2, lambda s, v: weight2[s] * v)
    for s in range(1, 17):
        a[s] = rhs2[s]
    for sweep in range(COARSE_SWEEPS - 1):
        old, new = (a, b) if sweep % 2 == 0 else (b, a)

        for s in range(1, 17):
            v = old[s]
            beside = (old[s - 1] + old[s + 1]) + around(v, 1, 4)
            new[s] = (KEEP * v + rhs2[s]) + weight2[s] * (0.0625 * beside)
    last = b if COARSE_SWEEPS % 2 == 0 else a
    half = iota((8, 256), 0) < 4
    for c in range(6):
        v = last[4 * place()[0] + c]
        spread[c] = jnp.concatenate(
            [
                jnp.where(half, jnp.broadcast_to(v[j:j + 1], (8, 256)), jnp.broadcast_to(v[j + 1:j + 2], (8, 256)))
                for j in (0, 2, 4, 14)
            ],
            axis=0,
        )
    for m in range(MIDS):
        t1[m] = x1[m] + spread[m // 2]
    for m in range(1, MIDS - 1):
        v = t1[m]
        beside = (t1[m - 1] + t1[m + 1]) + around(v, 2, 2)
        middle[m] = (KEEP * v + x1[m]) + weight1[m] * (0.25 * beside)
    for i in range(3, SLABS - 3):
        t0[i] = x0[i] + middle[(i - 1) // 2]
    for i in range(4, SLABS - 4):
        v = t0[i]
        beside = (t0[i - 1] + t0[i + 1]) + around(v, 1, 1)
        u[i] = (KEEP * v + x0[i]) + weight0[i] * beside
    for i in range(5, SLABS - 5):
        v = u[i]
        beside = (u[i - 1] + u[i + 1]) + around(v, 1, 1)
        w[i - 5] = (kap[i - 5] + 6.0) * v[:16, :128] - beside[:16, :128]


def lanes_of(values):
    lane = iota((8, 128), 1)
    out = jnp.zeros((8, 128), F32)
    for k, v in enumerate(values):
        out = jnp.where(lane == MARK + k, jnp.sum(v), out)
    return out


def first_up_kernel(gather, weight1, weight0, x0, x1, both, weight2, u, w, low, high, dots, *scratch):
    (*scratch, full) = scratch
    row, lane = iota((16, 256), 0), iota((16, 256), 1)
    y = jnp.where(row < 10, row, row - 16) + 4 * place()[1]
    inside = inside_lanes(lane) & (y >= 0) & (y < 4 * sizes()[1])
    assemble_coarse(gather, 1, weight2, lambda s, v: jnp.where(inside, v, 0.0))
    up_sweep(lambda *a: assemble_coarse(gather, 0, *a), weight2, weight1, weight0, x0, x1, both.at[1], full, w, *scratch)
    rz = curve = jnp.zeros((16, 128), F32)
    for k in range(16):
        v = full[k + 5][:16, :128]
        u[k] = v
        rz = rz + both[0, k] * v
        curve = curve + w[k] * v
    dots[...] = lanes_of([rz, curve])
    pack_near(lambda k: w[k], low, high)


def whole_sweep(body, upper, lower, shares, weight2, weight1, weight0, kap, full, w, x0, x1, r, sides, *scratch):
    near_sweep(body, upper, lower, weight0, weight1, x0, x1, r, sides)
    up_sweep(lambda *a: assemble_shares(*shares, *a), weight2, weight1, weight0, x0, x1, kap, full, w, *scratch)


def second_kernel(body, upper, lower, own, up1, down1, up2, down2, weight2, weight1, weight0, both, m0, n0, low, high, full, *scratch):
    shares = (own, up1, down1, up2, down2)
    whole_sweep(body, upper, lower, shares, weight2, weight1, weight0, both.at[1], full, n0, *scratch)
    for k in range(16):
        m0[k] = full[k + 5, :16, :128]
    pack_near(lambda k: n0[k], low, high)


def third_kernel(body, upper, lower, own, up1, down1, up2, down2, weight2, weight1, weight0, both, first, u0, w0, m0, n0,
                 r1, u1, w1, m1, n1, dots, full, last, *scratch):
    shares = (own, up1, down1, up2, down2)
    whole_sweep(body, upper, lower, shares, weight2, weight1, weight0, both.at[1], full, last, *scratch)
    alpha = first[0:1, MARK:MARK + 1] / first[0:1, MARK + 1:MARK + 2]
    sums = [jnp.zeros((16, 128), F32)] * 12
    for k in range(16):
        vw0, vm0, vn0 = w0[k], m0[k], n0[k]
        vr1 = both[0, k] - alpha * vw0
        vu1 = u0[k] - alpha * vm0
        vw1 = vw0 - alpha * vn0
        vm1 = vm0 - alpha * full[k + 5, :16, :128]
        vn1 = vn0 - alpha * last[k]
        r1[k], u1[k], w1[k], m1[k], n1[k] = vr1, vu1, vw1, vm1, vn1
        terms = [vr1 * vu1, vr1 * vm1, vr1 * vm0, vw1 * vu1, vw1 * vm1, vw1 * vm0,
                 vw0 * vu1, vw0 * vm1, vw0 * vm0, vn1 * vm1, vn1 * vm0, vn0 * vm0]
        sums = [s + t for s, t in zip(sums, terms)]
    dots[...] = lanes_of(sums)


def finish_kernel(first, second, u0, w0, m0, n0, r1, u1, w1, m1, n1, field, residual):
    g0, d0 = first[0:1, MARK:MARK + 1], first[0:1, MARK + 1:MARK + 2]
    (r1u1, r1m1, r1m0, w1u1, w1m1, w1m0, w0u1, w0m1, w0m0, n1m1, n1m0, n0m0) = [
        second[0:1, MARK + k:MARK + k + 1] for k in range(12)
    ]
    alpha0 = g0 / d0
    beta1 = r1u1 / g0
    curve1 = w1u1 + 2.0 * beta1 * w0u1 + beta1 * beta1 * d0
    alpha1 = r1u1 / curve1
    ab = alpha1 * beta1
    su = w1u1 + beta1 * w0u1 - alpha1 * (w1m1 + beta1 * w0m1) - ab * (w1m0 + beta1 * w0m0)
    g2 = (r1u1 - alpha1 * r1m1 - ab * r1m0) - alpha1 * su
    beta2 = g2 / r1u1
    uw = (w1u1 - 2.0 * alpha1 * w1m1 - 2.0 * ab * w1m0) + (alpha1 * alpha1 * n1m1 + 2.0 * alpha1 * ab * n1m0 + ab * ab * n0m0)
    curve2 = uw + 2.0 * beta2 * su + beta2 * beta2 * curve1
    alpha2 = g2 / curve2
    mix = alpha1 + alpha2 * beta2
    cu0, cu1, cm1, cm0 = alpha0 + mix * beta1, mix + alpha2, alpha2 * alpha1, alpha2 * ab
    cw0 = mix * beta1
    for k in range(16):
        field[k] = (cu0 * u0[k] + cu1 * u1[k]) - (cm1 * m1[k] + cm0 * m0[k])
        residual[k] = r1[k] - (cw0 * w0[k] + cu1 * w1[k]) + (cm1 * n1[k] + cm0 * n0[k])


def shape(*dims):
    return jax.ShapeDtypeStruct(dims, F32)


def call(kernel, outs, scratch=(), specs=None, count=0, grant=40):
    return pl.pallas_call(
        kernel,
        out_shape=outs,
        in_specs=specs or [VMEM] * count,
        out_specs=[VMEM] * len(outs),
        scratch_shapes=list(scratch),
        compiler_params=pltpu.CompilerParams(vmem_limit_bytes=grant * 1024 * 1024),
    )


def shift(v, axis, distance):
    count = lax.axis_size(axis)
    return lax.ppermute(v, axis, [((i + distance) % count, i) for i in range(count)])


def fine_exchange(own, low, high):
    above, below = shift(low, "gz", 1), shift(high, "gz", -1)
    first = jnp.concatenate([own[:, :5], above[:, 4:5], below[:, 4:5]], axis=1)
    last = jnp.concatenate([own[:, 11:], above[:, 5:6], below[:, 5:6]], axis=1)
    before, after = shift(last, "gx", -1), shift(first, "gx", 1)
    body = jnp.concatenate([own, above[:, :4], below[:, :4], before, after, own[:, :2]], axis=1).reshape(-1, 128)
    upper, lower = call(pack_rows_kernel, [shape(10 * UNITS // 8, 8, 128)] * 2, count=1)(body)
    return body, shift(upper, "gy", 1), shift(lower, "gy", -1)


def stack(*parts):
    return jnp.concatenate([part.reshape(-1, 8, 128) for part in parts])


def spread_rows(*rows):
    rows = jnp.concatenate(rows)
    return jnp.concatenate([rows, jnp.zeros((8 - rows.shape[0], 128), F32)])


def joint_exchange(own, low, high, weight0, weight1, state, final):
    above, below = shift(stack(low, state), "gz", 1), shift(stack(high, state), "gz", -1)
    packs_above, packs_below = above[:10].reshape(5, 16, 128), below[:10].reshape(5, 16, 128)
    if final:
        state = spread_rows(*[state[j:j + 1] + state[j + 1:j + 2] + above[10, j + 1:j + 2] + below[10, j:j + 1] for j in (0, 2, 4)])
    else:
        state = spread_rows(state[:1], above[10, :1])
    share_scratch = [pltpu.VMEM(s, F32) for s in ((16, 16, 256), (16, 16, 256), (10, 32, 256), (10, 32, 256), (2, 6, 32, 128))]
    (share,) = call(share_kernel, [shape(24, 128)], share_scratch, count=5)(own, packs_above, packs_below, weight0, weight1)
    ends = [packs_above[4:], packs_below[4:]]
    small = stack(share, state)
    before, after = shift(stack(own[11:], *ends, small), "gx", -1), shift(stack(own[:5], *ends, small), "gx", 1)
    across = shift(small, "gx", 2)
    if final:
        state = (state + before[17]) + (after[17] + across[3])
    else:
        state = state + shift(state, "gz", 4)
    shares = [v.reshape(24, 128) for v in (share, after[14:17], across[:3], before[14:17])]
    body = stack(own, *ends, before[:14], after[:14]).reshape(512, 128)
    upper, lower, coarse = call(
        pack_both_kernel, [shape(20, 8, 128), shape(20, 8, 128), shape(48, 128)], [pltpu.VMEM((4, 24, 128), F32)], count=5
    )(body, *shares)
    small = stack(coarse, state)
    upper, lower = shift(stack(upper, small), "gy", 1), shift(stack(lower, small), "gy", -1)
    up2, down2 = shift(small, "gy", 2), shift(small, "gy", -2)
    if final:
        state = jnp.broadcast_to(state[:1] + up2[6, 1:2] + down2[6, 2:3], (8, 128))
    else:
        ahead, behind = upper[26, :2] + up2[6, :2], lower[26, :2] + state[:2]
        state = spread_rows(ahead + behind, ahead, behind)
    groups = [coarse] + [v.reshape(48, 128) for v in (upper[20:26], lower[20:26], up2[:6], down2[:6])]
    return [body, upper, lower] + groups, state


def gather(unit):
    count = lax.axis_size("gx") * lax.axis_size("gy")
    return lax.all_to_all(jnp.broadcast_to(unit[None], (count,) + unit.shape), ("gx", "gy"), 0, 0, tiled=True)


def total(v):
    axes = ("gx", "gy", "gz")
    count = lax.axis_size("gx") * lax.axis_size("gy") * lax.axis_size("gz")
    parts = lax.all_to_all(jnp.broadcast_to(v[None, :1], (count, 1, 128)), axes, 0, 0, tiled=True)
    return jnp.broadcast_to(parts.sum(0), (8, 128))


def local(right_side, classes, table):
    def scratch(*shapes):
        return [pltpu.VMEM(s, F32) for s in shapes]

    block, halo, mids = shape(*BLOCK), shape(*HALO), shape(*MID)
    packs, tile = shape(5, 16, 128), shape(8, 128)
    down_scratch = scratch(HALO, MID, (2, 4, 16, 128), (16 * UNITS, 128))
    up_scratch = scratch((18, 16, 256), (18, 16, 256), (18, 16, 256), (6, 32, 256), MID, MID, HALO, HALO)

    both, low, high = call(
        prepare_kernel, [shape(2, *BLOCK), shape(2, 6, 16, 128), shape(2, 6, 16, 128)],
        [pltpu.VMEM(BLOCK, jnp.int32), pltpu.SMEM((CLASSES,), F32), pltpu.SemaphoreType.DMA((3,))], specs=[ANY] * 3, grant=60,
    )(right_side, classes, table)
    halos = fine_exchange(both, low, high)
    weight0, weight1, x0, x1, unit = call(
        first_down_kernel, [halo, mids, halo, mids, shape(2, 8, 128)], down_scratch + scratch((16 * UNITS, 128)), count=3
    )(*halos)
    weight2, u0, w0, low, high, dots = call(
        first_up_kernel, [shape(18, 16, 256), block, block, packs, packs, tile], up_scratch, count=6
    )(gather(unit), weight1, weight0, x0, x1, both)

    whole_scratch = scratch(HALO, MID, HALO, (512, 128)) + up_scratch[:-1]
    halos, state = joint_exchange(w0, low, high, weight0, weight1, dots, False)
    m0, n0, low, high = call(second_kernel, [block, block, packs, packs], scratch(HALO) + whole_scratch, count=12)(
        *halos, weight2, weight1, weight0, both
    )
    halos, first = joint_exchange(n0, low, high, weight0, weight1, state, True)
    r1, u1, w1, m1, n1, dots = call(
        third_kernel, [block] * 5 + [tile], scratch(HALO, BLOCK) + whole_scratch, count=17
    )(*halos, weight2, weight1, weight0, both, first, u0, w0, m0, n0)
    field, residual = call(finish_kernel, [block] * 2, count=11)(
        first, total(dots), u0, w0, m0, n0, r1, u1, w1, m1, n1
    )
    return field, residual


def solution(mesh):
    in_specs = (P("gx", "gy", "gz"), P("gx", "gy", "gz"), P())
    out_specs = (P("gx", "gy", "gz"), P("gx", "gy", "gz"))
    return jax.shard_map(local, mesh=mesh, in_specs=in_specs, out_specs=out_specs, check_vma=False)
```

```python
import functools

import jax
import jax.numpy as jnp
from jax import lax
from jax.experimental import pallas as pl
from jax.experimental.pallas import tpu as pltpu
from jax.sharding import PartitionSpec as P

CLASSES = 16
COARSE_SWEEPS = 6
OMEGA = 0.8
KEEP = 1.0 - OMEGA
F32 = jnp.float32
SLABS, MIDS, UNITS = 26, 12, 40
MARK = 64
BLOCK, HALO, MID = (16, 16, 128), (SLABS, 32, 256), (MIDS, 32, 256)
VMEM = pl.BlockSpec(memory_space=pltpu.VMEM)
ANY = pl.BlockSpec(memory_space=pl.ANY)


def iota(shape, dim):
    return lax.broadcasted_iota(jnp.int32, shape, dim)


def roll(v, shift, axis):
    shift = shift % v.shape[axis]
    return v if shift == 0 else pltpu.roll(v, shift, axis)


def around(v, rows, lanes):
    return (roll(v, rows, 0) + roll(v, -rows, 0)) + (roll(v, lanes, 1) + roll(v, -lanes, 1))


def pair_mean(v, step):
    rows = (iota(v.shape, 0) // step) % 2 == 0
    v = v + jnp.where(rows, roll(v, -step, 0), roll(v, step, 0))
    lanes = (iota(v.shape, 1) // step) % 2 == 0
    v = v + jnp.where(lanes, roll(v, -step, 1), roll(v, step, 1))
    return v * 0.125


def place():
    return tuple(lax.axis_index(axis) for axis in ("gx", "gy", "gz"))


def sizes():
    return tuple(lax.axis_size(axis) for axis in ("gx", "gy", "gz"))


def pack_fine(read, low_ref, high_ref):
    lane = iota((16, 128), 1)
    chunk = lane // 32
    for g in range(4):
        low = high = None
        for j in range(4):
            v = read(4 * g + j)
            first, last = roll(v, 32 * j, 1), roll(v, 32 * j + 32, 1)
            low = first if j == 0 else jnp.where(chunk == j, first, low)
            high = last if j == 0 else jnp.where(chunk == j, last, high)
        low_ref[g] = low
        high_ref[g] = high
    for g, slabs in ((4, (0, 1, 2, 3, 4)), (5, (15, 14, 13, 12, 11))):
        low, high = read(slabs[0]), roll(read(slabs[0]), 32, 1)
        for j in range(1, 5):
            v, here = read(slabs[j]), (lane >= 112 if j == 4 else chunk == j)
            low = jnp.where(here, roll(v, 112 if j == 4 else 32 * j, 1), low)
            high = jnp.where(here, roll(v, (32, 64, 96, 112, 0)[j], 1), high)
        low_ref[g] = low
        high_ref[g] = high


def pack_near(read, low_ref, high_ref):
    chunk = iota((16, 128), 1) // 8
    low = high = None
    for k in range(16):
        v = read(k)
        first, last = roll(v, 8 * k, 1), roll(v, 8 * k + 8, 1)
        low = first if k == 0 else jnp.where(chunk == k, first, low)
        high = last if k == 0 else jnp.where(chunk == k, last, high)
    low_ref[...] = low
    high_ref[...] = high


def prepare_kernel(rhs_in, classes_in, table_in, both, low, high, classes, table, sems):
    copies = [
        pltpu.make_async_copy(rhs_in, both.at[0], sems.at[0]),
        pltpu.make_async_copy(classes_in, classes, sems.at[1]),
        pltpu.make_async_copy(table_in, table, sems.at[2]),
    ]
    for copy in copies:
        copy.start()
    for copy in copies:
        copy.wait()
    for k in range(16):
        c = classes[k]
        v = jnp.zeros((16, 128), F32)
        for index in range(CLASSES):
            v = jnp.where(c == index, table[index], v)
        both[1, k] = v
    for t in range(2):
        pack_fine(lambda k, t=t: both[t, k], low.at[t], high.at[t])


def slab_sources(i):
    x = i - 5
    if 0 <= x < 16:
        return x, 16 + x // 4, 20 + x // 4, -32 * (x % 4), 96 - 32 * (x % 4)
    base, far = (24, -1 - x) if x < 0 else (31, x - 16)
    return base + (x + 5 if x < 0 else far), base + 5, base + 6, (0, -32, -64, -96, -112)[far], (96, 64, 32, 16, 0)[far]


def near_sources(i):
    x = i - 5
    base, above, k = (x, 16, x) if 0 <= x < 16 else ((23 + x, 23, 16 + x) if x < 0 else (x + 9, 30, x - 16))
    return base, above, above + 1, -8 * k, 120 - 8 * k


def assemble_fine(body, sides, i, sources=slab_sources):
    def unit(u):
        return jnp.concatenate([body[u][...], sides[u][...]], axis=0)

    main, above, below, up, down = sources(i)
    lane = iota((32, 128), 1)
    side = jnp.where(lane < 64, roll(unit(above), up, 1), roll(unit(below), down, 1))
    return jnp.concatenate([unit(main), side], axis=1)


def pack_rows_kernel(body, upper, lower):
    for g in range(body.shape[0] // 128):
        for t in range(5):
            here = pl.ds(8 * (5 * g + t), 8)
            upper[here] = body[pl.ds(128 * g + t, 8, stride=16), :]
            lower[here] = body[pl.ds(128 * g + 11 + t, 8, stride=16), :]


def units(body, first, count):
    return [body.at[pl.ds(first + 16 * u, 16)] for u in range(count)]


def unpack_rows(upper, lower, first, sides):
    sides[...] = jnp.zeros(sides.shape, F32)
    for g in range(sides.shape[0] // 128):
        for t in range(5):
            here = pl.ds(8 * (first + 5 * g + t), 8)
            sides[pl.ds(128 * g + t, 8, stride=16), :] = upper[here]
            sides[pl.ds(128 * g + 11 + t, 8, stride=16), :] = lower[here]
    return units(sides, 0, sides.shape[0] // 16)


def near(lane):
    return (lane < 160) | (lane >= 224)


def inside_lanes(lane):
    z = jnp.where(lane < 192, lane, lane - 256) + 128 * place()[2]
    return near(lane) & (z >= 0) & (z < 128 * sizes()[2])


def inside_fine():
    row, lane = iota((32, 256), 0), iota((32, 256), 1)
    y = jnp.where(row < 24, row, row - 32) + 16 * place()[1]
    return inside_lanes(lane) & (y >= 0) & (y < 16 * sizes()[1])


def fine_weights(body, sides, weight0, weight1, middle, quads, unit):
    inside, gx, nx = inside_fine(), place()[0], sizes()[0]

    def weigh(i):
        kap = assemble_fine(body, sides, i)
        x = 16 * gx + (i - 5)
        weight0[i] = jnp.where(inside & (x >= 0) & (x < 16 * nx), OMEGA / (kap + 6.0), 0.0)
        return kap

    weigh(0)
    weigh(SLABS - 1)
    for m in range(MIDS):
        kap1 = pair_mean(weigh(2 * m + 1) + weigh(2 * m + 2), 1)
        middle[m] = kap1
        x = 8 * gx + (m - 2)
        weight1[m] = jnp.where(inside & (x >= 0) & (x < 8 * nx), OMEGA / (kap1 + 1.5), 0.0)
    for c in range(4):
        kap2 = pair_mean(middle[2 + 2 * c] + middle[3 + 2 * c], 2)[:16]
        weight2 = OMEGA / (kap2 + 0.375)
        quads[0, c], quads[1, c] = weight2[:, :128], weight2[:, 128:]
    pack_coarse(quads, unit)


def pack_coarse(quads, unit):
    turn = iota((4, 128), 1) % 4
    for half in range(2):
        v = quads[half, 0, pl.ds(0, 4, stride=4), :]
        for c in range(1, 4):
            v = jnp.where(turn == c, quads[half, c, pl.ds(0, 4, stride=4), :], v)
        unit[4 * half:4 * half + 4] = v


def down_sweep(body, sides, weight0, weight1, x0, x1, unit, r, r1, quads):
    for i in range(SLABS):
        v = assemble_fine(body, sides, i)
        r[i] = v
        x0[i] = weight0[i] * v
    for m in range(MIDS):
        i = 2 * m + 1
        two = x0[i] + x0[i + 1]
        left = KEEP * (r[i] + r[i + 1]) + ((x0[i - 1] + x0[i + 2]) + two) + around(two, 1, 1)
        v = pair_mean(left, 1)
        r1[m] = v
        x1[m] = weight1[m] * v
    for c in range(4):
        m = 2 + 2 * c
        two = x1[m] + x1[m + 1]
        left = KEEP * (r1[m] + r1[m + 1]) + 0.25 * (((x1[m - 1] + x1[m + 2]) + two) + around(two, 2, 2))
        v = pair_mean(left, 2)[:16]
        quads[0, c], quads[1, c] = v[:, :128], v[:, 128:]
    pack_coarse(quads, unit)


def first_down_kernel(body, upper, lower, weight0, weight1, x0, x1, unit, r, r1, quads, sides, more):
    kap_sides = unpack_rows(upper, lower, 5 * UNITS // 8, more)
    fine_weights(units(body, 16 * UNITS, UNITS), kap_sides, weight0, weight1, r1, quads, unit.at[1])
    r_sides = unpack_rows(upper, lower, 0, sides)
    down_sweep(units(body, 0, UNITS), r_sides, weight0, weight1, x0, x1, unit.at[0], r, r1, quads)


def share_sweep(block, weight0, weight1, share, x0, r1, x1, quads):
    for k in range(16):
        x0[k] = weight0[k + 5, :16, :128] * block[k]
    zero, low = jnp.zeros((16, 128), F32), jnp.zeros((16, 256), F32)

    def tall(v):
        return jnp.concatenate([jnp.concatenate([v, zero], axis=1), low], axis=0)

    for m in range(10):
        x = 2 * (m - 1)
        if m == 0:
            left = tall(x0[0])
        elif m == 9:
            left = tall(x0[15])
        else:
            two = x0[x] + x0[x + 1]
            flat = KEEP * (block[x] + block[x + 1]) + two
            flat = flat + x0[x - 1] if x > 0 else flat
            flat = flat + x0[x + 2] if x < 14 else flat
            left = tall(flat) + around(tall(two), 1, 1)
        v = pair_mean(left, 1)
        r1[m] = v
        x1[m] = weight1[m + 1] * v
    for c in range(6):
        pair = [m for m in (2 * c - 1, 2 * c) if 0 <= m < 10]
        two = sum(x1[m] for m in pair)
        left = KEEP * sum(r1[m] for m in pair)
        beside = two + around(two, 2, 2)
        for m in (2 * c - 2, 2 * c + 1):
            beside = beside + x1[m] if 0 <= m < 10 else beside
        v = pair_mean(left + 0.25 * beside, 2)
        quads[0, c], quads[1, c] = v[:, :128], v[:, 128:]
    gy, gz = place()[1:]
    ny, nz = sizes()[1:]
    for half in range(2):
        for start, count, first in ((28, 1, 0), (0, 5, 1)):
            row, lane = iota((count, 128), 0), iota((count, 128), 1)
            y = row // 4 + gy - (1 if count == 1 else 0)
            inside = (y >= 0) & (y < ny)
            if half == 1:
                z = jnp.where(lane < 64, gz + 1, gz - 1)
                inside = inside & (z >= 0) & (z < nz)

            def rows(c):
                v = quads[half, c, pl.ds(start, count, stride=4), :] if count > 1 else quads[half, c, pl.ds(start, 1), :]
                return jnp.where(inside, v, 0.0)

            turn = lane % 4
            v = rows(1)
            for c in range(1, 4):
                v = jnp.where(turn == c, rows(c + 1), v)
            share[pl.ds(6 * half + first, count)] = v
            v = jnp.where(turn == 3, rows(0), jnp.where(turn == 0, rows(5), 0.0))
            share[pl.ds(12 + 6 * half + first, count)] = v


def join_z_kernel(final, own, share, state, above, below, first, last, small):
    lane = iota((6, 128), 1)
    for s in (0, 12):
        main, side = pl.ds(16 + s, 6), pl.ds(22 + s, 6)
        v = share[s:s + 6] + jnp.where(lane >= 124, above[side], 0.0) + jnp.where(lane < 4, below[side], 0.0)
        small[pl.ds(s, 6)] = v
        v = share[s + 6:s + 12] + jnp.where(lane < 32, above[main], jnp.where(lane >= 96, below[main], 0.0))
        small[pl.ds(s + 6, 6)] = v
    row = iota((8, 128), 0)
    if final:
        sums = [state[j:j + 1] + state[j + 1:j + 2] + above[41 + j:42 + j] + below[40 + j:41 + j] for j in (0, 2, 4)]
    else:
        sums = [state[0:1], above[40:41]]
    v = jnp.zeros((8, 128), F32)
    for j, part in enumerate(sums):
        v = jnp.where(row == j, part, v)
    small[24:32] = v
    for k in range(5):
        first[pl.ds(16 * k, 16)] = own[k]
        last[pl.ds(16 * k, 16)] = own[11 + k]
    for ref in (first, last):
        ref[80:96] = above[:16]
        ref[96:112] = below[:16]
        ref[112:144] = small[...]


def join_x_kernel(final, own, above, below, small, before, after, across, body, upper, lower, ahead, behind, stage):
    for k in range(16):
        body[pl.ds(16 * k, 16)] = own[k]
    body[256:272] = above[:16]
    body[272:288] = below[:16]
    body[288:400] = before[:112]
    body[400:512] = after[:112]
    pack_rows_kernel(body, upper, lower)
    gx = place()[0]
    for k, rows in enumerate((small[:24], after[112:136], across[:24], before[112:136])):
        stage[lax.rem(gx + k, 4)] = rows
    turn = iota((12, 128), 1) % 4
    for b in range(4):
        v = stage[b, :12]
        if b < 3:
            v = v + jnp.where(turn == 3, stage[b + 1, 12:], 0.0)
        if b > 0:
            v = v + jnp.where(turn == 0, stage[b - 1, 12:], 0.0)
        for ref in (upper, lower):
            ref[pl.ds(160 + 12 * b, 12)] = v
        for half in range(2):
            ahead[pl.ds(6 * b + 3 * half, 3)] = v[6 * half:6 * half + 3]
            behind[pl.ds(6 * b + 3 * half, 3)] = v[6 * half + 3:6 * half + 6]
    state = small[24:32]
    if not final:
        state = (state + before[136:144]) + (after[136:144] + across[24:32])
    for ref, start in ((upper, 208), (lower, 208), (ahead, 24), (behind, 24)):
        ref[pl.ds(start, 8)] = state


def near_sweep(body, upper, lower, weight0, weight1, x0, x1, r, sides):
    here, there = units(body, 0, 32), unpack_rows(upper, lower, 0, sides)
    for i in range(SLABS):
        v = assemble_fine(here, there, i, near_sources)
        r[i] = v
        x0[i] = weight0[i] * v
    for m in range(MIDS):
        i = 2 * m + 1
        two = x0[i] + x0[i + 1]
        left = KEEP * (r[i] + r[i + 1]) + ((x0[i - 1] + x0[i + 2]) + two) + around(two, 1, 1)
        x1[m] = weight1[m] * pair_mean(left, 1)


def unfold(v, k, out, change):
    turn = iota((16, 256), 1) % 4
    moved = {d: roll(v, d, 1) for d in range(-3, 4)}
    for c in range(4):
        slab = moved[-c]
        for j in range(1, 4):
            slab = jnp.where(turn == j, moved[j - c], slab)
        out[4 * k + c + 1] = change(4 * k + c + 1, slab)


def assemble_shares(own, up1, down1, up2, down2, out, change):
    def zeros(n):
        return jnp.zeros((n, 128), F32)

    for k in range(4):
        halves = []
        for half in range(2):
            s, t = 160 + 12 * k + 6 * half, 6 * k + 3 * half
            v = jnp.concatenate([own[s + 1:s + 6], zeros(10), own[s:s + 1]], axis=0)
            v = v + jnp.concatenate([zeros(3), up1[s:s + 6], zeros(7)], axis=0)
            v = v + jnp.concatenate([zeros(7), up2[t:t + 3], zeros(6)], axis=0)
            v = v + jnp.concatenate([down1[s + 5:s + 6], zeros(10), down1[s:s + 5]], axis=0)
            v = v + jnp.concatenate([zeros(10), down2[t:t + 3], zeros(3)], axis=0)
            halves.append(v)
        unfold(jnp.concatenate(halves, axis=1), k, out, change)


def assemble_coarse(gather, t, out, change):
    gy, ny = place()[1], sizes()[1]
    for k in range(4):
        own, up1, up2, down2, down1 = [ny * k + lax.rem(gy + d + ny, ny) for d in (0, 1, 2, -2, -1)]
        v = jnp.concatenate(
            [
                jnp.concatenate([
                    gather[own, t, s:s + 4], gather[up1, t, s:s + 4], gather[up2, t, s:s + 2],
                    gather[down2, t, s + 2:s + 4], gather[down1, t, s:s + 4],
                ], axis=0)
                for s in (0, 4)
            ],
            axis=1,
        )
        unfold(v, k, out, change)


def up_sweep(assemble, weight2, weight1, weight0, x0, x1, kap, u, w, a, b, rhs2, spread, middle, t1, t0):
    zero = jnp.zeros((16, 256), F32)
    for ref in (a, b):
        ref[0] = zero
        ref[17] = zero
    assemble(rhs2, lambda s, v: weight2[s] * v)
    for s in range(1, 17):
        a[s] = rhs2[s]
    for sweep in range(COARSE_SWEEPS - 1):
        old, new = (a, b) if sweep % 2 == 0 else (b, a)

        for s in range(1, 17):
            v = old[s]
            beside = (old[s - 1] + old[s + 1]) + around(v, 1, 4)
            new[s] = (KEEP * v + rhs2[s]) + weight2[s] * (0.0625 * beside)
    last = b if COARSE_SWEEPS % 2 == 0 else a
    half = iota((8, 256), 0) < 4
    for c in range(6):
        v = last[4 * place()[0] + c]
        spread[c] = jnp.concatenate(
            [
                jnp.where(half, jnp.broadcast_to(v[j:j + 1], (8, 256)), jnp.broadcast_to(v[j + 1:j + 2], (8, 256)))
                for j in (0, 2, 4, 14)
            ],
            axis=0,
        )
    for m in range(MIDS):
        t1[m] = x1[m] + spread[m // 2]
    for m in range(1, MIDS - 1):
        v = t1[m]
        beside = (t1[m - 1] + t1[m + 1]) + around(v, 2, 2)
        middle[m] = (KEEP * v + x1[m]) + weight1[m] * (0.25 * beside)
    for i in range(3, SLABS - 3):
        t0[i] = x0[i] + middle[(i - 1) // 2]
    for i in range(4, SLABS - 4):
        v = t0[i]
        beside = (t0[i - 1] + t0[i + 1]) + around(v, 1, 1)
        u[i] = (KEEP * v + x0[i]) + weight0[i] * beside
    for i in range(5, SLABS - 5):
        v = u[i]
        beside = (u[i - 1] + u[i + 1]) + around(v, 1, 1)
        w[i - 5] = (kap[i - 5] + 6.0) * v[:16, :128] - beside[:16, :128]


def lanes_of(values):
    lane = iota((8, 128), 1)
    out = jnp.zeros((8, 128), F32)
    for k, v in enumerate(values):
        out = jnp.where(lane == MARK + k, jnp.sum(v), out)
    return out


def first_up_kernel(gather, weight1, weight0, x0, x1, both, weight2, u, w, share, low, high, dots, *scratch):
    (*scratch, full, y0, y1, z1, quads) = scratch
    row, lane = iota((16, 256), 0), iota((16, 256), 1)
    y = jnp.where(row < 10, row, row - 16) + 4 * place()[1]
    inside = inside_lanes(lane) & (y >= 0) & (y < 4 * sizes()[1])
    assemble_coarse(gather, 1, weight2, lambda s, v: jnp.where(inside, v, 0.0))
    up_sweep(lambda *a: assemble_coarse(gather, 0, *a), weight2, weight1, weight0, x0, x1, both.at[1], full, w, *scratch)
    rz = curve = jnp.zeros((16, 128), F32)
    for k in range(16):
        v = full[k + 5][:16, :128]
        u[k] = v
        rz = rz + both[0, k] * v
        curve = curve + w[k] * v
    dots[...] = lanes_of([rz, curve])
    pack_near(lambda k: w[k], low, high)
    share_sweep(w, weight0, weight1, share, y0, y1, z1, quads)


def whole_sweep(body, shares, weight2, weight1, weight0, kap, full, w, x0, x1, r, sides, *scratch):
    near_sweep(body, shares[1], shares[2], weight0, weight1, x0, x1, r, sides)
    up_sweep(lambda *a: assemble_shares(*shares, *a), weight2, weight1, weight0, x0, x1, kap, full, w, *scratch)


def second_kernel(body, own, up1, down1, up2, down2, weight2, weight1, weight0, both, m0, n0, share, low, high, *scratch):
    (full, *scratch, y0, y1, z1, quads) = scratch
    shares = (own, up1, down1, up2, down2)
    whole_sweep(body, shares, weight2, weight1, weight0, both.at[1], full, n0, *scratch)
    for k in range(16):
        m0[k] = full[k + 5, :16, :128]
    pack_near(lambda k: n0[k], low, high)
    share_sweep(n0, weight0, weight1, share, y0, y1, z1, quads)


def third_kernel(body, own, up1, down1, up2, down2, weight2, weight1, weight0, both, u0, w0, m0, n0,
                 r1, u1, w1, m1, n1, first, dots, full, last, *scratch):
    shares = (own, up1, down1, up2, down2)
    whole_sweep(body, shares, weight2, weight1, weight0, both.at[1], full, last, *scratch)
    total0 = own[208:209] + up2[25:26] + down2[26:27]
    first[...] = jnp.broadcast_to(total0, (8, 128))
    alpha = total0[:, MARK:MARK + 1] / total0[:, MARK + 1:MARK + 2]
    sums = [jnp.zeros((16, 128), F32)] * 12
    for k in range(16):
        vw0, vm0, vn0 = w0[k], m0[k], n0[k]
        vr1 = both[0, k] - alpha * vw0
        vu1 = u0[k] - alpha * vm0
        vw1 = vw0 - alpha * vn0
        vm1 = vm0 - alpha * full[k + 5, :16, :128]
        vn1 = vn0 - alpha * last[k]
        r1[k], u1[k], w1[k], m1[k], n1[k] = vr1, vu1, vw1, vm1, vn1
        terms = [vr1 * vu1, vr1 * vm1, vr1 * vm0, vw1 * vu1, vw1 * vm1, vw1 * vm0,
                 vw0 * vu1, vw0 * vm1, vw0 * vm0, vn1 * vm1, vn1 * vm0, vn0 * vm0]
        sums = [s + t for s, t in zip(sums, terms)]
    dots[...] = lanes_of(sums)


def finish_kernel(first, second, u0, w0, m0, n0, r1, u1, w1, m1, n1, field, residual):
    g0, d0 = first[0:1, MARK:MARK + 1], first[0:1, MARK + 1:MARK + 2]
    (r1u1, r1m1, r1m0, w1u1, w1m1, w1m0, w0u1, w0m1, w0m0, n1m1, n1m0, n0m0) = [
        second[0:1, MARK + k:MARK + k + 1] for k in range(12)
    ]
    alpha0 = g0 / d0
    beta1 = r1u1 / g0
    curve1 = w1u1 + 2.0 * beta1 * w0u1 + beta1 * beta1 * d0
    alpha1 = r1u1 / curve1
    ab = alpha1 * beta1
    su = w1u1 + beta1 * w0u1 - alpha1 * (w1m1 + beta1 * w0m1) - ab * (w1m0 + beta1 * w0m0)
    g2 = (r1u1 - alpha1 * r1m1 - ab * r1m0) - alpha1 * su
    beta2 = g2 / r1u1
    uw = (w1u1 - 2.0 * alpha1 * w1m1 - 2.0 * ab * w1m0) + (alpha1 * alpha1 * n1m1 + 2.0 * alpha1 * ab * n1m0 + ab * ab * n0m0)
    curve2 = uw + 2.0 * beta2 * su + beta2 * beta2 * curve1
    alpha2 = g2 / curve2
    mix = alpha1 + alpha2 * beta2
    cu0, cu1, cm1, cm0 = alpha0 + mix * beta1, mix + alpha2, alpha2 * alpha1, alpha2 * ab
    cw0 = mix * beta1
    for k in range(16):
        field[k] = (cu0 * u0[k] + cu1 * u1[k]) - (cm1 * m1[k] + cm0 * m0[k])
        residual[k] = r1[k] - (cw0 * w0[k] + cu1 * w1[k]) + (cm1 * n1[k] + cm0 * n0[k])


def shape(*dims):
    return jax.ShapeDtypeStruct(dims, F32)


def call(kernel, outs, scratch=(), specs=None, count=0, grant=40):
    return pl.pallas_call(
        kernel,
        out_shape=outs,
        in_specs=specs or [VMEM] * count,
        out_specs=[VMEM] * len(outs),
        scratch_shapes=list(scratch),
        compiler_params=pltpu.CompilerParams(vmem_limit_bytes=grant * 1024 * 1024),
    )


def shift(v, axis, distance):
    count = lax.axis_size(axis)
    return lax.ppermute(v, axis, [((i + distance) % count, i) for i in range(count)])


def fine_exchange(own, low, high):
    above, below = shift(low, "gz", 1), shift(high, "gz", -1)
    first = jnp.concatenate([own[:, :5], above[:, 4:5], below[:, 4:5]], axis=1)
    last = jnp.concatenate([own[:, 11:], above[:, 5:6], below[:, 5:6]], axis=1)
    before, after = shift(last, "gx", -1), shift(first, "gx", 1)
    body = jnp.concatenate([own, above[:, :4], below[:, :4], before, after, own[:, :2]], axis=1).reshape(-1, 128)
    upper, lower = call(pack_rows_kernel, [shape(10 * UNITS, 128)] * 2, count=1)(body)
    return body, shift(upper, "gy", 1), shift(lower, "gy", -1)


def joint_exchange(own, share, low, high, state, final):
    above = shift(jnp.concatenate([low, share, state]), "gz", 1)
    below = shift(jnp.concatenate([high, share, state]), "gz", -1)
    first, last, small = call(
        functools.partial(join_z_kernel, final), [shape(144, 128), shape(144, 128), shape(32, 128)], count=5
    )(own, share, state, above, below)
    before, after, across = shift(last, "gx", -1), shift(first, "gx", 1), shift(small, "gx", 2)
    body, upper, lower, ahead, behind = call(
        functools.partial(join_x_kernel, final), [shape(512, 128), shape(216, 128), shape(216, 128), shape(32, 128), shape(32, 128)],
        [pltpu.VMEM((4, 24, 128), F32)], count=7,
    )(own, above, below, small, before, after, across)
    return body, upper, shift(upper, "gy", 1), shift(lower, "gy", -1), shift(ahead, "gy", 2), shift(behind, "gy", -2)


def gather(unit):
    count = lax.axis_size("gx") * lax.axis_size("gy")
    return lax.all_to_all(jnp.broadcast_to(unit[None], (count,) + unit.shape), ("gx", "gy"), 0, 0, tiled=True)


def total(v):
    axes = ("gx", "gy", "gz")
    count = lax.axis_size("gx") * lax.axis_size("gy") * lax.axis_size("gz")
    parts = lax.all_to_all(jnp.broadcast_to(v[None, :1], (count, 1, 128)), axes, 0, 0, tiled=True)
    return jnp.broadcast_to(parts.sum(0), (8, 128))


def local(right_side, classes, table):
    def scratch(*shapes):
        return [pltpu.VMEM(s, F32) for s in shapes]

    block, halo, mids, tile = shape(*BLOCK), shape(*HALO), shape(*MID), shape(8, 128)
    down_scratch = scratch(HALO, MID, (2, 4, 16, 128), (16 * UNITS, 128))
    up_scratch = scratch((18, 16, 256), (18, 16, 256), (18, 16, 256), (6, 32, 256), MID, MID, HALO, HALO)

    both, low, high = call(
        prepare_kernel, [shape(2, *BLOCK), shape(2, 6, 16, 128), shape(2, 6, 16, 128)],
        [pltpu.VMEM(BLOCK, jnp.int32), pltpu.SMEM((CLASSES,), F32), pltpu.SemaphoreType.DMA((3,))], specs=[ANY] * 3, grant=60,
    )(right_side, classes, table)
    halos = fine_exchange(both, low, high)
    weight0, weight1, x0, x1, unit = call(
        first_down_kernel, [halo, mids, halo, mids, shape(2, 8, 128)], down_scratch + scratch((16 * UNITS, 128)), count=3
    )(*halos)
    share_outs = [shape(24, 128), shape(16, 128), shape(16, 128)]
    share_scratch = scratch(BLOCK, (10, 32, 256), (10, 32, 256), (2, 6, 32, 128))
    weight2, u0, w0, share, low, high, dots = call(
        first_up_kernel, [shape(18, 16, 256), block, block, *share_outs, tile], up_scratch + share_scratch, count=6
    )(gather(unit), weight1, weight0, x0, x1, both)

    whole_scratch = scratch(HALO, MID, HALO, (512, 128)) + up_scratch[:-1]
    halos = joint_exchange(w0, share, low, high, dots, False)
    _, own, up1, down1, up2, _ = halos
    ahead, behind = up1[208:210] + up2[24:26], down1[208:210] + own[208:210]
    state = jnp.concatenate([ahead + behind, ahead, behind, jnp.zeros((2, 128), F32)])
    state = state + shift(state, "gz", 4)
    m0, n0, share, low, high = call(
        second_kernel, [block, block, *share_outs], scratch(HALO) + whole_scratch + share_scratch, count=10
    )(*halos, weight2, weight1, weight0, both)
    halos = joint_exchange(n0, share, low, high, state, True)
    r1, u1, w1, m1, n1, first, dots = call(
        third_kernel, [block] * 5 + [tile, tile], scratch(HALO, BLOCK) + whole_scratch, count=14
    )(*halos, weight2, weight1, weight0, both, u0, w0, m0, n0)
    field, residual = call(finish_kernel, [block] * 2, count=11)(
        first, total(dots), u0, w0, m0, n0, r1, u1, w1, m1, n1
    )
    return field, residual


def solution(mesh):
    in_specs = (P("gx", "gy", "gz"), P("gx", "gy", "gz"), P())
    out_specs = (P("gx", "gy", "gz"), P("gx", "gy", "gz"))
    return jax.shard_map(local, mesh=mesh, in_specs=in_specs, out_specs=out_specs, check_vma=False)
```

```python
import functools

import jax
import jax.numpy as jnp
from jax import lax
from jax.experimental import pallas as pl
from jax.experimental.pallas import tpu as pltpu
from jax.sharding import PartitionSpec as P

CLASSES = 16
COARSE_SWEEPS = 6
OMEGA = 0.8
KEEP = 1.0 - OMEGA
F32 = jnp.float32
SLABS, MIDS, UNITS = 26, 12, 40
MARK = 64
BLOCK, HALO, SHORT, MID = (16, 16, 128), (SLABS, 32, 256), (SLABS, 24, 256), (MIDS, 24, 256)
VMEM = pl.BlockSpec(memory_space=pltpu.VMEM)
ANY = pl.BlockSpec(memory_space=pl.ANY)


def iota(shape, dim):
    return lax.broadcasted_iota(jnp.int32, shape, dim)


def roll(v, shift, axis):
    shift = shift % v.shape[axis]
    return v if shift == 0 else pltpu.roll(v, shift, axis)


def around(v, rows, lanes):
    return (roll(v, rows, 0) + roll(v, -rows, 0)) + (roll(v, lanes, 1) + roll(v, -lanes, 1))


def pair_mean(v, step):
    rows = (iota(v.shape, 0) // step) % 2 == 0
    v = v + jnp.where(rows, roll(v, -step, 0), roll(v, step, 0))
    lanes = (iota(v.shape, 1) // step) % 2 == 0
    v = v + jnp.where(lanes, roll(v, -step, 1), roll(v, step, 1))
    return v * 0.125


def place():
    return tuple(lax.axis_index(axis) for axis in ("gx", "gy", "gz"))


def sizes():
    return tuple(lax.axis_size(axis) for axis in ("gx", "gy", "gz"))


def pack_fine(read, low_ref, high_ref):
    lane = iota((16, 128), 1)
    chunk = lane // 32
    for g in range(4):
        low = high = None
        for j in range(4):
            v = read(4 * g + j)
            first, last = roll(v, 32 * j, 1), roll(v, 32 * j + 32, 1)
            low = first if j == 0 else jnp.where(chunk == j, first, low)
            high = last if j == 0 else jnp.where(chunk == j, last, high)
        low_ref[g] = low
        high_ref[g] = high
    for g, slabs in ((4, (0, 1, 2, 3, 4)), (5, (15, 14, 13, 12, 11))):
        low, high = read(slabs[0]), roll(read(slabs[0]), 32, 1)
        for j in range(1, 5):
            v, here = read(slabs[j]), (lane >= 112 if j == 4 else chunk == j)
            low = jnp.where(here, roll(v, 112 if j == 4 else 32 * j, 1), low)
            high = jnp.where(here, roll(v, (32, 64, 96, 112, 0)[j], 1), high)
        low_ref[g] = low
        high_ref[g] = high


def pack_near(read, low_ref, high_ref):
    chunk = iota((16, 128), 1) // 8
    low = high = None
    for k in range(16):
        v = read(k)
        first, last = roll(v, 8 * k, 1), roll(v, 8 * k + 8, 1)
        low = first if k == 0 else jnp.where(chunk == k, first, low)
        high = last if k == 0 else jnp.where(chunk == k, last, high)
    low_ref[...] = low
    high_ref[...] = high


def prepare_kernel(rhs_in, classes_in, table_in, both, low, high, classes, table, sems):
    copies = [
        pltpu.make_async_copy(rhs_in, both.at[0], sems.at[0]),
        pltpu.make_async_copy(classes_in, classes, sems.at[1]),
        pltpu.make_async_copy(table_in, table, sems.at[2]),
    ]
    for copy in copies:
        copy.start()
    for copy in copies:
        copy.wait()
    for k in range(16):
        c = classes[k]
        v = jnp.zeros((16, 128), F32)
        for index in range(CLASSES):
            v = jnp.where(c == index, table[index], v)
        both[1, k] = v
    for t in range(2):
        pack_fine(lambda k, t=t: both[t, k], low.at[t], high.at[t])


def slab_sources(i):
    x = i - 5
    if 0 <= x < 16:
        return x, 16 + x // 4, 20 + x // 4, -32 * (x % 4), 96 - 32 * (x % 4)
    base, far = (24, -1 - x) if x < 0 else (31, x - 16)
    return base + (x + 5 if x < 0 else far), base + 5, base + 6, (0, -32, -64, -96, -112)[far], (96, 64, 32, 16, 0)[far]


def near_sources(i):
    x = i - 5
    base, above, k = (x, 16, x) if 0 <= x < 16 else ((23 + x, 23, 16 + x) if x < 0 else (x + 9, 30, x - 16))
    return base, above, above + 1, -8 * k, 120 - 8 * k


def assemble_fine(body, sides, i, sources=slab_sources):
    def unit(u):
        return jnp.concatenate([body[u][...], sides[u][...]], axis=0)

    main, above, below, up, down = sources(i)
    lane = iota((32, 128), 1)
    side = jnp.where(lane < 64, roll(unit(above), up, 1), roll(unit(below), down, 1))
    return jnp.concatenate([unit(main), side], axis=1)


def pack_rows_kernel(body, upper, lower):
    for g in range(body.shape[0] // 128):
        for t in range(5):
            here = pl.ds(8 * (5 * g + t), 8)
            upper[here] = body[pl.ds(128 * g + t, 8, stride=16), :]
            lower[here] = body[pl.ds(128 * g + 11 + t, 8, stride=16), :]


def units(body, first, count):
    return [body.at[pl.ds(first + 16 * u, 16)] for u in range(count)]


def unpack_rows(upper, lower, first, sides):
    sides[...] = jnp.zeros(sides.shape, F32)
    for g in range(sides.shape[0] // 128):
        for t in range(5):
            here = pl.ds(8 * (first + 5 * g + t), 8)
            sides[pl.ds(128 * g + t, 8, stride=16), :] = upper[here]
            sides[pl.ds(128 * g + 11 + t, 8, stride=16), :] = lower[here]
    return units(sides, 0, sides.shape[0] // 16)


def squeeze(v):
    return jnp.concatenate([v[:16], jnp.where(iota((8, v.shape[1]), 0) < 4, v[16:24], v[24:])], axis=0)


def near(lane):
    return (lane < 160) | (lane >= 224)


def inside_lanes(lane):
    z = jnp.where(lane < 192, lane, lane - 256) + 128 * place()[2]
    return near(lane) & (z >= 0) & (z < 128 * sizes()[2])


def inside_fine(rows):
    row, lane = iota((rows, 256), 0), iota((rows, 256), 1)
    y = jnp.where(row < rows // 2 + 8, row, row - rows) + 16 * place()[1]
    return inside_lanes(lane) & (y >= 0) & (y < 16 * sizes()[1])


def fine_weights(body, sides, weight0, weight0s, weight1, middle, quads, unit):
    gx, nx = place()[0], sizes()[0]
    inside, insides = inside_fine(32), inside_fine(24)

    def weigh(i):
        kap = assemble_fine(body, sides, i)
        x = 16 * gx + (i - 5)
        v = jnp.where(inside & (x >= 0) & (x < 16 * nx), OMEGA / (kap + 6.0), 0.0)
        weight0[i] = v
        weight0s[i] = squeeze(v)
        return squeeze(kap)

    weigh(0)
    weigh(SLABS - 1)
    for m in range(MIDS):
        kap1 = pair_mean(weigh(2 * m + 1) + weigh(2 * m + 2), 1)
        middle[m] = kap1
        x = 8 * gx + (m - 2)
        weight1[m] = jnp.where(insides & (x >= 0) & (x < 8 * nx), OMEGA / (kap1 + 1.5), 0.0)
    for c in range(4):
        kap2 = pair_mean(middle[2 + 2 * c] + middle[3 + 2 * c], 2)[:16]
        weight2 = OMEGA / (kap2 + 0.375)
        quads[0, c], quads[1, c] = weight2[:, :128], weight2[:, 128:]
    pack_coarse(quads, unit)


def pack_coarse(quads, unit):
    turn = iota((4, 128), 1) % 4
    for half in range(2):
        v = quads[half, 0, pl.ds(0, 4, stride=4), :]
        for c in range(1, 4):
            v = jnp.where(turn == c, quads[half, c, pl.ds(0, 4, stride=4), :], v)
        unit[4 * half:4 * half + 4] = v


def near_sweep(read, weight0, weight1, x0, x1, r1, r, tall):
    for i in range(SLABS):
        v = read(i)
        r[i] = squeeze(v)
        v = weight0[i] * v
        tall[i] = v
        x0[i] = squeeze(v)
    for m in range(MIDS):
        i = 2 * m + 1
        two = tall[i] + tall[i + 1]
        rows = squeeze(roll(two, 1, 0) + roll(two, -1, 0))
        two = x0[i] + x0[i + 1]
        lanes = roll(two, 1, 1) + roll(two, -1, 1)
        v = pair_mean(KEEP * (r[i] + r[i + 1]) + ((x0[i - 1] + x0[i + 2]) + two) + (rows + lanes), 1)
        if r1 is not None:
            r1[m] = v
        x1[m] = weight1[m] * v


def first_down_kernel(body, upper, lower, weight0, weight0s, weight1, x0, x1, unit, r, tall, r1, quads, sides):
    there = unpack_rows(upper, lower, 5 * UNITS // 8, sides)
    fine_weights(units(body, 16 * UNITS, UNITS), there, weight0, weight0s, weight1, r1, quads, unit.at[1])
    here, there = units(body, 0, UNITS), unpack_rows(upper, lower, 0, sides)
    near_sweep(lambda i: assemble_fine(here, there, i), weight0, weight1, x0, x1, r1, r, tall)
    for c in range(4):
        m = 2 + 2 * c
        two = x1[m] + x1[m + 1]
        left = KEEP * (r1[m] + r1[m + 1]) + 0.25 * (((x1[m - 1] + x1[m + 2]) + two) + around(two, 2, 2))
        v = pair_mean(left, 2)[:16]
        quads[0, c], quads[1, c] = v[:, :128], v[:, 128:]
    pack_coarse(quads, unit.at[0])


def share_sweep(block, weight0, weight1, share, x0, r1, x1, quads):
    for k in range(16):
        x0[k] = weight0[k + 5, :16, :128] * block[k]
    zero, low = jnp.zeros((16, 128), F32), jnp.zeros((8, 256), F32)

    def tall(v):
        return jnp.concatenate([jnp.concatenate([v, zero], axis=1), low], axis=0)

    for m in range(10):
        x = 2 * (m - 1)
        if m == 0:
            left = tall(x0[0])
        elif m == 9:
            left = tall(x0[15])
        else:
            two = x0[x] + x0[x + 1]
            flat = KEEP * (block[x] + block[x + 1]) + two
            flat = flat + x0[x - 1] if x > 0 else flat
            flat = flat + x0[x + 2] if x < 14 else flat
            left = tall(flat) + around(tall(two), 1, 1)
        v = pair_mean(left, 1)
        r1[m] = v
        x1[m] = weight1[m + 1] * v
    for c in range(6):
        pair = [m for m in (2 * c - 1, 2 * c) if 0 <= m < 10]
        two = sum(x1[m] for m in pair)
        left = KEEP * sum(r1[m] for m in pair)
        beside = two + around(two, 2, 2)
        for m in (2 * c - 2, 2 * c + 1):
            beside = beside + x1[m] if 0 <= m < 10 else beside
        v = pair_mean(left + 0.25 * beside, 2)
        quads[0, c], quads[1, c] = v[:, :128], v[:, 128:]
    gy, gz = place()[1:]
    ny, nz = sizes()[1:]
    for half in range(2):
        for start, count, first in ((20, 1, 0), (0, 5, 1)):
            row, lane = iota((count, 128), 0), iota((count, 128), 1)
            y = row // 4 + gy - (1 if count == 1 else 0)
            inside = (y >= 0) & (y < ny)
            if half == 1:
                z = jnp.where(lane < 64, gz + 1, gz - 1)
                inside = inside & (z >= 0) & (z < nz)

            def rows(c):
                v = quads[half, c, pl.ds(start, count, stride=4), :] if count > 1 else quads[half, c, pl.ds(start, 1), :]
                return jnp.where(inside, v, 0.0)

            turn = lane % 4
            v = rows(1)
            for c in range(1, 4):
                v = jnp.where(turn == c, rows(c + 1), v)
            share[pl.ds(6 * half + first, count)] = v
            v = jnp.where(turn == 3, rows(0), jnp.where(turn == 0, rows(5), 0.0))
            share[pl.ds(12 + 6 * half + first, count)] = v


def join_z_kernel(final, own, share, state, above, below, first, last, small):
    lane = iota((6, 128), 1)
    for s in (0, 12):
        main, side = pl.ds(16 + s, 6), pl.ds(22 + s, 6)
        v = share[s:s + 6] + jnp.where(lane >= 124, above[side], 0.0) + jnp.where(lane < 4, below[side], 0.0)
        small[pl.ds(s, 6)] = v
        v = share[s + 6:s + 12] + jnp.where(lane < 32, above[main], jnp.where(lane >= 96, below[main], 0.0))
        small[pl.ds(s + 6, 6)] = v
    row = iota((8, 128), 0)
    if final:
        sums = [state[j:j + 1] + state[j + 1:j + 2] + above[41 + j:42 + j] + below[40 + j:41 + j] for j in (0, 2, 4)]
    else:
        sums = [state[0:1], above[40:41]]
    v = jnp.zeros((8, 128), F32)
    for j, part in enumerate(sums):
        v = jnp.where(row == j, part, v)
    small[24:32] = v
    for k in range(5):
        first[pl.ds(16 * k, 16)] = own[k]
        last[pl.ds(16 * k, 16)] = own[11 + k]
    for ref in (first, last):
        ref[80:96] = above[:16]
        ref[96:112] = below[:16]
        ref[112:144] = small[...]


def join_x_kernel(final, own, above, below, small, before, after, across, body, upper, lower, ahead, behind, stage):
    for k in range(16):
        body[pl.ds(16 * k, 16)] = own[k]
    body[256:272] = above[:16]
    body[272:288] = below[:16]
    body[288:400] = before[:112]
    body[400:512] = after[:112]
    pack_rows_kernel(body, upper, lower)
    gx = place()[0]
    for k, rows in enumerate((small[:24], after[112:136], across[:24], before[112:136])):
        stage[lax.rem(gx + k, 4)] = rows
    turn = iota((12, 128), 1) % 4
    for b in range(4):
        v = stage[b, :12]
        if b < 3:
            v = v + jnp.where(turn == 3, stage[b + 1, 12:], 0.0)
        if b > 0:
            v = v + jnp.where(turn == 0, stage[b - 1, 12:], 0.0)
        for ref in (upper, lower):
            ref[pl.ds(160 + 12 * b, 12)] = v
        for half in range(2):
            ahead[pl.ds(6 * b + 3 * half, 3)] = v[6 * half:6 * half + 3]
            behind[pl.ds(6 * b + 3 * half, 3)] = v[6 * half + 3:6 * half + 6]
    state = small[24:32]
    if not final:
        state = (state + before[136:144]) + (after[136:144] + across[24:32])
    for ref, start in ((upper, 208), (lower, 208), (ahead, 24), (behind, 24)):
        ref[pl.ds(start, 8)] = state


def unfold(v, c):
    turn = iota(v.shape, 1) % 4
    slab = roll(v, -c, 1)
    for j in range(1, 4):
        slab = jnp.where(turn == j, roll(v, j - c, 1), slab)
    return slab


def assemble_shares(own, up1, down1, up2, down2, out, change):
    def zeros(n):
        return jnp.zeros((n, 128), F32)

    for k in range(4):
        halves = []
        for half in range(2):
            s, t = 160 + 12 * k + 6 * half, 6 * k + 3 * half
            v = jnp.concatenate([own[s + 1:s + 6], zeros(10), own[s:s + 1]], axis=0)
            v = v + jnp.concatenate([zeros(3), up1[s:s + 6], zeros(7)], axis=0)
            v = v + jnp.concatenate([zeros(7), up2[t:t + 3], zeros(6)], axis=0)
            v = v + jnp.concatenate([down1[s + 5:s + 6], zeros(10), down1[s:s + 5]], axis=0)
            v = v + jnp.concatenate([zeros(10), down2[t:t + 3], zeros(3)], axis=0)
            halves.append(v)
        out[k] = change(k, jnp.concatenate(halves, axis=1))


def assemble_coarse(gather, t, out, change):
    gy, ny = place()[1], sizes()[1]
    for k in range(4):
        own, up1, up2, down2, down1 = [ny * k + lax.rem(gy + d + ny, ny) for d in (0, 1, 2, -2, -1)]
        v = jnp.concatenate(
            [
                jnp.concatenate([
                    gather[own, t, s:s + 4], gather[up1, t, s:s + 4], gather[up2, t, s:s + 2],
                    gather[down2, t, s + 2:s + 4], gather[down1, t, s:s + 4],
                ], axis=0)
                for s in (0, 4)
            ],
            axis=1,
        )
        out[k] = change(k, v)


def up_sweep(assemble, weight2, weight1, weight0, x0, x1, kap, u, w, a, b, rhs2, spread, middle, t1, t0):
    zero = jnp.zeros((16, 256), F32)
    for ref in (a, b):
        ref[0] = zero
        ref[5] = zero
    assemble(rhs2, lambda g, v: weight2[g] * v)
    for g in range(4):
        a[g + 1] = rhs2[g]
    turn = iota((16, 256), 1) % 4
    for sweep in range(COARSE_SWEEPS - 1):
        old, new = (a, b) if sweep % 2 == 0 else (b, a)
        ahead = [None] + [roll(old[g], -4, 1) for g in range(1, 5)] + [None]
        back = [None] + [roll(old[g], 4, 1) for g in range(1, 5)] + [None]
        for g in range(1, 5):
            v = old[g]
            up = roll(jnp.where(turn == 3, zero if g == 1 else ahead[g - 1], v), 1, 1)
            down = roll(jnp.where(turn == 0, zero if g == 4 else back[g + 1], v), -1, 1)
            beside = (up + down) + (ahead[g] + back[g]) + (roll(v, 1, 0) + roll(v, -1, 0))
            new[g] = (KEEP * v + rhs2[g - 1]) + weight2[g - 1] * (0.0625 * beside)
    last = b if COARSE_SWEEPS % 2 == 0 else a
    gx = place()[0]
    half = iota((8, 256), 0) < 4
    for c in range(6):
        g, t = (gx, 3) if c == 0 else ((gx + 2, 0) if c == 5 else (gx + 1, c - 1))
        v = unfold(last[g], t)
        spread[c] = jnp.concatenate(
            [
                jnp.where(half, jnp.broadcast_to(v[j:j + 1], (8, 256)), jnp.broadcast_to(v[k:k + 1], (8, 256)))
                for j, k in ((0, 1), (2, 3), (4, 15))
            ],
            axis=0,
        )
    for m in range(MIDS):
        t1[m] = x1[m] + spread[m // 2]
    for m in range(1, MIDS - 1):
        v = t1[m]
        beside = (t1[m - 1] + t1[m + 1]) + around(v, 2, 2)
        middle[m] = (KEEP * v + x1[m]) + weight1[m] * (0.25 * beside)
    for i in range(3, SLABS - 3):
        t0[i] = x0[i] + middle[(i - 1) // 2]
    for i in range(4, SLABS - 4):
        v = t0[i]
        beside = (t0[i - 1] + t0[i + 1]) + around(v, 1, 1)
        u[i] = (KEEP * v + x0[i]) + weight0[i] * beside
    for i in range(5, SLABS - 5):
        v = u[i]
        beside = (u[i - 1] + u[i + 1]) + around(v, 1, 1)
        w[i - 5] = (kap[i - 5] + 6.0) * v[:16, :128] - beside[:16, :128]


def lanes_of(values):
    lane = iota((8, 128), 1)
    out = jnp.zeros((8, 128), F32)
    for k, v in enumerate(values):
        out = jnp.where(lane == MARK + k, jnp.sum(v), out)
    return out


def first_up_kernel(gather, weight1, weight0, x0, x1, both, weight2, u, w, share, low, high, dots, *scratch):
    (*scratch, full, y0, y1, z1, quads) = scratch
    row, lane = iota((16, 256), 0), iota((16, 256), 1)
    y = jnp.where(row < 10, row, row - 16) + 4 * place()[1]
    inside = inside_lanes(lane) & (y >= 0) & (y < 4 * sizes()[1])
    assemble_coarse(gather, 1, weight2, lambda s, v: jnp.where(inside, v, 0.0))
    up_sweep(lambda *a: assemble_coarse(gather, 0, *a), weight2, weight1, weight0, x0, x1, both.at[1], full, w, *scratch)
    rz = curve = jnp.zeros((16, 128), F32)
    for k in range(16):
        v = full[k + 5][:16, :128]
        u[k] = v
        rz = rz + both[0, k] * v
        curve = curve + w[k] * v
    dots[...] = lanes_of([rz, curve])
    pack_near(lambda k: w[k], low, high)
    share_sweep(w, weight0, weight1, share, y0, y1, z1, quads)


def whole_sweep(body, shares, weight2, weight1, weight0, weight0s, kap, full, w, x0, x1, r, tall, sides, *scratch):
    here, there = units(body, 0, 32), unpack_rows(shares[1], shares[2], 0, sides)
    near_sweep(lambda i: assemble_fine(here, there, i, near_sources), weight0, weight1, x0, x1, None, r, tall)
    up_sweep(lambda *a: assemble_shares(*shares, *a), weight2, weight1, weight0s, x0, x1, kap, full, w, *scratch)


def second_kernel(body, own, up1, down1, up2, down2, weight2, weight1, weight0, weight0s, both, m0, n0, share, low, high, *scratch):
    (full, *scratch, y0, y1, z1, quads) = scratch
    shares = (own, up1, down1, up2, down2)
    whole_sweep(body, shares, weight2, weight1, weight0, weight0s, both.at[1], full, n0, *scratch)
    for k in range(16):
        m0[k] = full[k + 5, :16, :128]
    pack_near(lambda k: n0[k], low, high)
    share_sweep(n0, weight0, weight1, share, y0, y1, z1, quads)


def third_kernel(body, own, up1, down1, up2, down2, weight2, weight1, weight0, weight0s, both, u0, w0, m0, n0,
                 r1, u1, w1, m1, n1, first, dots, full, last, *scratch):
    shares = (own, up1, down1, up2, down2)
    whole_sweep(body, shares, weight2, weight1, weight0, weight0s, both.at[1], full, last, *scratch)
    total0 = own[208:209] + up2[25:26] + down2[26:27]
    first[...] = jnp.broadcast_to(total0, (8, 128))
    alpha = total0[:, MARK:MARK + 1] / total0[:, MARK + 1:MARK + 2]
    sums = [jnp.zeros((16, 128), F32)] * 12
    for k in range(16):
        vw0, vm0, vn0 = w0[k], m0[k], n0[k]
        vr1 = both[0, k] - alpha * vw0
        vu1 = u0[k] - alpha * vm0
        vw1 = vw0 - alpha * vn0
        vm1 = vm0 - alpha * full[k + 5, :16, :128]
        vn1 = vn0 - alpha * last[k]
        r1[k], u1[k], w1[k], m1[k], n1[k] = vr1, vu1, vw1, vm1, vn1
        terms = [vr1 * vu1, vr1 * vm1, vr1 * vm0, vw1 * vu1, vw1 * vm1, vw1 * vm0,
                 vw0 * vu1, vw0 * vm1, vw0 * vm0, vn1 * vm1, vn1 * vm0, vn0 * vm0]
        sums = [s + t for s, t in zip(sums, terms)]
    dots[...] = lanes_of(sums)


def finish_kernel(first, second, u0, w0, m0, n0, r1, u1, w1, m1, n1, field, residual):
    g0, d0 = first[0:1, MARK:MARK + 1], first[0:1, MARK + 1:MARK + 2]
    (r1u1, r1m1, r1m0, w1u1, w1m1, w1m0, w0u1, w0m1, w0m0, n1m1, n1m0, n0m0) = [
        second[0:1, MARK + k:MARK + k + 1] for k in range(12)
    ]
    alpha0 = g0 / d0
    beta1 = r1u1 / g0
    curve1 = w1u1 + 2.0 * beta1 * w0u1 + beta1 * beta1 * d0
    alpha1 = r1u1 / curve1
    ab = alpha1 * beta1
    su = w1u1 + beta1 * w0u1 - alpha1 * (w1m1 + beta1 * w0m1) - ab * (w1m0 + beta1 * w0m0)
    g2 = (r1u1 - alpha1 * r1m1 - ab * r1m0) - alpha1 * su
    beta2 = g2 / r1u1
    uw = (w1u1 - 2.0 * alpha1 * w1m1 - 2.0 * ab * w1m0) + (alpha1 * alpha1 * n1m1 + 2.0 * alpha1 * ab * n1m0 + ab * ab * n0m0)
    curve2 = uw + 2.0 * beta2 * su + beta2 * beta2 * curve1
    alpha2 = g2 / curve2
    mix = alpha1 + alpha2 * beta2
    cu0, cu1, cm1, cm0 = alpha0 + mix * beta1, mix + alpha2, alpha2 * alpha1, alpha2 * ab
    cw0 = mix * beta1
    for k in range(16):
        field[k] = (cu0 * u0[k] + cu1 * u1[k]) - (cm1 * m1[k] + cm0 * m0[k])
        residual[k] = r1[k] - (cw0 * w0[k] + cu1 * w1[k]) + (cm1 * n1[k] + cm0 * n0[k])


def shape(*dims):
    return jax.ShapeDtypeStruct(dims, F32)


def call(kernel, outs, scratch=(), specs=None, count=0, grant=40):
    return pl.pallas_call(
        kernel,
        out_shape=outs,
        in_specs=specs or [VMEM] * count,
        out_specs=[VMEM] * len(outs),
        scratch_shapes=list(scratch),
        compiler_params=pltpu.CompilerParams(vmem_limit_bytes=grant * 1024 * 1024),
    )


def shift(v, axis, distance):
    count = lax.axis_size(axis)
    return lax.ppermute(v, axis, [((i + distance) % count, i) for i in range(count)])


def fine_exchange(own, low, high):
    above, below = shift(low, "gz", 1), shift(high, "gz", -1)
    first = jnp.concatenate([own[:, :5], above[:, 4:5], below[:, 4:5]], axis=1)
    last = jnp.concatenate([own[:, 11:], above[:, 5:6], below[:, 5:6]], axis=1)
    before, after = shift(last, "gx", -1), shift(first, "gx", 1)
    body = jnp.concatenate([own, above[:, :4], below[:, :4], before, after, own[:, :2]], axis=1).reshape(-1, 128)
    upper, lower = call(pack_rows_kernel, [shape(10 * UNITS, 128)] * 2, count=1)(body)
    return body, shift(upper, "gy", 1), shift(lower, "gy", -1)


def joint_exchange(own, share, low, high, state, final):
    above = shift(jnp.concatenate([low, share, state]), "gz", 1)
    below = shift(jnp.concatenate([high, share, state]), "gz", -1)
    first, last, small = call(
        functools.partial(join_z_kernel, final), [shape(144, 128), shape(144, 128), shape(32, 128)], count=5
    )(own, share, state, above, below)
    before, after, across = shift(last, "gx", -1), shift(first, "gx", 1), shift(small, "gx", 2)
    body, upper, lower, ahead, behind = call(
        functools.partial(join_x_kernel, final), [shape(512, 128), shape(216, 128), shape(216, 128), shape(32, 128), shape(32, 128)],
        [pltpu.VMEM((4, 24, 128), F32)], count=7,
    )(own, above, below, small, before, after, across)
    return body, upper, shift(upper, "gy", 1), shift(lower, "gy", -1), shift(ahead, "gy", 2), shift(behind, "gy", -2)


def gather(unit):
    count = lax.axis_size("gx") * lax.axis_size("gy")
    return lax.all_to_all(jnp.broadcast_to(unit[None], (count,) + unit.shape), ("gx", "gy"), 0, 0, tiled=True)


def total(v):
    axes = ("gx", "gy", "gz")
    count = lax.axis_size("gx") * lax.axis_size("gy") * lax.axis_size("gz")
    parts = lax.all_to_all(jnp.broadcast_to(v[None, :1], (count, 1, 128)), axes, 0, 0, tiled=True)
    return jnp.broadcast_to(parts.sum(0), (8, 128))


def local(right_side, classes, table):
    def scratch(*shapes):
        return [pltpu.VMEM(s, F32) for s in shapes]

    block, short, mids, tile = shape(*BLOCK), shape(*SHORT), shape(*MID), shape(8, 128)
    up_scratch = scratch((6, 16, 256), (6, 16, 256), (4, 16, 256), (6, 24, 256), MID, MID, SHORT, SHORT)

    both, low, high = call(
        prepare_kernel, [shape(2, *BLOCK), shape(2, 6, 16, 128), shape(2, 6, 16, 128)],
        [pltpu.VMEM(BLOCK, jnp.int32), pltpu.SMEM((CLASSES,), F32), pltpu.SemaphoreType.DMA((3,))], specs=[ANY] * 3, grant=60,
    )(right_side, classes, table)
    halos = fine_exchange(both, low, high)
    weight0, weight0s, weight1, x0, x1, unit = call(
        first_down_kernel, [shape(*HALO), short, mids, short, mids, shape(2, 8, 128)],
        scratch(SHORT, HALO, MID, (2, 4, 16, 128), (16 * UNITS, 128)), count=3,
    )(*halos)
    share_outs = [shape(24, 128), shape(16, 128), shape(16, 128)]
    share_scratch = scratch(BLOCK, (10, 24, 256), (10, 24, 256), (2, 6, 24, 128))
    weight2, u0, w0, share, low, high, dots = call(
        first_up_kernel, [shape(4, 16, 256), block, block, *share_outs, tile], up_scratch + share_scratch, count=6
    )(gather(unit), weight1, weight0s, x0, x1, both)

    whole_scratch = scratch(SHORT, MID, SHORT, HALO, (512, 128)) + up_scratch[:-1]
    halos = joint_exchange(w0, share, low, high, dots, False)
    _, own, up1, down1, up2, _ = halos
    ahead, behind = up1[208:210] + up2[24:26], down1[208:210] + own[208:210]
    state = jnp.concatenate([ahead + behind, ahead, behind, jnp.zeros((2, 128), F32)])
    state = state + shift(state, "gz", 4)
    m0, n0, share, low, high = call(
        second_kernel, [block, block, *share_outs], scratch(SHORT) + whole_scratch + share_scratch, count=11
    )(*halos, weight2, weight1, weight0, weight0s, both)
    halos = joint_exchange(n0, share, low, high, state, True)
    r1, u1, w1, m1, n1, first, dots = call(
        third_kernel, [block] * 5 + [tile, tile], scratch(SHORT, BLOCK) + whole_scratch, count=15
    )(*halos, weight2, weight1, weight0, weight0s, both, u0, w0, m0, n0)
    field, residual = call(finish_kernel, [block] * 2, count=11)(
        first, total(dots), u0, w0, m0, n0, r1, u1, w1, m1, n1
    )
    return field, residual


def solution(mesh):
    in_specs = (P("gx", "gy", "gz"), P("gx", "gy", "gz"), P())
    out_specs = (P("gx", "gy", "gz"), P("gx", "gy", "gz"))
    return jax.shard_map(local, mesh=mesh, in_specs=in_specs, out_specs=out_specs, check_vma=False)
```

```python
import functools

import jax
import jax.numpy as jnp
from jax import lax
from jax.experimental import pallas as pl
from jax.experimental.pallas import tpu as pltpu
from jax.sharding import PartitionSpec as P

CLASSES = 16
COARSE_SWEEPS = 6
OMEGA = 0.8
KEEP = 1.0 - OMEGA
F32 = jnp.float32
SLABS, MIDS, UNITS = 26, 12, 40
MARK = 64
BLOCK, HALO, SHORT, MID = (16, 16, 128), (SLABS, 32, 256), (SLABS, 24, 256), (MIDS, 24, 256)
VMEM = pl.BlockSpec(memory_space=pltpu.VMEM)
ANY = pl.BlockSpec(memory_space=pl.ANY)


def iota(shape, dim):
    return lax.broadcasted_iota(jnp.int32, shape, dim)


def roll(v, shift, axis):
    shift = shift % v.shape[axis]
    return v if shift == 0 else pltpu.roll(v, shift, axis)


def around(v, rows, lanes):
    return (roll(v, rows, 0) + roll(v, -rows, 0)) + (roll(v, lanes, 1) + roll(v, -lanes, 1))


def pair_mean(v, step):
    rows = (iota(v.shape, 0) // step) % 2 == 0
    v = v + jnp.where(rows, roll(v, -step, 0), roll(v, step, 0))
    lanes = (iota(v.shape, 1) // step) % 2 == 0
    v = v + jnp.where(lanes, roll(v, -step, 1), roll(v, step, 1))
    return v * 0.125


def place():
    return tuple(lax.axis_index(axis) for axis in ("gx", "gy", "gz"))


def sizes():
    return tuple(lax.axis_size(axis) for axis in ("gx", "gy", "gz"))


def pack_fine(read, low_ref, high_ref):
    lane = iota((16, 128), 1)
    chunk = lane // 32
    for g in range(4):
        low = high = None
        for j in range(4):
            v = read(4 * g + j)
            first, last = roll(v, 32 * j, 1), roll(v, 32 * j + 32, 1)
            low = first if j == 0 else jnp.where(chunk == j, first, low)
            high = last if j == 0 else jnp.where(chunk == j, last, high)
        low_ref[g] = low
        high_ref[g] = high
    for g, slabs in ((4, (0, 1, 2, 3, 4)), (5, (15, 14, 13, 12, 11))):
        low, high = read(slabs[0]), roll(read(slabs[0]), 32, 1)
        for j in range(1, 5):
            v, here = read(slabs[j]), (lane >= 112 if j == 4 else chunk == j)
            low = jnp.where(here, roll(v, 112 if j == 4 else 32 * j, 1), low)
            high = jnp.where(here, roll(v, (32, 64, 96, 112, 0)[j], 1), high)
        low_ref[g] = low
        high_ref[g] = high


def pack_near(read, low_ref, high_ref):
    chunk = iota((16, 128), 1) // 8
    low = high = None
    for k in range(16):
        v = read(k)
        first, last = roll(v, 8 * k, 1), roll(v, 8 * k + 8, 1)
        low = first if k == 0 else jnp.where(chunk == k, first, low)
        high = last if k == 0 else jnp.where(chunk == k, last, high)
    low_ref[...] = low
    high_ref[...] = high


def prepare_kernel(rhs_in, classes_in, table_in, both, low, high, classes, table, sems):
    copies = [
        pltpu.make_async_copy(rhs_in, both.at[0], sems.at[0]),
        pltpu.make_async_copy(classes_in, classes, sems.at[1]),
        pltpu.make_async_copy(table_in, table, sems.at[2]),
    ]
    for copy in copies:
        copy.start()
    for copy in copies:
        copy.wait()
    for k in range(16):
        c = classes[k]
        v = jnp.zeros((16, 128), F32)
        for index in range(CLASSES):
            v = jnp.where(c == index, table[index], v)
        both[1, k] = v
    for t in range(2):
        pack_fine(lambda k, t=t: both[t, k], low.at[t], high.at[t])


def slab_sources(i):
    x = i - 5
    if 0 <= x < 16:
        return x, 16 + x // 4, 20 + x // 4, -32 * (x % 4), 96 - 32 * (x % 4)
    base, far = (24, -1 - x) if x < 0 else (31, x - 16)
    return base + (x + 5 if x < 0 else far), base + 5, base + 6, (0, -32, -64, -96, -112)[far], (96, 64, 32, 16, 0)[far]


def near_sources(i):
    x = i - 5
    base, above, k = (x, 16, x) if 0 <= x < 16 else ((23 + x, 23, 16 + x) if x < 0 else (x + 9, 30, x - 16))
    return base, above, above + 1, -8 * k, 120 - 8 * k


def assemble_fine(body, sides, i, sources=slab_sources):
    def unit(u):
        return jnp.concatenate([body[u][...], sides[u][...]], axis=0)

    main, above, below, up, down = sources(i)
    lane = iota((32, 128), 1)
    side = jnp.where(lane < 64, roll(unit(above), up, 1), roll(unit(below), down, 1))
    return jnp.concatenate([unit(main), side], axis=1)


def pack_rows_kernel(body, upper, lower):
    for g in range(body.shape[0] // 128):
        for t in range(5):
            here = pl.ds(8 * (5 * g + t), 8)
            upper[here] = body[pl.ds(128 * g + t, 8, stride=16), :]
            lower[here] = body[pl.ds(128 * g + 11 + t, 8, stride=16), :]


def units(body, first, count):
    return [body.at[pl.ds(first + 16 * u, 16)] for u in range(count)]


def unpack_rows(upper, lower, first, sides):
    sides[...] = jnp.zeros(sides.shape, F32)
    for g in range(sides.shape[0] // 128):
        for t in range(5):
            here = pl.ds(8 * (first + 5 * g + t), 8)
            sides[pl.ds(128 * g + t, 8, stride=16), :] = upper[here]
            sides[pl.ds(128 * g + 11 + t, 8, stride=16), :] = lower[here]
    return units(sides, 0, sides.shape[0] // 16)


def squeeze(v):
    return jnp.concatenate([v[:16], jnp.where(iota((8, v.shape[1]), 0) < 4, v[16:24], v[24:])], axis=0)


def near(lane):
    return (lane < 160) | (lane >= 224)


def inside_lanes(lane):
    z = jnp.where(lane < 192, lane, lane - 256) + 128 * place()[2]
    return near(lane) & (z >= 0) & (z < 128 * sizes()[2])


def inside_fine(rows):
    row, lane = iota((rows, 256), 0), iota((rows, 256), 1)
    y = jnp.where(row < rows // 2 + 8, row, row - rows) + 16 * place()[1]
    return inside_lanes(lane) & (y >= 0) & (y < 16 * sizes()[1])


def fine_weights(body, sides, weight0, weight0s, weight1, middle, quads, unit):
    gx, nx = place()[0], sizes()[0]
    inside, insides = inside_fine(32), inside_fine(24)

    def weigh(i):
        kap = assemble_fine(body, sides, i)
        x = 16 * gx + (i - 5)
        v = jnp.where(inside & (x >= 0) & (x < 16 * nx), OMEGA / (kap + 6.0), 0.0)
        weight0[i] = v
        weight0s[i] = squeeze(v)
        return squeeze(kap)

    weigh(0)
    weigh(SLABS - 1)
    for m in range(MIDS):
        kap1 = pair_mean(weigh(2 * m + 1) + weigh(2 * m + 2), 1)
        middle[m] = kap1
        x = 8 * gx + (m - 2)
        weight1[m] = jnp.where(insides & (x >= 0) & (x < 8 * nx), OMEGA / (kap1 + 1.5), 0.0)
    for c in range(4):
        kap2 = pair_mean(middle[2 + 2 * c] + middle[3 + 2 * c], 2)[:16]
        weight2 = OMEGA / (kap2 + 0.375)
        quads[0, c], quads[1, c] = weight2[:, :128], weight2[:, 128:]
    pack_coarse(quads, unit)


def pack_coarse(quads, unit):
    turn = iota((4, 128), 1) % 4
    for half in range(2):
        v = quads[half, 0, pl.ds(0, 4, stride=4), :]
        for c in range(1, 4):
            v = jnp.where(turn == c, quads[half, c, pl.ds(0, 4, stride=4), :], v)
        unit[4 * half:4 * half + 4] = v


def near_sweep(read, weight0, weight1, x0, x1, r1, r, tall):
    for i in range(SLABS):
        v = read(i)
        r[i] = squeeze(v)
        v = weight0[i] * v
        tall[i] = v
        x0[i] = squeeze(v)
    def middle_slab(m, carry):
        i = 2 * m + 1
        two = tall[i] + tall[i + 1]
        rows = squeeze(roll(two, 1, 0) + roll(two, -1, 0))
        two = x0[i] + x0[i + 1]
        lanes = roll(two, 1, 1) + roll(two, -1, 1)
        v = pair_mean(KEEP * (r[i] + r[i + 1]) + ((x0[i - 1] + x0[i + 2]) + two) + (rows + lanes), 1)
        if r1 is not None:
            r1[m] = v
        x1[m] = weight1[m] * v
        return carry

    lax.fori_loop(0, MIDS, middle_slab, 0, unroll=4)


def first_down_kernel(body, upper, lower, weight0, weight0s, weight1, x0, x1, unit, r, tall, r1, quads, sides):
    there = unpack_rows(upper, lower, 5 * UNITS // 8, sides)
    fine_weights(units(body, 16 * UNITS, UNITS), there, weight0, weight0s, weight1, r1, quads, unit.at[1])
    here, there = units(body, 0, UNITS), unpack_rows(upper, lower, 0, sides)
    near_sweep(lambda i: assemble_fine(here, there, i), weight0, weight1, x0, x1, r1, r, tall)
    for c in range(4):
        m = 2 + 2 * c
        two = x1[m] + x1[m + 1]
        left = KEEP * (r1[m] + r1[m + 1]) + 0.25 * (((x1[m - 1] + x1[m + 2]) + two) + around(two, 2, 2))
        v = pair_mean(left, 2)[:16]
        quads[0, c], quads[1, c] = v[:, :128], v[:, 128:]
    pack_coarse(quads, unit.at[0])


def share_sweep(block, weight0, weight1, share, x0, r1, x1, quads):
    for k in range(16):
        x0[k] = weight0[k + 5, :16, :128] * block[k]
    zero, low = jnp.zeros((16, 128), F32), jnp.zeros((8, 256), F32)

    def tall(v):
        return jnp.concatenate([jnp.concatenate([v, zero], axis=1), low], axis=0)

    for m in range(10):
        x = 2 * (m - 1)
        if m == 0:
            left = tall(x0[0])
        elif m == 9:
            left = tall(x0[15])
        else:
            two = x0[x] + x0[x + 1]
            flat = KEEP * (block[x] + block[x + 1]) + two
            flat = flat + x0[x - 1] if x > 0 else flat
            flat = flat + x0[x + 2] if x < 14 else flat
            left = tall(flat) + around(tall(two), 1, 1)
        v = pair_mean(left, 1)
        r1[m] = v
        x1[m] = weight1[m + 1] * v
    for c in range(6):
        pair = [m for m in (2 * c - 1, 2 * c) if 0 <= m < 10]
        two = sum(x1[m] for m in pair)
        left = KEEP * sum(r1[m] for m in pair)
        beside = two + around(two, 2, 2)
        for m in (2 * c - 2, 2 * c + 1):
            beside = beside + x1[m] if 0 <= m < 10 else beside
        v = pair_mean(left + 0.25 * beside, 2)
        quads[0, c], quads[1, c] = v[:, :128], v[:, 128:]
    gy, gz = place()[1:]
    ny, nz = sizes()[1:]
    for half in range(2):
        for start, count, first in ((20, 1, 0), (0, 5, 1)):
            row, lane = iota((count, 128), 0), iota((count, 128), 1)
            y = row // 4 + gy - (1 if count == 1 else 0)
            inside = (y >= 0) & (y < ny)
            if half == 1:
                z = jnp.where(lane < 64, gz + 1, gz - 1)
                inside = inside & (z >= 0) & (z < nz)

            def rows(c):
                v = quads[half, c, pl.ds(start, count, stride=4), :] if count > 1 else quads[half, c, pl.ds(start, 1), :]
                return jnp.where(inside, v, 0.0)

            turn = lane % 4
            v = rows(1)
            for c in range(1, 4):
                v = jnp.where(turn == c, rows(c + 1), v)
            share[pl.ds(6 * half + first, count)] = v
            v = jnp.where(turn == 3, rows(0), jnp.where(turn == 0, rows(5), 0.0))
            share[pl.ds(12 + 6 * half + first, count)] = v


def join_z_kernel(final, own, share, state, above, below, first, last, small):
    lane = iota((6, 128), 1)
    for s in (0, 12):
        main, side = pl.ds(16 + s, 6), pl.ds(22 + s, 6)
        v = share[s:s + 6] + jnp.where(lane >= 124, above[side], 0.0) + jnp.where(lane < 4, below[side], 0.0)
        small[pl.ds(s, 6)] = v
        v = share[s + 6:s + 12] + jnp.where(lane < 32, above[main], jnp.where(lane >= 96, below[main], 0.0))
        small[pl.ds(s + 6, 6)] = v
    row = iota((8, 128), 0)
    if final:
        sums = [state[j:j + 1] + state[j + 1:j + 2] + above[41 + j:42 + j] + below[40 + j:41 + j] for j in (0, 2, 4)]
    else:
        sums = [state[0:1], above[40:41]]
    v = jnp.zeros((8, 128), F32)
    for j, part in enumerate(sums):
        v = jnp.where(row == j, part, v)
    small[24:32] = v
    for k in range(5):
        first[pl.ds(16 * k, 16)] = own[k]
        last[pl.ds(16 * k, 16)] = own[11 + k]
    for ref in (first, last):
        ref[80:96] = above[:16]
        ref[96:112] = below[:16]
        ref[112:144] = small[...]


def join_x_kernel(final, own, above, below, small, before, after, across, body, upper, lower, ahead, behind, stage):
    for k in range(16):
        body[pl.ds(16 * k, 16)] = own[k]
    body[256:272] = above[:16]
    body[272:288] = below[:16]
    body[288:400] = before[:112]
    body[400:512] = after[:112]
    pack_rows_kernel(body, upper, lower)
    gx = place()[0]
    for k, rows in enumerate((small[:24], after[112:136], across[:24], before[112:136])):
        stage[lax.rem(gx + k, 4)] = rows
    turn = iota((12, 128), 1) % 4
    for b in range(4):
        v = stage[b, :12]
        if b < 3:
            v = v + jnp.where(turn == 3, stage[b + 1, 12:], 0.0)
        if b > 0:
            v = v + jnp.where(turn == 0, stage[b - 1, 12:], 0.0)
        for ref in (upper, lower):
            ref[pl.ds(160 + 12 * b, 12)] = v
        for half in range(2):
            ahead[pl.ds(6 * b + 3 * half, 3)] = v[6 * half:6 * half + 3]
            behind[pl.ds(6 * b + 3 * half, 3)] = v[6 * half + 3:6 * half + 6]
    state = small[24:32]
    if not final:
        state = (state + before[136:144]) + (after[136:144] + across[24:32])
    for ref, start in ((upper, 208), (lower, 208), (ahead, 24), (behind, 24)):
        ref[pl.ds(start, 8)] = state


def unfold(v, c):
    turn = iota(v.shape, 1) % 4
    slab = roll(v, -c, 1)
    for j in range(1, 4):
        slab = jnp.where(turn == j, roll(v, j - c, 1), slab)
    return slab


def assemble_shares(own, up1, down1, up2, down2, out, change):
    def zeros(n):
        return jnp.zeros((n, 128), F32)

    for k in range(4):
        halves = []
        for half in range(2):
            s, t = 160 + 12 * k + 6 * half, 6 * k + 3 * half
            v = jnp.concatenate([own[s + 1:s + 6], zeros(10), own[s:s + 1]], axis=0)
            v = v + jnp.concatenate([zeros(3), up1[s:s + 6], zeros(7)], axis=0)
            v = v + jnp.concatenate([zeros(7), up2[t:t + 3], zeros(6)], axis=0)
            v = v + jnp.concatenate([down1[s + 5:s + 6], zeros(10), down1[s:s + 5]], axis=0)
            v = v + jnp.concatenate([zeros(10), down2[t:t + 3], zeros(3)], axis=0)
            halves.append(v)
        out[k] = change(k, jnp.concatenate(halves, axis=1))


def assemble_coarse(gather, t, out, change):
    gy, ny = place()[1], sizes()[1]
    for k in range(4):
        own, up1, up2, down2, down1 = [ny * k + lax.rem(gy + d + ny, ny) for d in (0, 1, 2, -2, -1)]
        v = jnp.concatenate(
            [
                jnp.concatenate([
                    gather[own, t, s:s + 4], gather[up1, t, s:s + 4], gather[up2, t, s:s + 2],
                    gather[down2, t, s + 2:s + 4], gather[down1, t, s:s + 4],
                ], axis=0)
                for s in (0, 4)
            ],
            axis=1,
        )
        out[k] = change(k, v)


def up_sweep(assemble, weight2, weight1, weight0, x0, x1, kap, u, w, a, b, rhs2, spread, middle, t1, t0):
    zero = jnp.zeros((16, 256), F32)
    for ref in (a, b):
        ref[0] = zero
        ref[5] = zero
    assemble(rhs2, lambda g, v: weight2[g] * v)
    for g in range(4):
        a[g + 1] = rhs2[g]
    turn = iota((16, 256), 1) % 4
    for sweep in range(COARSE_SWEEPS - 1):
        old, new = (a, b) if sweep % 2 == 0 else (b, a)
        ahead = [None] + [roll(old[g], -4, 1) for g in range(1, 5)] + [None]
        back = [None] + [roll(old[g], 4, 1) for g in range(1, 5)] + [None]
        for g in range(1, 5):
            v = old[g]
            up = roll(jnp.where(turn == 3, zero if g == 1 else ahead[g - 1], v), 1, 1)
            down = roll(jnp.where(turn == 0, zero if g == 4 else back[g + 1], v), -1, 1)
            beside = (up + down) + (ahead[g] + back[g]) + (roll(v, 1, 0) + roll(v, -1, 0))
            new[g] = (KEEP * v + rhs2[g - 1]) + weight2[g - 1] * (0.0625 * beside)
    last = b if COARSE_SWEEPS % 2 == 0 else a
    gx = place()[0]
    half = iota((8, 256), 0) < 4
    for c in range(6):
        g, t = (gx, 3) if c == 0 else ((gx + 2, 0) if c == 5 else (gx + 1, c - 1))
        v = unfold(last[g], t)
        spread[c] = jnp.concatenate(
            [
                jnp.where(half, jnp.broadcast_to(v[j:j + 1], (8, 256)), jnp.broadcast_to(v[k:k + 1], (8, 256)))
                for j, k in ((0, 1), (2, 3), (4, 15))
            ],
            axis=0,
        )
    for m in range(MIDS):
        t1[m] = x1[m] + spread[m // 2]
    for m in range(1, MIDS - 1):
        v = t1[m]
        beside = (t1[m - 1] + t1[m + 1]) + around(v, 2, 2)
        middle[m] = (KEEP * v + x1[m]) + weight1[m] * (0.25 * beside)
    for i in range(3, SLABS - 3):
        t0[i] = x0[i] + middle[(i - 1) // 2]
    for i in range(4, SLABS - 4):
        v = t0[i]
        beside = (t0[i - 1] + t0[i + 1]) + around(v, 1, 1)
        u[i] = (KEEP * v + x0[i]) + weight0[i] * beside
    for i in range(5, SLABS - 5):
        v = u[i]
        beside = (u[i - 1] + u[i + 1]) + around(v, 1, 1)
        w[i - 5] = (kap[i - 5] + 6.0) * v[:16, :128] - beside[:16, :128]


def lanes_of(values):
    lane = iota((8, 128), 1)
    out = jnp.zeros((8, 128), F32)
    for k, v in enumerate(values):
        out = jnp.where(lane == MARK + k, jnp.sum(v), out)
    return out


def first_up_kernel(gather, weight1, weight0, x0, x1, both, weight2, u, w, share, low, high, dots, *scratch):
    (*scratch, full, y0, y1, z1, quads) = scratch
    row, lane = iota((16, 256), 0), iota((16, 256), 1)
    y = jnp.where(row < 10, row, row - 16) + 4 * place()[1]
    inside = inside_lanes(lane) & (y >= 0) & (y < 4 * sizes()[1])
    assemble_coarse(gather, 1, weight2, lambda s, v: jnp.where(inside, v, 0.0))
    up_sweep(lambda *a: assemble_coarse(gather, 0, *a), weight2, weight1, weight0, x0, x1, both.at[1], full, w, *scratch)
    rz = curve = jnp.zeros((16, 128), F32)
    for k in range(16):
        v = full[k + 5][:16, :128]
        u[k] = v
        rz = rz + both[0, k] * v
        curve = curve + w[k] * v
    dots[...] = lanes_of([rz, curve])
    pack_near(lambda k: w[k], low, high)
    share_sweep(w, weight0, weight1, share, y0, y1, z1, quads)


def whole_sweep(body, shares, weight2, weight1, weight0, weight0s, kap, full, w, x0, x1, r, tall, sides, *scratch):
    here, there = units(body, 0, 32), unpack_rows(shares[1], shares[2], 0, sides)
    near_sweep(lambda i: assemble_fine(here, there, i, near_sources), weight0, weight1, x0, x1, None, r, tall)
    up_sweep(lambda *a: assemble_shares(*shares, *a), weight2, weight1, weight0s, x0, x1, kap, full, w, *scratch)


def second_kernel(body, own, up1, down1, up2, down2, weight2, weight1, weight0, weight0s, both, m0, n0, share, low, high, *scratch):
    (full, *scratch, y0, y1, z1, quads) = scratch
    shares = (own, up1, down1, up2, down2)
    whole_sweep(body, shares, weight2, weight1, weight0, weight0s, both.at[1], full, n0, *scratch)
    for k in range(16):
        m0[k] = full[k + 5, :16, :128]
    pack_near(lambda k: n0[k], low, high)
    share_sweep(n0, weight0, weight1, share, y0, y1, z1, quads)


def third_kernel(body, own, up1, down1, up2, down2, weight2, weight1, weight0, weight0s, both, u0, w0, m0, n0,
                 r1, u1, w1, m1, n1, first, dots, full, last, *scratch):
    shares = (own, up1, down1, up2, down2)
    whole_sweep(body, shares, weight2, weight1, weight0, weight0s, both.at[1], full, last, *scratch)
    total0 = own[208:209] + up2[25:26] + down2[26:27]
    first[...] = jnp.broadcast_to(total0, (8, 128))
    alpha = total0[:, MARK:MARK + 1] / total0[:, MARK + 1:MARK + 2]
    sums = [jnp.zeros((16, 128), F32)] * 12
    for k in range(16):
        vw0, vm0, vn0 = w0[k], m0[k], n0[k]
        vr1 = both[0, k] - alpha * vw0
        vu1 = u0[k] - alpha * vm0
        vw1 = vw0 - alpha * vn0
        vm1 = vm0 - alpha * full[k + 5, :16, :128]
        vn1 = vn0 - alpha * last[k]
        r1[k], u1[k], w1[k], m1[k], n1[k] = vr1, vu1, vw1, vm1, vn1
        terms = [vr1 * vu1, vr1 * vm1, vr1 * vm0, vw1 * vu1, vw1 * vm1, vw1 * vm0,
                 vw0 * vu1, vw0 * vm1, vw0 * vm0, vn1 * vm1, vn1 * vm0, vn0 * vm0]
        sums = [s + t for s, t in zip(sums, terms)]
    dots[...] = lanes_of(sums)


def finish_kernel(first, second, u0, w0, m0, n0, r1, u1, w1, m1, n1, field, residual):
    g0, d0 = first[0:1, MARK:MARK + 1], first[0:1, MARK + 1:MARK + 2]
    (r1u1, r1m1, r1m0, w1u1, w1m1, w1m0, w0u1, w0m1, w0m0, n1m1, n1m0, n0m0) = [
        second[0:1, MARK + k:MARK + k + 1] for k in range(12)
    ]
    alpha0 = g0 / d0
    beta1 = r1u1 / g0
    curve1 = w1u1 + 2.0 * beta1 * w0u1 + beta1 * beta1 * d0
    alpha1 = r1u1 / curve1
    ab = alpha1 * beta1
    su = w1u1 + beta1 * w0u1 - alpha1 * (w1m1 + beta1 * w0m1) - ab * (w1m0 + beta1 * w0m0)
    g2 = (r1u1 - alpha1 * r1m1 - ab * r1m0) - alpha1 * su
    beta2 = g2 / r1u1
    uw = (w1u1 - 2.0 * alpha1 * w1m1 - 2.0 * ab * w1m0) + (alpha1 * alpha1 * n1m1 + 2.0 * alpha1 * ab * n1m0 + ab * ab * n0m0)
    curve2 = uw + 2.0 * beta2 * su + beta2 * beta2 * curve1
    alpha2 = g2 / curve2
    mix = alpha1 + alpha2 * beta2
    cu0, cu1, cm1, cm0 = alpha0 + mix * beta1, mix + alpha2, alpha2 * alpha1, alpha2 * ab
    cw0 = mix * beta1
    for k in range(16):
        field[k] = (cu0 * u0[k] + cu1 * u1[k]) - (cm1 * m1[k] + cm0 * m0[k])
        residual[k] = r1[k] - (cw0 * w0[k] + cu1 * w1[k]) + (cm1 * n1[k] + cm0 * n0[k])


def shape(*dims):
    return jax.ShapeDtypeStruct(dims, F32)


def call(kernel, outs, scratch=(), specs=None, count=0, grant=40):
    return pl.pallas_call(
        kernel,
        out_shape=outs,
        in_specs=specs or [VMEM] * count,
        out_specs=[VMEM] * len(outs),
        scratch_shapes=list(scratch),
        compiler_params=pltpu.CompilerParams(vmem_limit_bytes=grant * 1024 * 1024),
    )


def shift(v, axis, distance):
    count = lax.axis_size(axis)
    return lax.ppermute(v, axis, [((i + distance) % count, i) for i in range(count)])


def fine_exchange(own, low, high):
    above, below = shift(low, "gz", 1), shift(high, "gz", -1)
    first = jnp.concatenate([own[:, :5], above[:, 4:5], below[:, 4:5]], axis=1)
    last = jnp.concatenate([own[:, 11:], above[:, 5:6], below[:, 5:6]], axis=1)
    before, after = shift(last, "gx", -1), shift(first, "gx", 1)
    body = jnp.concatenate([own, above[:, :4], below[:, :4], before, after, own[:, :2]], axis=1).reshape(-1, 128)
    upper, lower = call(pack_rows_kernel, [shape(10 * UNITS, 128)] * 2, count=1)(body)
    return body, shift(upper, "gy", 1), shift(lower, "gy", -1)


def joint_exchange(own, share, low, high, state, final):
    above = shift(jnp.concatenate([low, share, state]), "gz", 1)
    below = shift(jnp.concatenate([high, share, state]), "gz", -1)
    first, last, small = call(
        functools.partial(join_z_kernel, final), [shape(144, 128), shape(144, 128), shape(32, 128)], count=5
    )(own, share, state, above, below)
    before, after, across = shift(last, "gx", -1), shift(first, "gx", 1), shift(small, "gx", 2)
    body, upper, lower, ahead, behind = call(
        functools.partial(join_x_kernel, final), [shape(512, 128), shape(216, 128), shape(216, 128), shape(32, 128), shape(32, 128)],
        [pltpu.VMEM((4, 24, 128), F32)], count=7,
    )(own, above, below, small, before, after, across)
    return body, upper, shift(upper, "gy", 1), shift(lower, "gy", -1), shift(ahead, "gy", 2), shift(behind, "gy", -2)


def gather(unit):
    count = lax.axis_size("gx") * lax.axis_size("gy")
    return lax.all_to_all(jnp.broadcast_to(unit[None], (count,) + unit.shape), ("gx", "gy"), 0, 0, tiled=True)


def total(v):
    axes = ("gx", "gy", "gz")
    count = lax.axis_size("gx") * lax.axis_size("gy") * lax.axis_size("gz")
    parts = lax.all_to_all(jnp.broadcast_to(v[None, :1], (count, 1, 128)), axes, 0, 0, tiled=True)
    return jnp.broadcast_to(parts.sum(0), (8, 128))


def local(right_side, classes, table):
    def scratch(*shapes):
        return [pltpu.VMEM(s, F32) for s in shapes]

    block, short, mids, tile = shape(*BLOCK), shape(*SHORT), shape(*MID), shape(8, 128)
    up_scratch = scratch((6, 16, 256), (6, 16, 256), (4, 16, 256), (6, 24, 256), MID, MID, SHORT, SHORT)

    both, low, high = call(
        prepare_kernel, [shape(2, *BLOCK), shape(2, 6, 16, 128), shape(2, 6, 16, 128)],
        [pltpu.VMEM(BLOCK, jnp.int32), pltpu.SMEM((CLASSES,), F32), pltpu.SemaphoreType.DMA((3,))], specs=[ANY] * 3, grant=60,
    )(right_side, classes, table)
    halos = fine_exchange(both, low, high)
    weight0, weight0s, weight1, x0, x1, unit = call(
        first_down_kernel, [shape(*HALO), short, mids, short, mids, shape(2, 8, 128)],
        scratch(SHORT, HALO, MID, (2, 4, 16, 128), (16 * UNITS, 128)), count=3,
    )(*halos)
    share_outs = [shape(24, 128), shape(16, 128), shape(16, 128)]
    share_scratch = scratch(BLOCK, (10, 24, 256), (10, 24, 256), (2, 6, 24, 128))
    weight2, u0, w0, share, low, high, dots = call(
        first_up_kernel, [shape(4, 16, 256), block, block, *share_outs, tile], up_scratch + share_scratch, count=6
    )(gather(unit), weight1, weight0s, x0, x1, both)

    whole_scratch = scratch(SHORT, MID, SHORT, HALO, (512, 128)) + up_scratch[:-1]
    halos = joint_exchange(w0, share, low, high, dots, False)
    _, own, up1, down1, up2, _ = halos
    ahead, behind = up1[208:210] + up2[24:26], down1[208:210] + own[208:210]
    state = jnp.concatenate([ahead + behind, ahead, behind, jnp.zeros((2, 128), F32)])
    state = state + shift(state, "gz", 4)
    m0, n0, share, low, high = call(
        second_kernel, [block, block, *share_outs], scratch(SHORT) + whole_scratch + share_scratch, count=11
    )(*halos, weight2, weight1, weight0, weight0s, both)
    halos = joint_exchange(n0, share, low, high, state, True)
    r1, u1, w1, m1, n1, first, dots = call(
        third_kernel, [block] * 5 + [tile, tile], scratch(SHORT, BLOCK) + whole_scratch, count=15
    )(*halos, weight2, weight1, weight0, weight0s, both, u0, w0, m0, n0)
    field, residual = call(finish_kernel, [block] * 2, count=11)(
        first, total(dots), u0, w0, m0, n0, r1, u1, w1, m1, n1
    )
    return field, residual


def solution(mesh):
    in_specs = (P("gx", "gy", "gz"), P("gx", "gy", "gz"), P())
    out_specs = (P("gx", "gy", "gz"), P("gx", "gy", "gz"))
    return jax.shard_map(local, mesh=mesh, in_specs=in_specs, out_specs=out_specs, check_vma=False)
```

```python
import functools

import jax
import jax.numpy as jnp
from jax import lax
from jax.experimental import pallas as pl
from jax.experimental.pallas import tpu as pltpu
from jax.sharding import PartitionSpec as P

CLASSES = 16
COARSE_SWEEPS = 6
OMEGA = 0.8
KEEP = 1.0 - OMEGA
F32 = jnp.float32
SLABS, MIDS, UNITS = 26, 12, 40
MARK = 64
BLOCK, HALO, SHORT, MID = (16, 16, 128), (SLABS, 32, 256), (SLABS, 24, 256), (MIDS, 24, 256)
VMEM = pl.BlockSpec(memory_space=pltpu.VMEM)
ANY = pl.BlockSpec(memory_space=pl.ANY)


def iota(shape, dim):
    return lax.broadcasted_iota(jnp.int32, shape, dim)


def roll(v, shift, axis):
    shift = shift % v.shape[axis]
    return v if shift == 0 else pltpu.roll(v, shift, axis)


def around(v, rows, lanes):
    return (roll(v, rows, 0) + roll(v, -rows, 0)) + (roll(v, lanes, 1) + roll(v, -lanes, 1))


def pair_mean(v, step):
    rows = (iota(v.shape, 0) // step) % 2 == 0
    v = v + jnp.where(rows, roll(v, -step, 0), roll(v, step, 0))
    lanes = (iota(v.shape, 1) // step) % 2 == 0
    v = v + jnp.where(lanes, roll(v, -step, 1), roll(v, step, 1))
    return v * 0.125


def place():
    return tuple(lax.axis_index(axis) for axis in ("gx", "gy", "gz"))


def sizes():
    return tuple(lax.axis_size(axis) for axis in ("gx", "gy", "gz"))


def pack_fine(read, low_ref, high_ref):
    lane = iota((16, 128), 1)
    chunk = lane // 32
    for g in range(4):
        low = high = None
        for j in range(4):
            v = read(4 * g + j)
            first, last = roll(v, 32 * j, 1), roll(v, 32 * j + 32, 1)
            low = first if j == 0 else jnp.where(chunk == j, first, low)
            high = last if j == 0 else jnp.where(chunk == j, last, high)
        low_ref[g] = low
        high_ref[g] = high
    for g, slabs in ((4, (0, 1, 2, 3, 4)), (5, (15, 14, 13, 12, 11))):
        low, high = read(slabs[0]), roll(read(slabs[0]), 32, 1)
        for j in range(1, 5):
            v, here = read(slabs[j]), (lane >= 112 if j == 4 else chunk == j)
            low = jnp.where(here, roll(v, 112 if j == 4 else 32 * j, 1), low)
            high = jnp.where(here, roll(v, (32, 64, 96, 112, 0)[j], 1), high)
        low_ref[g] = low
        high_ref[g] = high


def pack_near(read, low_ref, high_ref):
    chunk = iota((16, 128), 1) // 8
    low = high = None
    for k in range(16):
        v = read(k)
        first, last = roll(v, 8 * k, 1), roll(v, 8 * k + 8, 1)
        low = first if k == 0 else jnp.where(chunk == k, first, low)
        high = last if k == 0 else jnp.where(chunk == k, last, high)
    low_ref[...] = low
    high_ref[...] = high


def prepare_kernel(rhs_in, classes_in, table_in, both, low, high, classes, table, sems):
    copies = [
        pltpu.make_async_copy(rhs_in, both.at[0], sems.at[0]),
        pltpu.make_async_copy(classes_in, classes, sems.at[1]),
        pltpu.make_async_copy(table_in, table, sems.at[2]),
    ]
    for copy in copies:
        copy.start()
    for copy in copies:
        copy.wait()
    for k in range(16):
        c = classes[k]
        v = jnp.zeros((16, 128), F32)
        for index in range(CLASSES):
            v = jnp.where(c == index, table[index], v)
        both[1, k] = v
    for t in range(2):
        pack_fine(lambda k, t=t: both[t, k], low.at[t], high.at[t])


def slab_sources(i):
    x = i - 5
    if 0 <= x < 16:
        return x, 16 + x // 4, 20 + x // 4, -32 * (x % 4), 96 - 32 * (x % 4)
    base, far = (24, -1 - x) if x < 0 else (31, x - 16)
    return base + (x + 5 if x < 0 else far), base + 5, base + 6, (0, -32, -64, -96, -112)[far], (96, 64, 32, 16, 0)[far]


def near_sources(i):
    x = i - 5
    base, above, k = (x, 16, x) if 0 <= x < 16 else ((23 + x, 23, 16 + x) if x < 0 else (x + 9, 30, x - 16))
    return base, above, above + 1, -8 * k, 120 - 8 * k


def assemble_fine(body, sides, i, sources=slab_sources):
    def unit(u):
        return jnp.concatenate([body[u][...], sides[u][...]], axis=0)

    main, above, below, up, down = sources(i)
    lane = iota((32, 128), 1)
    side = jnp.where(lane < 64, roll(unit(above), up, 1), roll(unit(below), down, 1))
    return jnp.concatenate([unit(main), side], axis=1)


def pack_rows_kernel(body, upper, lower):
    for g in range(body.shape[0] // 128):
        for t in range(5):
            here = pl.ds(8 * (5 * g + t), 8)
            upper[here] = body[pl.ds(128 * g + t, 8, stride=16), :]
            lower[here] = body[pl.ds(128 * g + 11 + t, 8, stride=16), :]


def units(body, first, count):
    return [body.at[pl.ds(first + 16 * u, 16)] for u in range(count)]


def unpack_rows(upper, lower, first, sides):
    sides[...] = jnp.zeros(sides.shape, F32)
    for g in range(sides.shape[0] // 128):
        for t in range(5):
            here = pl.ds(8 * (first + 5 * g + t), 8)
            sides[pl.ds(128 * g + t, 8, stride=16), :] = upper[here]
            sides[pl.ds(128 * g + 11 + t, 8, stride=16), :] = lower[here]
    return units(sides, 0, sides.shape[0] // 16)


def squeeze(v):
    return jnp.concatenate([v[:16], jnp.where(iota((8, v.shape[1]), 0) < 4, v[16:24], v[24:])], axis=0)


def near(lane):
    return (lane < 160) | (lane >= 224)


def inside_lanes(lane):
    z = jnp.where(lane < 192, lane, lane - 256) + 128 * place()[2]
    return near(lane) & (z >= 0) & (z < 128 * sizes()[2])


def inside_fine(rows):
    row, lane = iota((rows, 256), 0), iota((rows, 256), 1)
    y = jnp.where(row < rows // 2 + 8, row, row - rows) + 16 * place()[1]
    return inside_lanes(lane) & (y >= 0) & (y < 16 * sizes()[1])


def fine_weights(body, sides, weight0, weight0s, weight1, middle, quads, unit):
    gx, nx = place()[0], sizes()[0]
    inside, insides = inside_fine(32), inside_fine(24)

    def weigh(i):
        kap = assemble_fine(body, sides, i)
        x = 16 * gx + (i - 5)
        v = jnp.where(inside & (x >= 0) & (x < 16 * nx), OMEGA / (kap + 6.0), 0.0)
        weight0[i] = v
        weight0s[i] = squeeze(v)
        return squeeze(kap)

    weigh(0)
    weigh(SLABS - 1)
    for m in range(MIDS):
        kap1 = pair_mean(weigh(2 * m + 1) + weigh(2 * m + 2), 1)
        middle[m] = kap1
        x = 8 * gx + (m - 2)
        weight1[m] = jnp.where(insides & (x >= 0) & (x < 8 * nx), OMEGA / (kap1 + 1.5), 0.0)
    for c in range(4):
        kap2 = pair_mean(middle[2 + 2 * c] + middle[3 + 2 * c], 2)[:16]
        weight2 = OMEGA / (kap2 + 0.375)
        quads[0, c], quads[1, c] = weight2[:, :128], weight2[:, 128:]
    pack_coarse(quads, unit)


def pack_coarse(quads, unit):
    turn = iota((4, 128), 1) % 4
    for half in range(2):
        v = quads[half, 0, pl.ds(0, 4, stride=4), :]
        for c in range(1, 4):
            v = jnp.where(turn == c, quads[half, c, pl.ds(0, 4, stride=4), :], v)
        unit[4 * half:4 * half + 4] = v


def near_sweep(read, weight0, weight1, x0, x1, r1, r, tall):
    for i in range(SLABS):
        v = read(i)
        r[i] = squeeze(v)
        v = weight0[i] * v
        tall[i] = v
        x0[i] = squeeze(v)
    def middle_slab(m, carry):
        i = 2 * m + 1
        two = tall[i] + tall[i + 1]
        rows = squeeze(roll(two, 1, 0) + roll(two, -1, 0))
        two = x0[i] + x0[i + 1]
        lanes = roll(two, 1, 1) + roll(two, -1, 1)
        v = pair_mean(KEEP * (r[i] + r[i + 1]) + ((x0[i - 1] + x0[i + 2]) + two) + (rows + lanes), 1)
        if r1 is not None:
            r1[m] = v
        x1[m] = weight1[m] * v
        return carry

    lax.fori_loop(0, MIDS, middle_slab, 0, unroll=4)


def first_down_kernel(body, upper, lower, weight0, weight0s, weight1, x0, x1, unit, r, tall, r1, quads, sides):
    there = unpack_rows(upper, lower, 5 * UNITS // 8, sides)
    fine_weights(units(body, 16 * UNITS, UNITS), there, weight0, weight0s, weight1, r1, quads, unit.at[1])
    here, there = units(body, 0, UNITS), unpack_rows(upper, lower, 0, sides)
    near_sweep(lambda i: assemble_fine(here, there, i), weight0, weight1, x0, x1, r1, r, tall)
    for c in range(4):
        m = 2 + 2 * c
        two = x1[m] + x1[m + 1]
        left = KEEP * (r1[m] + r1[m + 1]) + 0.25 * (((x1[m - 1] + x1[m + 2]) + two) + around(two, 2, 2))
        v = pair_mean(left, 2)[:16]
        quads[0, c], quads[1, c] = v[:, :128], v[:, 128:]
    pack_coarse(quads, unit.at[0])


def share_sweep(block, weight0, weight1, share, x0, r1, x1, quads):
    for k in range(16):
        x0[k] = weight0[k + 5, :16, :128] * block[k]
    zero, low = jnp.zeros((16, 128), F32), jnp.zeros((8, 256), F32)

    def tall(v):
        return jnp.concatenate([jnp.concatenate([v, zero], axis=1), low], axis=0)

    for m in range(10):
        x = 2 * (m - 1)
        if m == 0:
            left = tall(x0[0])
        elif m == 9:
            left = tall(x0[15])
        else:
            two = x0[x] + x0[x + 1]
            flat = KEEP * (block[x] + block[x + 1]) + two
            flat = flat + x0[x - 1] if x > 0 else flat
            flat = flat + x0[x + 2] if x < 14 else flat
            left = tall(flat) + around(tall(two), 1, 1)
        v = pair_mean(left, 1)
        r1[m] = v
        x1[m] = weight1[m + 1] * v
    for c in range(6):
        pair = [m for m in (2 * c - 1, 2 * c) if 0 <= m < 10]
        two = sum(x1[m] for m in pair)
        left = KEEP * sum(r1[m] for m in pair)
        beside = two + around(two, 2, 2)
        for m in (2 * c - 2, 2 * c + 1):
            beside = beside + x1[m] if 0 <= m < 10 else beside
        v = pair_mean(left + 0.25 * beside, 2)
        quads[0, c], quads[1, c] = v[:, :128], v[:, 128:]
    gy, gz = place()[1:]
    ny, nz = sizes()[1:]
    for half in range(2):
        for start, count, first in ((20, 1, 0), (0, 5, 1)):
            row, lane = iota((count, 128), 0), iota((count, 128), 1)
            y = row // 4 + gy - (1 if count == 1 else 0)
            inside = (y >= 0) & (y < ny)
            if half == 1:
                z = jnp.where(lane < 64, gz + 1, gz - 1)
                inside = inside & (z >= 0) & (z < nz)

            def rows(c):
                v = quads[half, c, pl.ds(start, count, stride=4), :] if count > 1 else quads[half, c, pl.ds(start, 1), :]
                return jnp.where(inside, v, 0.0)

            turn = lane % 4
            v = rows(1)
            for c in range(1, 4):
                v = jnp.where(turn == c, rows(c + 1), v)
            share[pl.ds(6 * half + first, count)] = v
            v = jnp.where(turn == 3, rows(0), jnp.where(turn == 0, rows(5), 0.0))
            share[pl.ds(12 + 6 * half + first, count)] = v


def join_z_kernel(final, own, share, state, above, below, first, last, small):
    lane = iota((6, 128), 1)
    for s in (0, 12):
        main, side = pl.ds(16 + s, 6), pl.ds(22 + s, 6)
        v = share[s:s + 6] + jnp.where(lane >= 124, above[side], 0.0) + jnp.where(lane < 4, below[side], 0.0)
        small[pl.ds(s, 6)] = v
        v = share[s + 6:s + 12] + jnp.where(lane < 32, above[main], jnp.where(lane >= 96, below[main], 0.0))
        small[pl.ds(s + 6, 6)] = v
    row = iota((8, 128), 0)
    if final:
        sums = [state[j:j + 1] + state[j + 1:j + 2] + above[41 + j:42 + j] + below[40 + j:41 + j] for j in (0, 2, 4)]
    else:
        sums = [state[0:1], above[40:41]]
    v = jnp.zeros((8, 128), F32)
    for j, part in enumerate(sums):
        v = jnp.where(row == j, part, v)
    small[24:32] = v
    for k in range(5):
        first[pl.ds(16 * k, 16)] = own[k]
        last[pl.ds(16 * k, 16)] = own[11 + k]
    for ref in (first, last):
        ref[80:96] = above[:16]
        ref[96:112] = below[:16]
        ref[112:144] = small[...]


def join_x_kernel(final, own, above, below, small, sums, before, after, across, body, upper, lower, ahead, behind, stage):
    for k in range(16):
        body[pl.ds(16 * k, 16)] = own[k]
    body[256:272] = above[:16]
    body[272:288] = below[:16]
    body[288:400] = before[:112]
    body[400:512] = after[:112]
    pack_rows_kernel(body, upper, lower)
    gx = place()[0]
    for k, rows in enumerate((small[:24], after[112:136], across[:24], before[112:136])):
        stage[lax.rem(gx + k, 4)] = rows
    turn = iota((12, 128), 1) % 4
    for b in range(4):
        v = stage[b, :12]
        if b < 3:
            v = v + jnp.where(turn == 3, stage[b + 1, 12:], 0.0)
        if b > 0:
            v = v + jnp.where(turn == 0, stage[b - 1, 12:], 0.0)
        for ref in (upper, lower):
            ref[pl.ds(160 + 12 * b, 12)] = v
        for half in range(2):
            ahead[pl.ds(6 * b + 3 * half, 3)] = v[6 * half:6 * half + 3]
            behind[pl.ds(6 * b + 3 * half, 3)] = v[6 * half + 3:6 * half + 6]
    state = sums[...]
    if final:
        state = (state + before[136:144]) + (after[136:144] + across[24:32])
    for ref, start in ((upper, 208), (lower, 208), (ahead, 24), (behind, 24)):
        ref[pl.ds(start, 8)] = state


def unfold(v, c):
    turn = iota(v.shape, 1) % 4
    slab = roll(v, -c, 1)
    for j in range(1, 4):
        slab = jnp.where(turn == j, roll(v, j - c, 1), slab)
    return slab


def assemble_shares(own, up1, down1, up2, down2, out, change):
    def zeros(n):
        return jnp.zeros((n, 128), F32)

    for k in range(4):
        halves = []
        for half in range(2):
            s, t = 160 + 12 * k + 6 * half, 6 * k + 3 * half
            v = jnp.concatenate([own[s + 1:s + 6], zeros(10), own[s:s + 1]], axis=0)
            v = v + jnp.concatenate([zeros(3), up1[s:s + 6], zeros(7)], axis=0)
            v = v + jnp.concatenate([zeros(7), up2[t:t + 3], zeros(6)], axis=0)
            v = v + jnp.concatenate([down1[s + 5:s + 6], zeros(10), down1[s:s + 5]], axis=0)
            v = v + jnp.concatenate([zeros(10), down2[t:t + 3], zeros(3)], axis=0)
            halves.append(v)
        out[k] = change(k, jnp.concatenate(halves, axis=1))


def assemble_coarse(gather, t, out, change):
    gy, ny = place()[1], sizes()[1]
    for k in range(4):
        own, up1, up2, down2, down1 = [ny * k + lax.rem(gy + d + ny, ny) for d in (0, 1, 2, -2, -1)]
        v = jnp.concatenate(
            [
                jnp.concatenate([
                    gather[own, t, s:s + 4], gather[up1, t, s:s + 4], gather[up2, t, s:s + 2],
                    gather[down2, t, s + 2:s + 4], gather[down1, t, s:s + 4],
                ], axis=0)
                for s in (0, 4)
            ],
            axis=1,
        )
        out[k] = change(k, v)


def up_sweep(assemble, weight2, weight1, weight0, x0, x1, kap, u, w, a, b, rhs2, spread, middle, t1, t0):
    zero = jnp.zeros((16, 256), F32)
    for ref in (a, b):
        ref[0] = zero
        ref[5] = zero
    assemble(rhs2, lambda g, v: weight2[g] * v)
    for g in range(4):
        a[g + 1] = rhs2[g]
    turn = iota((16, 256), 1) % 4
    for sweep in range(COARSE_SWEEPS - 1):
        old, new = (a, b) if sweep % 2 == 0 else (b, a)
        ahead = [None] + [roll(old[g], -4, 1) for g in range(1, 5)] + [None]
        back = [None] + [roll(old[g], 4, 1) for g in range(1, 5)] + [None]
        for g in range(1, 5):
            v = old[g]
            up = roll(jnp.where(turn == 3, zero if g == 1 else ahead[g - 1], v), 1, 1)
            down = roll(jnp.where(turn == 0, zero if g == 4 else back[g + 1], v), -1, 1)
            beside = (up + down) + (ahead[g] + back[g]) + (roll(v, 1, 0) + roll(v, -1, 0))
            new[g] = (KEEP * v + rhs2[g - 1]) + weight2[g - 1] * (0.0625 * beside)
    last = b if COARSE_SWEEPS % 2 == 0 else a
    gx = place()[0]
    half = iota((8, 256), 0) < 4
    for c in range(6):
        g, t = (gx, 3) if c == 0 else ((gx + 2, 0) if c == 5 else (gx + 1, c - 1))
        v = unfold(last[g], t)
        spread[c] = jnp.concatenate(
            [
                jnp.where(half, jnp.broadcast_to(v[j:j + 1], (8, 256)), jnp.broadcast_to(v[k:k + 1], (8, 256)))
                for j, k in ((0, 1), (2, 3), (4, 15))
            ],
            axis=0,
        )
    for m in range(MIDS):
        t1[m] = x1[m] + spread[m // 2]
    for m in range(1, MIDS - 1):
        v = t1[m]
        beside = (t1[m - 1] + t1[m + 1]) + around(v, 2, 2)
        middle[m] = (KEEP * v + x1[m]) + weight1[m] * (0.25 * beside)
    for i in range(3, SLABS - 3):
        t0[i] = x0[i] + middle[(i - 1) // 2]
    for i in range(4, SLABS - 4):
        v = t0[i]
        beside = (t0[i - 1] + t0[i + 1]) + around(v, 1, 1)
        u[i] = (KEEP * v + x0[i]) + weight0[i] * beside
    for i in range(5, SLABS - 5):
        v = u[i]
        beside = (u[i - 1] + u[i + 1]) + around(v, 1, 1)
        w[i - 5] = (kap[i - 5] + 6.0) * v[:16, :128] - beside[:16, :128]


def lanes_of(values):
    rows = [jnp.sum(v, axis=0, keepdims=True) for v in values]
    sums = jnp.sum(jnp.concatenate(rows + [jnp.zeros((16 - len(rows), 128), F32)], axis=0), axis=1, keepdims=True)
    picked = jnp.where(iota((16, 128), 1) == MARK + iota((16, 128), 0), sums, 0.0)
    return jnp.broadcast_to(jnp.sum(picked, axis=0, keepdims=True), (8, 128))


def first_up_kernel(gather, weight1, weight0, x0, x1, both, weight2, u, w, share, low, high, dots, *scratch):
    (*scratch, full, y0, y1, z1, quads) = scratch
    row, lane = iota((16, 256), 0), iota((16, 256), 1)
    y = jnp.where(row < 10, row, row - 16) + 4 * place()[1]
    inside = inside_lanes(lane) & (y >= 0) & (y < 4 * sizes()[1])
    assemble_coarse(gather, 1, weight2, lambda s, v: jnp.where(inside, v, 0.0))
    up_sweep(lambda *a: assemble_coarse(gather, 0, *a), weight2, weight1, weight0, x0, x1, both.at[1], full, w, *scratch)
    rz = curve = jnp.zeros((16, 128), F32)
    for k in range(16):
        v = full[k + 5][:16, :128]
        u[k] = v
        rz = rz + both[0, k] * v
        curve = curve + w[k] * v
    dots[...] = lanes_of([rz, curve])
    pack_near(lambda k: w[k], low, high)
    share_sweep(w, weight0, weight1, share, y0, y1, z1, quads)


def near_kernel(body, up1, down1, weight0, weight1, x0, x1, r, tall, sides):
    here, there = units(body, 0, 32), unpack_rows(up1, down1, 0, sides)
    near_sweep(lambda i: assemble_fine(here, there, i, near_sources), weight0, weight1, x0, x1, None, r, tall)


def second_kernel(x0, x1, own, up1, down1, up2, down2, weight2, weight1, weight0s, both, m0, n0, share, low, high, *scratch):
    (full, *scratch, y0, y1, z1, quads) = scratch
    shares = (own, up1, down1, up2, down2)
    up_sweep(lambda *a: assemble_shares(*shares, *a), weight2, weight1, weight0s, x0, x1, both.at[1], full, n0, *scratch)
    for k in range(16):
        m0[k] = full[k + 5, :16, :128]
    pack_near(lambda k: n0[k], low, high)
    share_sweep(n0, weight0s, weight1, share, y0, y1, z1, quads)


def third_kernel(x0, x1, own, up1, down1, up2, down2, weight2, weight1, weight0s, both, u0, w0, m0, n0,
                 r1, u1, w1, m1, n1, first, dots, full, last, *scratch):
    shares = (own, up1, down1, up2, down2)
    up_sweep(lambda *a: assemble_shares(*shares, *a), weight2, weight1, weight0s, x0, x1, both.at[1], full, last, *scratch)
    total0 = own[208:209] + up2[25:26] + down2[26:27]
    first[...] = jnp.broadcast_to(total0, (8, 128))
    alpha = total0[:, MARK:MARK + 1] / total0[:, MARK + 1:MARK + 2]
    sums = [jnp.zeros((16, 128), F32)] * 12
    for k in range(16):
        vw0, vm0, vn0 = w0[k], m0[k], n0[k]
        vr1 = both[0, k] - alpha * vw0
        vu1 = u0[k] - alpha * vm0
        vw1 = vw0 - alpha * vn0
        vm1 = vm0 - alpha * full[k + 5, :16, :128]
        vn1 = vn0 - alpha * last[k]
        r1[k], u1[k], w1[k], m1[k], n1[k] = vr1, vu1, vw1, vm1, vn1
        terms = [vr1 * vu1, vr1 * vm1, vr1 * vm0, vw1 * vu1, vw1 * vm1, vw1 * vm0,
                 vw0 * vu1, vw0 * vm1, vw0 * vm0, vn1 * vm1, vn1 * vm0, vn0 * vm0]
        sums = [s + t for s, t in zip(sums, terms)]
    dots[...] = lanes_of(sums)


def finish_kernel(first, second, u0, w0, m0, n0, r1, u1, w1, m1, n1, field, residual):
    g0, d0 = first[0:1, MARK:MARK + 1], first[0:1, MARK + 1:MARK + 2]
    (r1u1, r1m1, r1m0, w1u1, w1m1, w1m0, w0u1, w0m1, w0m0, n1m1, n1m0, n0m0) = [
        second[0:1, MARK + k:MARK + k + 1] for k in range(12)
    ]
    alpha0 = g0 / d0
    beta1 = r1u1 / g0
    curve1 = w1u1 + 2.0 * beta1 * w0u1 + beta1 * beta1 * d0
    alpha1 = r1u1 / curve1
    ab = alpha1 * beta1
    su = w1u1 + beta1 * w0u1 - alpha1 * (w1m1 + beta1 * w0m1) - ab * (w1m0 + beta1 * w0m0)
    g2 = (r1u1 - alpha1 * r1m1 - ab * r1m0) - alpha1 * su
    beta2 = g2 / r1u1
    uw = (w1u1 - 2.0 * alpha1 * w1m1 - 2.0 * ab * w1m0) + (alpha1 * alpha1 * n1m1 + 2.0 * alpha1 * ab * n1m0 + ab * ab * n0m0)
    curve2 = uw + 2.0 * beta2 * su + beta2 * beta2 * curve1
    alpha2 = g2 / curve2
    mix = alpha1 + alpha2 * beta2
    cu0, cu1, cm1, cm0 = alpha0 + mix * beta1, mix + alpha2, alpha2 * alpha1, alpha2 * ab
    cw0 = mix * beta1
    for k in range(16):
        field[k] = (cu0 * u0[k] + cu1 * u1[k]) - (cm1 * m1[k] + cm0 * m0[k])
        residual[k] = r1[k] - (cw0 * w0[k] + cu1 * w1[k]) + (cm1 * n1[k] + cm0 * n0[k])


def shape(*dims):
    return jax.ShapeDtypeStruct(dims, F32)


def call(kernel, outs, scratch=(), specs=None, count=0, grant=40, flops=0):
    return pl.pallas_call(
        kernel,
        out_shape=outs,
        in_specs=specs or [VMEM] * count,
        out_specs=[VMEM] * len(outs),
        scratch_shapes=list(scratch),
        compiler_params=pltpu.CompilerParams(vmem_limit_bytes=grant * 1024 * 1024),
        cost_estimate=pl.CostEstimate(flops=flops, bytes_accessed=flops, transcendentals=0) if flops else None,
    )


def shift(v, axis, distance):
    count = lax.axis_size(axis)
    return lax.ppermute(v, axis, [((i + distance) % count, i) for i in range(count)])


def fine_exchange(own, low, high):
    above, below = shift(low, "gz", 1), shift(high, "gz", -1)
    first = jnp.concatenate([own[:, :5], above[:, 4:5], below[:, 4:5]], axis=1)
    last = jnp.concatenate([own[:, 11:], above[:, 5:6], below[:, 5:6]], axis=1)
    before, after = shift(last, "gx", -1), shift(first, "gx", 1)
    body = jnp.concatenate([own, above[:, :4], below[:, :4], before, after, own[:, :2]], axis=1).reshape(-1, 128)
    upper, lower = call(pack_rows_kernel, [shape(10 * UNITS, 128)] * 2, count=1)(body)
    return body, shift(upper, "gy", 1), shift(lower, "gy", -1)


def joint_exchange(own, share, low, high, state, final):
    above = shift(jnp.concatenate([low, share, state]), "gz", 1)
    below = shift(jnp.concatenate([high, share, state]), "gz", -1)
    first, last, small = call(
        functools.partial(join_z_kernel, final), [shape(144, 128), shape(144, 128), shape(32, 128)], count=5
    )(own, share, state, above, below)
    before, after, across = shift(last, "gx", -1), shift(first, "gx", 1), shift(small, "gx", 2)
    state = small[24:] if final else small[24:] + shift(small[24:], "gz", 4)
    body, upper, lower, ahead, behind = call(
        functools.partial(join_x_kernel, final), [shape(512, 128), shape(216, 128), shape(216, 128), shape(32, 128), shape(32, 128)],
        [pltpu.VMEM((4, 24, 128), F32)], count=8,
    )(own, above, below, small, state, before, after, across)
    return body, upper, shift(upper, "gy", 1), shift(lower, "gy", -1), shift(ahead, "gy", 2), shift(behind, "gy", -2)


def gather(unit):
    count = lax.axis_size("gx") * lax.axis_size("gy")
    return lax.all_to_all(jnp.broadcast_to(unit[None], (count,) + unit.shape), ("gx", "gy"), 0, 0, tiled=True)


def total(v):
    axes = ("gx", "gy", "gz")
    count = lax.axis_size("gx") * lax.axis_size("gy") * lax.axis_size("gz")
    parts = lax.all_to_all(jnp.broadcast_to(v[None, :1], (count, 1, 128)), axes, 0, 0, tiled=True)
    return jnp.broadcast_to(parts.sum(0), (8, 128))


def local(right_side, classes, table):
    def scratch(*shapes):
        return [pltpu.VMEM(s, F32) for s in shapes]

    block, short, mids, tile = shape(*BLOCK), shape(*SHORT), shape(*MID), shape(8, 128)
    up_scratch = scratch((6, 16, 256), (6, 16, 256), (4, 16, 256), (6, 24, 256), MID, MID, SHORT, SHORT)

    both, low, high = call(
        prepare_kernel, [shape(2, *BLOCK), shape(2, 6, 16, 128), shape(2, 6, 16, 128)],
        [pltpu.VMEM(BLOCK, jnp.int32), pltpu.SMEM((CLASSES,), F32), pltpu.SemaphoreType.DMA((3,))], specs=[ANY] * 3, grant=60,
    )(right_side, classes, table)
    halos = fine_exchange(both, low, high)
    weight0, weight0s, weight1, x0, x1, unit = call(
        first_down_kernel, [shape(*HALO), short, mids, short, mids, shape(2, 8, 128)],
        scratch(SHORT, HALO, MID, (2, 4, 16, 128), (16 * UNITS, 128)), count=3,
    )(*halos)
    share_outs = [shape(24, 128), shape(16, 128), shape(16, 128)]
    share_scratch = scratch(BLOCK, (10, 24, 256), (10, 24, 256), (2, 6, 24, 128))
    weight2, u0, w0, share, low, high, dots = call(
        first_up_kernel, [shape(4, 16, 256), block, block, *share_outs, tile], up_scratch + share_scratch, count=6
    )(gather(unit), weight1, weight0s, x0, x1, both)

    def near(body, up1, down1):
        return call(near_kernel, [short, mids], scratch(SHORT, HALO, (512, 128)), count=5, flops=4_000_000)(
            body, up1, down1, weight0, weight1
        )

    body, own, up1, down1, up2, down2 = joint_exchange(w0, share, low, high, dots, False)
    x0, x1 = near(body, up1, down1)
    ahead, behind = up1[208:210] + up2[24:26], down1[208:210] + own[208:210]
    state = jnp.concatenate([ahead + behind, ahead, behind, jnp.zeros((2, 128), F32)])
    m0, n0, share, low, high = call(
        second_kernel, [block, block, *share_outs], scratch(SHORT) + up_scratch[:-1] + share_scratch, count=11
    )(x0, x1, own, up1, down1, up2, down2, weight2, weight1, weight0s, both)
    body, own, up1, down1, up2, down2 = joint_exchange(n0, share, low, high, state, True)
    x0, x1 = near(body, up1, down1)
    r1, u1, w1, m1, n1, first, dots = call(
        third_kernel, [block] * 5 + [tile, tile], scratch(SHORT, BLOCK) + up_scratch[:-1], count=15
    )(x0, x1, own, up1, down1, up2, down2, weight2, weight1, weight0s, both, u0, w0, m0, n0)
    field, residual = call(finish_kernel, [block] * 2, count=11)(
        first, total(dots), u0, w0, m0, n0, r1, u1, w1, m1, n1
    )
    return field, residual


def solution(mesh):
    in_specs = (P("gx", "gy", "gz"), P("gx", "gy", "gz"), P())
    out_specs = (P("gx", "gy", "gz"), P("gx", "gy", "gz"))
    return jax.shard_map(local, mesh=mesh, in_specs=in_specs, out_specs=out_specs, check_vma=False)
```

```python
import functools

import jax
import jax.numpy as jnp
from jax import lax
from jax.experimental import pallas as pl
from jax.experimental.pallas import tpu as pltpu
from jax.sharding import PartitionSpec as P

CLASSES = 16
COARSE_SWEEPS = 6
OMEGA = 0.8
KEEP = 1.0 - OMEGA
F32 = jnp.float32
SLABS, MIDS, UNITS = 26, 12, 40
MARK = 64
BLOCK, HALO, SHORT, MID = (16, 16, 128), (SLABS, 32, 256), (SLABS, 24, 256), (MIDS, 24, 256)
VMEM = pl.BlockSpec(memory_space=pltpu.VMEM)
ANY = pl.BlockSpec(memory_space=pl.ANY)


def iota(shape, dim):
    return lax.broadcasted_iota(jnp.int32, shape, dim)


def roll(v, shift, axis):
    shift = shift % v.shape[axis]
    return v if shift == 0 else pltpu.roll(v, shift, axis)


def around(v, rows, lanes):
    return (roll(v, rows, 0) + roll(v, -rows, 0)) + (roll(v, lanes, 1) + roll(v, -lanes, 1))


def pair_mean(v, step):
    rows = (iota(v.shape, 0) // step) % 2 == 0
    v = v + jnp.where(rows, roll(v, -step, 0), roll(v, step, 0))
    lanes = (iota(v.shape, 1) // step) % 2 == 0
    v = v + jnp.where(lanes, roll(v, -step, 1), roll(v, step, 1))
    return v * 0.125


def place():
    return tuple(lax.axis_index(axis) for axis in ("gx", "gy", "gz"))


def sizes():
    return tuple(lax.axis_size(axis) for axis in ("gx", "gy", "gz"))


def pack_fine(read, low_ref, high_ref):
    lane = iota((16, 128), 1)
    chunk = lane // 32
    for g in range(4):
        low = high = None
        for j in range(4):
            v = read(4 * g + j)
            first, last = roll(v, 32 * j, 1), roll(v, 32 * j + 32, 1)
            low = first if j == 0 else jnp.where(chunk == j, first, low)
            high = last if j == 0 else jnp.where(chunk == j, last, high)
        low_ref[g] = low
        high_ref[g] = high
    for g, slabs in ((4, (0, 1, 2, 3, 4)), (5, (15, 14, 13, 12, 11))):
        low, high = read(slabs[0]), roll(read(slabs[0]), 32, 1)
        for j in range(1, 5):
            v, here = read(slabs[j]), (lane >= 112 if j == 4 else chunk == j)
            low = jnp.where(here, roll(v, 112 if j == 4 else 32 * j, 1), low)
            high = jnp.where(here, roll(v, (32, 64, 96, 112, 0)[j], 1), high)
        low_ref[g] = low
        high_ref[g] = high


def pack_near(read, low_ref, high_ref):
    chunk = iota((16, 128), 1) // 8
    low = high = None
    for k in range(16):
        v = read(k)
        first, last = roll(v, 8 * k, 1), roll(v, 8 * k + 8, 1)
        low = first if k == 0 else jnp.where(chunk == k, first, low)
        high = last if k == 0 else jnp.where(chunk == k, last, high)
    low_ref[...] = low
    high_ref[...] = high


def prepare_kernel(rhs_in, classes_in, table_in, both, low, high, classes, table, sems):
    copies = [
        pltpu.make_async_copy(rhs_in, both.at[0], sems.at[0]),
        pltpu.make_async_copy(classes_in, classes, sems.at[1]),
        pltpu.make_async_copy(table_in, table, sems.at[2]),
    ]
    for copy in copies:
        copy.start()
    for copy in copies:
        copy.wait()
    for k in range(16):
        c = classes[k]
        v = jnp.zeros((16, 128), F32)
        for index in range(CLASSES):
            v = jnp.where(c == index, table[index], v)
        both[1, k] = v
    for t in range(2):
        pack_fine(lambda k, t=t: both[t, k], low.at[t], high.at[t])


def slab_sources(i):
    x = i - 5
    if 0 <= x < 16:
        return x, 16 + x // 4, 20 + x // 4, -32 * (x % 4), 96 - 32 * (x % 4)
    base, far = (24, -1 - x) if x < 0 else (31, x - 16)
    return base + (x + 5 if x < 0 else far), base + 5, base + 6, (0, -32, -64, -96, -112)[far], (96, 64, 32, 16, 0)[far]


def near_sources(i):
    x = i - 5
    base, above, k = (x, 16, x) if 0 <= x < 16 else ((23 + x, 23, 16 + x) if x < 0 else (x + 9, 30, x - 16))
    return base, above, above + 1, -8 * k, 120 - 8 * k


def assemble_half(refs, i, sources):
    main, above, below, up, down = sources(i)
    lane = iota((16, 128), 1)
    side = jnp.where(lane < 64, roll(refs[above][...], up, 1), roll(refs[below][...], down, 1))
    return jnp.concatenate([refs[main][...], side], axis=1)


def assemble_fine(body, sides, i, sources=slab_sources):
    return jnp.concatenate([assemble_half(body, i, sources), assemble_half(sides, i, sources)], axis=0)


class Joined:
    def __init__(self, top, bottom):
        self.top, self.bottom = top, bottom

    def __getitem__(self, i):
        return jnp.concatenate([self.top[i], self.bottom[i]], axis=0)


def pack_rows_kernel(body, upper, lower):
    for g in range(body.shape[0] // 128):
        for t in range(5):
            here = pl.ds(8 * (5 * g + t), 8)
            upper[here] = body[pl.ds(128 * g + t, 8, stride=16), :]
            lower[here] = body[pl.ds(128 * g + 11 + t, 8, stride=16), :]


def units(body, first, count):
    return [body.at[pl.ds(first + 16 * u, 16)] for u in range(count)]


def unpack_rows(upper, lower, first, sides):
    sides[...] = jnp.zeros(sides.shape, F32)
    for g in range(sides.shape[0] // 128):
        for t in range(5):
            here = pl.ds(8 * (first + 5 * g + t), 8)
            sides[pl.ds(128 * g + t, 8, stride=16), :] = upper[here]
            sides[pl.ds(128 * g + 11 + t, 8, stride=16), :] = lower[here]
    return units(sides, 0, sides.shape[0] // 16)


def squeeze(v):
    return jnp.concatenate([v[:16], jnp.where(iota((8, v.shape[1]), 0) < 4, v[16:24], v[24:])], axis=0)


def near(lane):
    return (lane < 160) | (lane >= 224)


def inside_lanes(lane):
    z = jnp.where(lane < 192, lane, lane - 256) + 128 * place()[2]
    return near(lane) & (z >= 0) & (z < 128 * sizes()[2])


def squeeze_half(v):
    return jnp.where(iota((8, v.shape[1]), 0) < 4, v[:8], v[8:])


def weigh(kap, extra, i, shift, cells, inside):
    x = cells * place()[0] + (i - shift)
    return jnp.where(inside & (x >= 0) & (x < cells * sizes()[0]), OMEGA / (kap + extra), 0.0)


def own_weights_kernel(body, weight0, weight1, unit, middle, quads):
    here = units(body, 16 * UNITS, UNITS)
    inside = inside_lanes(iota((16, 256), 1))
    for m in range(-1, MIDS + 1):
        pair = []
        for i in (2 * m + 1, 2 * m + 2):
            if 0 <= i < SLABS:
                kap = assemble_half(here, i, slab_sources)
                weight0[i] = weigh(kap, 6.0, i, 5, 16, inside)
                pair.append(kap)
        if 0 <= m < MIDS:
            kap1 = pair_mean(pair[0] + pair[1], 1)
            middle[m] = kap1
            weight1[m] = weigh(kap1, 1.5, m, 2, 8, inside)
    for c in range(4):
        weight2 = OMEGA / (pair_mean(middle[2 + 2 * c] + middle[3 + 2 * c], 2) + 0.375)
        quads[0, c], quads[1, c] = weight2[:, :128], weight2[:, 128:]
    pack_coarse(quads, unit)


def halo_weights(there, weight0, weight0s, weight1):
    row, lane = iota((16, 256), 0), iota((16, 256), 1)
    y = jnp.where(row < 8, row + 16, row - 16) + 16 * place()[1]
    inside = inside_lanes(lane) & (y >= 0) & (y < 16 * sizes()[1])
    y = jnp.where(iota((8, 256), 0) < 4, 1, -1) + place()[1]
    insides = inside_lanes(iota((8, 256), 1)) & (y >= 0) & (y < sizes()[1])
    for m in range(-1, MIDS + 1):
        pair = []
        for i in (2 * m + 1, 2 * m + 2):
            if 0 <= i < SLABS:
                kap = assemble_half(there, i, slab_sources)
                v = weigh(kap, 6.0, i, 5, 16, inside)
                weight0[i] = v
                weight0s[i] = squeeze_half(v)
                pair.append(squeeze_half(kap))
        if 0 <= m < MIDS:
            weight1[m] = weigh(pair_mean(pair[0] + pair[1], 1), 1.5, m, 2, 8, insides)


def pack_coarse(quads, unit):
    turn = iota((4, 128), 1) % 4
    for half in range(2):
        v = quads[half, 0, pl.ds(0, 4, stride=4), :]
        for c in range(1, 4):
            v = jnp.where(turn == c, quads[half, c, pl.ds(0, 4, stride=4), :], v)
        unit[4 * half:4 * half + 4] = v


def near_sweep(read, weight0, weight1, x0, x1, r1, r, tall):
    for i in range(SLABS):
        v = read(i)
        r[i] = squeeze(v)
        v = weight0[i] * v
        tall[i] = v
        x0[i] = squeeze(v)
    def middle_slab(m, carry):
        i = 2 * m + 1
        two = tall[i] + tall[i + 1]
        rows = squeeze(roll(two, 1, 0) + roll(two, -1, 0))
        two = x0[i] + x0[i + 1]
        lanes = roll(two, 1, 1) + roll(two, -1, 1)
        v = pair_mean(KEEP * (r[i] + r[i + 1]) + ((x0[i - 1] + x0[i + 2]) + two) + (rows + lanes), 1)
        if r1 is not None:
            r1[m] = v
        x1[m] = weight1[m] * v
        return carry

    lax.fori_loop(0, MIDS, middle_slab, 0, unroll=4)


def first_down_kernel(body, upper, lower, own0, own1, halo0, halo0s, halo1, x0, x1, unit, r, tall, r1, quads, sides):
    halo_weights(unpack_rows(upper, lower, 5 * UNITS // 8, sides), halo0, halo0s, halo1)
    here, there = units(body, 0, UNITS), unpack_rows(upper, lower, 0, sides)
    weight0, weight1 = Joined(own0, halo0), Joined(own1, halo1)
    near_sweep(lambda i: assemble_fine(here, there, i), weight0, weight1, x0, x1, r1, r, tall)
    for c in range(4):
        m = 2 + 2 * c
        two = x1[m] + x1[m + 1]
        left = KEEP * (r1[m] + r1[m + 1]) + 0.25 * (((x1[m - 1] + x1[m + 2]) + two) + around(two, 2, 2))
        v = pair_mean(left, 2)[:16]
        quads[0, c], quads[1, c] = v[:, :128], v[:, 128:]
    pack_coarse(quads, unit)


def share_sweep(block, weight0, weight1, share, x0, r1, x1, quads):
    for k in range(16):
        x0[k] = weight0.top[k + 5, :, :128] * block[k]
    zero, low = jnp.zeros((16, 128), F32), jnp.zeros((8, 256), F32)

    def tall(v):
        return jnp.concatenate([jnp.concatenate([v, zero], axis=1), low], axis=0)

    for m in range(10):
        x = 2 * (m - 1)
        if m == 0:
            left = tall(x0[0])
        elif m == 9:
            left = tall(x0[15])
        else:
            two = x0[x] + x0[x + 1]
            flat = KEEP * (block[x] + block[x + 1]) + two
            flat = flat + x0[x - 1] if x > 0 else flat
            flat = flat + x0[x + 2] if x < 14 else flat
            left = tall(flat) + around(tall(two), 1, 1)
        v = pair_mean(left, 1)
        r1[m] = v
        x1[m] = weight1[m + 1] * v
    for c in range(6):
        pair = [m for m in (2 * c - 1, 2 * c) if 0 <= m < 10]
        two = sum(x1[m] for m in pair)
        left = KEEP * sum(r1[m] for m in pair)
        beside = two + around(two, 2, 2)
        for m in (2 * c - 2, 2 * c + 1):
            beside = beside + x1[m] if 0 <= m < 10 else beside
        v = pair_mean(left + 0.25 * beside, 2)
        quads[0, c], quads[1, c] = v[:, :128], v[:, 128:]
    gy, gz = place()[1:]
    ny, nz = sizes()[1:]
    for half in range(2):
        for start, count, first in ((20, 1, 0), (0, 5, 1)):
            row, lane = iota((count, 128), 0), iota((count, 128), 1)
            y = row // 4 + gy - (1 if count == 1 else 0)
            inside = (y >= 0) & (y < ny)
            if half == 1:
                z = jnp.where(lane < 64, gz + 1, gz - 1)
                inside = inside & (z >= 0) & (z < nz)

            def rows(c):
                v = quads[half, c, pl.ds(start, count, stride=4), :] if count > 1 else quads[half, c, pl.ds(start, 1), :]
                return jnp.where(inside, v, 0.0)

            turn = lane % 4
            v = rows(1)
            for c in range(1, 4):
                v = jnp.where(turn == c, rows(c + 1), v)
            share[pl.ds(6 * half + first, count)] = v
            v = jnp.where(turn == 3, rows(0), jnp.where(turn == 0, rows(5), 0.0))
            share[pl.ds(12 + 6 * half + first, count)] = v


def join_z_kernel(final, own, share, state, above, below, first, last, small):
    lane = iota((6, 128), 1)
    for s in (0, 12):
        main, side = pl.ds(16 + s, 6), pl.ds(22 + s, 6)
        v = share[s:s + 6] + jnp.where(lane >= 124, above[side], 0.0) + jnp.where(lane < 4, below[side], 0.0)
        small[pl.ds(s, 6)] = v
        v = share[s + 6:s + 12] + jnp.where(lane < 32, above[main], jnp.where(lane >= 96, below[main], 0.0))
        small[pl.ds(s + 6, 6)] = v
    row = iota((8, 128), 0)
    if final:
        sums = [state[j:j + 1] + state[j + 1:j + 2] + above[41 + j:42 + j] + below[40 + j:41 + j] for j in (0, 2, 4)]
    else:
        sums = [state[0:1], above[40:41]]
    v = jnp.zeros((8, 128), F32)
    for j, part in enumerate(sums):
        v = jnp.where(row == j, part, v)
    small[24:32] = v
    for k in range(5):
        first[pl.ds(16 * k, 16)] = own[k]
        last[pl.ds(16 * k, 16)] = own[11 + k]
    for ref in (first, last):
        ref[80:96] = above[:16]
        ref[96:112] = below[:16]
        ref[112:144] = small[...]


def join_x_kernel(final, own, above, below, small, sums, before, after, across, body, upper, lower, ahead, behind, stage):
    for k in range(16):
        body[pl.ds(16 * k, 16)] = own[k]
    body[256:272] = above[:16]
    body[272:288] = below[:16]
    body[288:400] = before[:112]
    body[400:512] = after[:112]
    pack_rows_kernel(body, upper, lower)
    gx = place()[0]
    for k, rows in enumerate((small[:24], after[112:136], across[:24], before[112:136])):
        stage[lax.rem(gx + k, 4)] = rows
    turn = iota((12, 128), 1) % 4
    for b in range(4):
        v = stage[b, :12]
        if b < 3:
            v = v + jnp.where(turn == 3, stage[b + 1, 12:], 0.0)
        if b > 0:
            v = v + jnp.where(turn == 0, stage[b - 1, 12:], 0.0)
        for ref in (upper, lower):
            ref[pl.ds(160 + 12 * b, 12)] = v
        for half in range(2):
            ahead[pl.ds(6 * b + 3 * half, 3)] = v[6 * half:6 * half + 3]
            behind[pl.ds(6 * b + 3 * half, 3)] = v[6 * half + 3:6 * half + 6]
    state = sums[...]
    if final:
        state = (state + before[136:144]) + (after[136:144] + across[24:32])
    for ref, start in ((upper, 208), (lower, 208), (ahead, 24), (behind, 24)):
        ref[pl.ds(start, 8)] = state


def unfold(v, c):
    turn = iota(v.shape, 1) % 4
    slab = roll(v, -c, 1)
    for j in range(1, 4):
        slab = jnp.where(turn == j, roll(v, j - c, 1), slab)
    return slab


def assemble_shares(own, up1, down1, up2, down2, out, change):
    def zeros(n):
        return jnp.zeros((n, 128), F32)

    for k in range(4):
        halves = []
        for half in range(2):
            s, t = 160 + 12 * k + 6 * half, 6 * k + 3 * half
            v = jnp.concatenate([own[s + 1:s + 6], zeros(10), own[s:s + 1]], axis=0)
            v = v + jnp.concatenate([zeros(3), up1[s:s + 6], zeros(7)], axis=0)
            v = v + jnp.concatenate([zeros(7), up2[t:t + 3], zeros(6)], axis=0)
            v = v + jnp.concatenate([down1[s + 5:s + 6], zeros(10), down1[s:s + 5]], axis=0)
            v = v + jnp.concatenate([zeros(10), down2[t:t + 3], zeros(3)], axis=0)
            halves.append(v)
        out[k] = change(k, jnp.concatenate(halves, axis=1))


def assemble_coarse(gather, t, out, change):
    gy, ny = place()[1], sizes()[1]
    for k in range(4):
        own, up1, up2, down2, down1 = [ny * k + lax.rem(gy + d + ny, ny) for d in (0, 1, 2, -2, -1)]
        v = jnp.concatenate(
            [
                jnp.concatenate([
                    gather[own, t, s:s + 4], gather[up1, t, s:s + 4], gather[up2, t, s:s + 2],
                    gather[down2, t, s + 2:s + 4], gather[down1, t, s:s + 4],
                ], axis=0)
                for s in (0, 4)
            ],
            axis=1,
        )
        out[k] = change(k, v)


def up_sweep(assemble, weight2, weight1, weight0, x0, x1, kap, u, w, a, b, rhs2, spread, middle, t1, t0):
    zero = jnp.zeros((16, 256), F32)
    for ref in (a, b):
        ref[0] = zero
        ref[5] = zero
    assemble(rhs2, lambda g, v: weight2[g] * v)
    for g in range(4):
        a[g + 1] = rhs2[g]
    turn = iota((16, 256), 1) % 4
    for sweep in range(COARSE_SWEEPS - 1):
        old, new = (a, b) if sweep % 2 == 0 else (b, a)
        ahead = [None] + [roll(old[g], -4, 1) for g in range(1, 5)] + [None]
        back = [None] + [roll(old[g], 4, 1) for g in range(1, 5)] + [None]
        for g in range(1, 5):
            v = old[g]
            up = roll(jnp.where(turn == 3, zero if g == 1 else ahead[g - 1], v), 1, 1)
            down = roll(jnp.where(turn == 0, zero if g == 4 else back[g + 1], v), -1, 1)
            beside = (up + down) + (ahead[g] + back[g]) + (roll(v, 1, 0) + roll(v, -1, 0))
            new[g] = (KEEP * v + rhs2[g - 1]) + weight2[g - 1] * (0.0625 * beside)
    last = b if COARSE_SWEEPS % 2 == 0 else a
    gx = place()[0]
    half = iota((8, 256), 0) < 4
    for c in range(6):
        g, t = (gx, 3) if c == 0 else ((gx + 2, 0) if c == 5 else (gx + 1, c - 1))
        v = unfold(last[g], t)
        spread[c] = jnp.concatenate(
            [
                jnp.where(half, jnp.broadcast_to(v[j:j + 1], (8, 256)), jnp.broadcast_to(v[k:k + 1], (8, 256)))
                for j, k in ((0, 1), (2, 3), (4, 15))
            ],
            axis=0,
        )
    for m in range(MIDS):
        t1[m] = x1[m] + spread[m // 2]
    for m in range(1, MIDS - 1):
        v = t1[m]
        beside = (t1[m - 1] + t1[m + 1]) + around(v, 2, 2)
        middle[m] = (KEEP * v + x1[m]) + weight1[m] * (0.25 * beside)
    for i in range(3, SLABS - 3):
        t0[i] = x0[i] + middle[(i - 1) // 2]
    for i in range(4, SLABS - 4):
        v = t0[i]
        beside = (t0[i - 1] + t0[i + 1]) + around(v, 1, 1)
        u[i] = (KEEP * v + x0[i]) + weight0[i] * beside
    for i in range(5, SLABS - 5):
        v = u[i]
        beside = (u[i - 1] + u[i + 1]) + around(v, 1, 1)
        w[i - 5] = (kap[i - 5] + 6.0) * v[:16, :128] - beside[:16, :128]


def lanes_of(values):
    rows = [jnp.sum(v, axis=0, keepdims=True) for v in values]
    sums = jnp.sum(jnp.concatenate(rows + [jnp.zeros((16 - len(rows), 128), F32)], axis=0), axis=1, keepdims=True)
    picked = jnp.where(iota((16, 128), 1) == MARK + iota((16, 128), 0), sums, 0.0)
    return jnp.broadcast_to(jnp.sum(picked, axis=0, keepdims=True), (8, 128))


def wide(row, k):
    return jnp.broadcast_to(row[:, MARK + k:MARK + k + 1], (16, 128))


def first_up_kernel(gather, own0, halo0s, own1, halo1, x0, x1, both, weight2, u, w, share, low, high, dots, *scratch):
    (*scratch, full, y0, y1, z1, quads) = scratch
    weight0, weight1 = Joined(own0, halo0s), Joined(own1, halo1)
    row, lane = iota((16, 256), 0), iota((16, 256), 1)
    y = jnp.where(row < 10, row, row - 16) + 4 * place()[1]
    inside = inside_lanes(lane) & (y >= 0) & (y < 4 * sizes()[1])
    assemble_coarse(gather, 1, weight2, lambda s, v: jnp.where(inside, v, 0.0))
    up_sweep(lambda *a: assemble_coarse(gather, 0, *a), weight2, weight1, weight0, x0, x1, both.at[1], full, w, *scratch)
    rz = curve = jnp.zeros((16, 128), F32)
    for k in range(16):
        v = full[k + 5][:16, :128]
        u[k] = v
        rz = rz + both[0, k] * v
        curve = curve + w[k] * v
    dots[...] = lanes_of([rz, curve])
    pack_near(lambda k: w[k], low, high)
    share_sweep(w, weight0, weight1, share, y0, y1, z1, quads)


def near_kernel(body, up1, down1, own0, halo0, own1, halo1, x0, x1, r, tall, sides):
    weight0, weight1 = Joined(own0, halo0), Joined(own1, halo1)
    here, there = units(body, 0, 32), unpack_rows(up1, down1, 0, sides)
    near_sweep(lambda i: assemble_fine(here, there, i, near_sources), weight0, weight1, x0, x1, None, r, tall)


def second_kernel(x0, x1, own, up1, down1, up2, down2, weight2, own0, halo0s, own1, halo1, both,
                  m0, n0, share, low, high, *scratch):
    weight0s, weight1 = Joined(own0, halo0s), Joined(own1, halo1)
    (full, *scratch, y0, y1, z1, quads) = scratch
    shares = (own, up1, down1, up2, down2)
    up_sweep(lambda *a: assemble_shares(*shares, *a), weight2, weight1, weight0s, x0, x1, both.at[1], full, n0, *scratch)
    for k in range(16):
        m0[k] = full[k + 5, :16, :128]
    pack_near(lambda k: n0[k], low, high)
    share_sweep(n0, weight0s, weight1, share, y0, y1, z1, quads)


def third_kernel(x0, x1, own, up1, down1, up2, down2, weight2, own0, halo0s, own1, halo1, both, u0, w0, m0, n0,
                 r1, u1, w1, m1, n1, first, dots, full, last, *scratch):
    weight0s, weight1 = Joined(own0, halo0s), Joined(own1, halo1)
    shares = (own, up1, down1, up2, down2)
    up_sweep(lambda *a: assemble_shares(*shares, *a), weight2, weight1, weight0s, x0, x1, both.at[1], full, last, *scratch)
    total0 = own[208:209] + up2[25:26] + down2[26:27]
    first[...] = jnp.broadcast_to(total0, (8, 128))
    alpha = wide(total0, 0) / wide(total0, 1)
    sums = [jnp.zeros((16, 128), F32)] * 12
    for k in range(16):
        vw0, vm0, vn0 = w0[k], m0[k], n0[k]
        vr1 = both[0, k] - alpha * vw0
        vu1 = u0[k] - alpha * vm0
        vw1 = vw0 - alpha * vn0
        vm1 = vm0 - alpha * full[k + 5, :16, :128]
        vn1 = vn0 - alpha * last[k]
        r1[k], u1[k], w1[k], m1[k], n1[k] = vr1, vu1, vw1, vm1, vn1
        terms = [vr1 * vu1, vr1 * vm1, vr1 * vm0, vw1 * vu1, vw1 * vm1, vw1 * vm0,
                 vw0 * vu1, vw0 * vm1, vw0 * vm0, vn1 * vm1, vn1 * vm0, vn0 * vm0]
        sums = [s + t for s, t in zip(sums, terms)]
    dots[...] = lanes_of(sums)


def finish_kernel(first, second, u0, w0, m0, n0, r1, u1, w1, m1, n1, field_out, residual_out, field, residual, sems):
    g0, d0 = [wide(first[0:1], k) for k in range(2)]
    (r1u1, r1m1, r1m0, w1u1, w1m1, w1m0, w0u1, w0m1, w0m0, n1m1, n1m0, n0m0) = [wide(second[0:1], k) for k in range(12)]
    alpha0 = g0 / d0
    beta1 = r1u1 / g0
    curve1 = w1u1 + 2.0 * beta1 * w0u1 + beta1 * beta1 * d0
    alpha1 = r1u1 / curve1
    ab = alpha1 * beta1
    su = w1u1 + beta1 * w0u1 - alpha1 * (w1m1 + beta1 * w0m1) - ab * (w1m0 + beta1 * w0m0)
    g2 = (r1u1 - alpha1 * r1m1 - ab * r1m0) - alpha1 * su
    beta2 = g2 / r1u1
    uw = (w1u1 - 2.0 * alpha1 * w1m1 - 2.0 * ab * w1m0) + (alpha1 * alpha1 * n1m1 + 2.0 * alpha1 * ab * n1m0 + ab * ab * n0m0)
    curve2 = uw + 2.0 * beta2 * su + beta2 * beta2 * curve1
    alpha2 = g2 / curve2
    mix = alpha1 + alpha2 * beta2
    cu0, cu1, cm1, cm0 = alpha0 + mix * beta1, mix + alpha2, alpha2 * alpha1, alpha2 * ab
    cw0 = mix * beta1
    copies = []
    for k in range(16):
        field[k] = (cu0 * u0[k] + cu1 * u1[k]) - (cm1 * m1[k] + cm0 * m0[k])
        residual[k] = r1[k] - (cw0 * w0[k] + cu1 * w1[k]) + (cm1 * n1[k] + cm0 * n0[k])
        if k % 4 == 3:
            part = pl.ds(k - 3, 4)
            copies.append(pltpu.make_async_copy(field.at[part], field_out.at[part], sems.at[0, k // 4]))
            copies.append(pltpu.make_async_copy(residual.at[part], residual_out.at[part], sems.at[1, k // 4]))
            copies[-2].start()
            copies[-1].start()
    for copy in copies:
        copy.wait()


def shape(*dims):
    return jax.ShapeDtypeStruct(dims, F32)


def call(kernel, outs, scratch=(), specs=None, count=0, grant=40, flops=0, out=VMEM):
    return pl.pallas_call(
        kernel,
        out_shape=outs,
        in_specs=specs or [VMEM] * count,
        out_specs=[out] * len(outs),
        scratch_shapes=list(scratch),
        compiler_params=pltpu.CompilerParams(vmem_limit_bytes=grant * 1024 * 1024),
        cost_estimate=pl.CostEstimate(flops=flops, bytes_accessed=flops, transcendentals=0) if flops else None,
    )


def shift(v, axis, distance):
    count = lax.axis_size(axis)
    return lax.ppermute(v, axis, [((i + distance) % count, i) for i in range(count)])


def fine_exchange(own, low, high):
    above, below = shift(low, "gz", 1), shift(high, "gz", -1)
    first = jnp.concatenate([own[:, :5], above[:, 4:5], below[:, 4:5]], axis=1)
    last = jnp.concatenate([own[:, 11:], above[:, 5:6], below[:, 5:6]], axis=1)
    before, after = shift(last, "gx", -1), shift(first, "gx", 1)
    body = jnp.concatenate([own, above[:, :4], below[:, :4], before, after, own[:, :2]], axis=1).reshape(-1, 128)
    upper, lower = call(pack_rows_kernel, [shape(10 * UNITS, 128)] * 2, count=1)(body)
    return body, shift(upper, "gy", 1), shift(lower, "gy", -1)


def joint_exchange(own, share, low, high, state, final):
    above = shift(jnp.concatenate([low, share, state]), "gz", 1)
    below = shift(jnp.concatenate([high, share, state]), "gz", -1)
    first, last, small = call(
        functools.partial(join_z_kernel, final), [shape(144, 128), shape(144, 128), shape(32, 128)], count=5
    )(own, share, state, above, below)
    before, after, across = shift(last, "gx", -1), shift(first, "gx", 1), shift(small, "gx", 2)
    state = small[24:] if final else small[24:] + shift(small[24:], "gz", 4)
    body, upper, lower, ahead, behind = call(
        functools.partial(join_x_kernel, final), [shape(512, 128), shape(216, 128), shape(216, 128), shape(32, 128), shape(32, 128)],
        [pltpu.VMEM((4, 24, 128), F32)], count=8,
    )(own, above, below, small, state, before, after, across)
    return body, upper, shift(upper, "gy", 1), shift(lower, "gy", -1), shift(ahead, "gy", 2), shift(behind, "gy", -2)


def gather(unit):
    count = lax.axis_size("gx") * lax.axis_size("gy")
    return lax.all_to_all(jnp.broadcast_to(unit[None], (count,) + unit.shape), ("gx", "gy"), 0, 0, tiled=True)


def total(v):
    axes = ("gx", "gy", "gz")
    count = lax.axis_size("gx") * lax.axis_size("gy") * lax.axis_size("gz")
    parts = lax.all_to_all(jnp.broadcast_to(v[None, :1], (count, 1, 128)), axes, 0, 0, tiled=True)
    return jnp.broadcast_to(parts.sum(0), (8, 128))


def local(right_side, classes, table):
    def scratch(*shapes):
        return [pltpu.VMEM(s, F32) for s in shapes]

    block, short, mids, tile = shape(*BLOCK), shape(*SHORT), shape(*MID), shape(8, 128)
    up_scratch = scratch((6, 16, 256), (6, 16, 256), (4, 16, 256), (6, 24, 256), MID, MID, SHORT, SHORT)

    both, low, high = call(
        prepare_kernel, [shape(2, *BLOCK), shape(2, 6, 16, 128), shape(2, 6, 16, 128)],
        [pltpu.VMEM(BLOCK, jnp.int32), pltpu.SMEM((CLASSES,), F32), pltpu.SemaphoreType.DMA((3,))], specs=[ANY] * 3, grant=60,
    )(right_side, classes, table)
    halos = fine_exchange(both, low, high)
    own0, own1, unit2 = call(
        own_weights_kernel, [shape(SLABS, 16, 256), shape(MIDS, 16, 256), tile],
        scratch((MIDS, 16, 256), (2, 4, 16, 128)), count=1, flops=4_000_000,
    )(halos[0])
    halo0, halo0s, halo1, x0, x1, unit = call(
        first_down_kernel, [shape(SLABS, 16, 256), shape(SLABS, 8, 256), shape(MIDS, 8, 256), short, mids, tile],
        scratch(SHORT, HALO, MID, (2, 4, 16, 128), (16 * UNITS, 128)), count=5,
    )(*halos, own0, own1)
    share_outs = [shape(24, 128), shape(16, 128), shape(16, 128)]
    share_scratch = scratch(BLOCK, (10, 24, 256), (10, 24, 256), (2, 6, 24, 128))
    weight2, u0, w0, share, low, high, dots = call(
        first_up_kernel, [shape(4, 16, 256), block, block, *share_outs, tile], up_scratch + share_scratch, count=8
    )(gather(jnp.stack([unit, unit2])), own0, halo0s, own1, halo1, x0, x1, both)

    def near(body, up1, down1):
        return call(near_kernel, [short, mids], scratch(SHORT, HALO, (512, 128)), count=7, flops=4_000_000)(
            body, up1, down1, own0, halo0, own1, halo1
        )

    body, own, up1, down1, up2, down2 = joint_exchange(w0, share, low, high, dots, False)
    x0, x1 = near(body, up1, down1)
    ahead, behind = up1[208:210] + up2[24:26], down1[208:210] + own[208:210]
    state = jnp.concatenate([ahead + behind, ahead, behind, jnp.zeros((2, 128), F32)])
    m0, n0, share, low, high = call(
        second_kernel, [block, block, *share_outs], scratch(SHORT) + up_scratch[:-1] + share_scratch, count=13
    )(x0, x1, own, up1, down1, up2, down2, weight2, own0, halo0s, own1, halo1, both)
    body, own, up1, down1, up2, down2 = joint_exchange(n0, share, low, high, state, True)
    x0, x1 = near(body, up1, down1)
    r1, u1, w1, m1, n1, first, dots = call(
        third_kernel, [block] * 5 + [tile, tile], scratch(SHORT, BLOCK) + up_scratch[:-1], count=17
    )(x0, x1, own, up1, down1, up2, down2, weight2, own0, halo0s, own1, halo1, both, u0, w0, m0, n0)
    field, residual = call(
        finish_kernel, [block] * 2, scratch(BLOCK, BLOCK) + [pltpu.SemaphoreType.DMA((2, 4))], count=11, out=ANY
    )(
        first, total(dots), u0, w0, m0, n0, r1, u1, w1, m1, n1
    )
    return field, residual


def solution(mesh):
    in_specs = (P("gx", "gy", "gz"), P("gx", "gy", "gz"), P())
    out_specs = (P("gx", "gy", "gz"), P("gx", "gy", "gz"))
    return jax.shard_map(local, mesh=mesh, in_specs=in_specs, out_specs=out_specs, check_vma=False)
```

```python
import functools

import jax
import jax.numpy as jnp
from jax import lax
from jax.experimental import pallas as pl
from jax.experimental.pallas import tpu as pltpu
from jax.sharding import PartitionSpec as P

CLASSES = 16
COARSE_SWEEPS = 6
OMEGA = 0.8
KEEP = 1.0 - OMEGA
F32 = jnp.float32
SLABS, MIDS, UNITS = 26, 12, 40
MARK = 64
BLOCK, HALO, SHORT, MID = (16, 16, 128), (SLABS, 32, 256), (SLABS, 24, 256), (MIDS, 24, 256)
VMEM = pl.BlockSpec(memory_space=pltpu.VMEM)
ANY = pl.BlockSpec(memory_space=pl.ANY)


def iota(shape, dim):
    return lax.broadcasted_iota(jnp.int32, shape, dim)


def roll(v, shift, axis):
    shift = shift % v.shape[axis]
    return v if shift == 0 else pltpu.roll(v, shift, axis)


def around(v, rows, lanes):
    return (roll(v, rows, 0) + roll(v, -rows, 0)) + (roll(v, lanes, 1) + roll(v, -lanes, 1))


def pair_mean(v, step):
    rows = (iota(v.shape, 0) // step) % 2 == 0
    v = v + jnp.where(rows, roll(v, -step, 0), roll(v, step, 0))
    lanes = (iota(v.shape, 1) // step) % 2 == 0
    v = v + jnp.where(lanes, roll(v, -step, 1), roll(v, step, 1))
    return v * 0.125


def place():
    return tuple(lax.axis_index(axis) for axis in ("gx", "gy", "gz"))


def sizes():
    return tuple(lax.axis_size(axis) for axis in ("gx", "gy", "gz"))


def pack_fine(read, low_ref, high_ref):
    lane = iota((16, 128), 1)
    chunk = lane // 32
    for g in range(4):
        low = high = None
        for j in range(4):
            v = read(4 * g + j)
            first, last = roll(v, 32 * j, 1), roll(v, 32 * j + 32, 1)
            low = first if j == 0 else jnp.where(chunk == j, first, low)
            high = last if j == 0 else jnp.where(chunk == j, last, high)
        low_ref[g] = low
        high_ref[g] = high
    for g, slabs in ((4, (0, 1, 2, 3, 4)), (5, (15, 14, 13, 12, 11))):
        low, high = read(slabs[0]), roll(read(slabs[0]), 32, 1)
        for j in range(1, 5):
            v, here = read(slabs[j]), (lane >= 112 if j == 4 else chunk == j)
            low = jnp.where(here, roll(v, 112 if j == 4 else 32 * j, 1), low)
            high = jnp.where(here, roll(v, (32, 64, 96, 112, 0)[j], 1), high)
        low_ref[g] = low
        high_ref[g] = high


def pack_near(read, low_ref, high_ref):
    chunk = iota((16, 128), 1) // 8
    low = high = None
    for k in range(16):
        v = read(k)
        first, last = roll(v, 8 * k, 1), roll(v, 8 * k + 8, 1)
        low = first if k == 0 else jnp.where(chunk == k, first, low)
        high = last if k == 0 else jnp.where(chunk == k, last, high)
    low_ref[...] = low
    high_ref[...] = high


def prepare_kernel(rhs_in, classes_in, table_in, both, low, high, classes, table, sems):
    copies = [
        pltpu.make_async_copy(rhs_in, both.at[0], sems.at[0]),
        pltpu.make_async_copy(classes_in, classes, sems.at[1]),
        pltpu.make_async_copy(table_in, table, sems.at[2]),
    ]
    for copy in copies:
        copy.start()
    for copy in copies:
        copy.wait()
    for k in range(16):
        c = classes[k]
        v = jnp.zeros((16, 128), F32)
        for index in range(CLASSES):
            v = jnp.where(c == index, table[index], v)
        both[1, k] = v
    for t in range(2):
        pack_fine(lambda k, t=t: both[t, k], low.at[t], high.at[t])


def slab_sources(i):
    x = i - 5
    if 0 <= x < 16:
        return x, 16 + x // 4, 20 + x // 4, -32 * (x % 4), 96 - 32 * (x % 4)
    base, far = (24, -1 - x) if x < 0 else (31, x - 16)
    return base + (x + 5 if x < 0 else far), base + 5, base + 6, (0, -32, -64, -96, -112)[far], (96, 64, 32, 16, 0)[far]


def near_sources(i):
    x = i - 5
    base, above, k = (x, 16, x) if 0 <= x < 16 else ((23 + x, 23, 16 + x) if x < 0 else (x + 9, 30, x - 16))
    return base, above, above + 1, -8 * k, 120 - 8 * k


def assemble_half(refs, i, sources):
    main, above, below, up, down = sources(i)
    lane = iota((16, 128), 1)
    side = jnp.where(lane < 64, roll(refs[above][...], up, 1), roll(refs[below][...], down, 1))
    return jnp.concatenate([refs[main][...], side], axis=1)


def assemble_fine(body, sides, i, sources=slab_sources):
    return jnp.concatenate([assemble_half(body, i, sources), assemble_half(sides, i, sources)], axis=0)


class Joined:
    def __init__(self, top, bottom):
        self.top, self.bottom = top, bottom

    def __getitem__(self, i):
        return jnp.concatenate([self.top[i], self.bottom[i]], axis=0)


def pack_rows_kernel(body, upper, lower):
    for g in range(body.shape[0] // 128):
        for t in range(5):
            here = pl.ds(8 * (5 * g + t), 8)
            upper[here] = body[pl.ds(128 * g + t, 8, stride=16), :]
            lower[here] = body[pl.ds(128 * g + 11 + t, 8, stride=16), :]


def units(body, first, count):
    return [body.at[pl.ds(first + 16 * u, 16)] for u in range(count)]


def unpack_rows(upper, lower, first, sides):
    sides[...] = jnp.zeros(sides.shape, F32)
    for g in range(sides.shape[0] // 128):
        for t in range(5):
            here = pl.ds(8 * (first + 5 * g + t), 8)
            sides[pl.ds(128 * g + t, 8, stride=16), :] = upper[here]
            sides[pl.ds(128 * g + 11 + t, 8, stride=16), :] = lower[here]
    return units(sides, 0, sides.shape[0] // 16)


def squeeze(v):
    return jnp.concatenate([v[:16], jnp.where(iota((8, v.shape[1]), 0) < 4, v[16:24], v[24:])], axis=0)


def near(lane):
    return (lane < 160) | (lane >= 224)


def inside_lanes(lane):
    z = jnp.where(lane < 192, lane, lane - 256) + 128 * place()[2]
    return near(lane) & (z >= 0) & (z < 128 * sizes()[2])


def squeeze_half(v):
    return jnp.where(iota((8, v.shape[1]), 0) < 4, v[:8], v[8:])


def weigh(kap, extra, i, shift, cells, inside):
    x = cells * place()[0] + (i - shift)
    return jnp.where(inside & (x >= 0) & (x < cells * sizes()[0]), OMEGA / (kap + extra), 0.0)


def own_weights_kernel(body, weight0, weight1, unit, middle, quads):
    here = units(body, 16 * UNITS, UNITS)
    inside = inside_lanes(iota((16, 256), 1))
    for m in range(-1, MIDS + 1):
        pair = []
        for i in (2 * m + 1, 2 * m + 2):
            if 0 <= i < SLABS:
                kap = assemble_half(here, i, slab_sources)
                weight0[i] = weigh(kap, 6.0, i, 5, 16, inside)
                pair.append(kap)
        if 0 <= m < MIDS:
            kap1 = pair_mean(pair[0] + pair[1], 1)
            middle[m] = kap1
            weight1[m] = weigh(kap1, 1.5, m, 2, 8, inside)
    for c in range(4):
        weight2 = OMEGA / (pair_mean(middle[2 + 2 * c] + middle[3 + 2 * c], 2) + 0.375)
        quads[0, c], quads[1, c] = weight2[:, :128], weight2[:, 128:]
    pack_coarse(quads, unit)


def halo_weights(there, weight0, weight0s, weight1):
    row, lane = iota((16, 256), 0), iota((16, 256), 1)
    y = jnp.where(row < 8, row + 16, row - 16) + 16 * place()[1]
    inside = inside_lanes(lane) & (y >= 0) & (y < 16 * sizes()[1])
    y = jnp.where(iota((8, 256), 0) < 4, 1, -1) + place()[1]
    insides = inside_lanes(iota((8, 256), 1)) & (y >= 0) & (y < sizes()[1])
    for m in range(-1, MIDS + 1):
        pair = []
        for i in (2 * m + 1, 2 * m + 2):
            if 0 <= i < SLABS:
                kap = assemble_half(there, i, slab_sources)
                v = weigh(kap, 6.0, i, 5, 16, inside)
                weight0[i] = v
                weight0s[i] = squeeze_half(v)
                pair.append(squeeze_half(kap))
        if 0 <= m < MIDS:
            weight1[m] = weigh(pair_mean(pair[0] + pair[1], 1), 1.5, m, 2, 8, insides)


def pack_coarse(quads, unit):
    turn = iota((4, 128), 1) % 4
    for half in range(2):
        v = quads[half, 0, pl.ds(0, 4, stride=4), :]
        for c in range(1, 4):
            v = jnp.where(turn == c, quads[half, c, pl.ds(0, 4, stride=4), :], v)
        unit[4 * half:4 * half + 4] = v


def near_sweep(read, weight0, weight1, x0, x1, r1, r, tall):
    for i in range(SLABS):
        v = read(i)
        r[i] = squeeze(v)
        v = weight0[i] * v
        tall[i] = v
        x0[i] = squeeze(v)
    def middle_slab(m, carry):
        i = 2 * m + 1
        two = tall[i] + tall[i + 1]
        rows = squeeze(roll(two, 1, 0) + roll(two, -1, 0))
        two = x0[i] + x0[i + 1]
        lanes = roll(two, 1, 1) + roll(two, -1, 1)
        v = pair_mean(KEEP * (r[i] + r[i + 1]) + ((x0[i - 1] + x0[i + 2]) + two) + (rows + lanes), 1)
        if r1 is not None:
            r1[m] = v
        x1[m] = weight1[m] * v
        return carry

    lax.fori_loop(0, MIDS, middle_slab, 0, unroll=4)


def first_down_kernel(body, upper, lower, own0, own1, halo0, halo0s, halo1, x0, x1, unit, r, tall, r1, quads, sides):
    halo_weights(unpack_rows(upper, lower, 5 * UNITS // 8, sides), halo0, halo0s, halo1)
    here, there = units(body, 0, UNITS), unpack_rows(upper, lower, 0, sides)
    weight0, weight1 = Joined(own0, halo0), Joined(own1, halo1)
    near_sweep(lambda i: assemble_fine(here, there, i), weight0, weight1, x0, x1, r1, r, tall)
    for c in range(4):
        m = 2 + 2 * c
        two = x1[m] + x1[m + 1]
        left = KEEP * (r1[m] + r1[m + 1]) + 0.25 * (((x1[m - 1] + x1[m + 2]) + two) + around(two, 2, 2))
        v = pair_mean(left, 2)[:16]
        quads[0, c], quads[1, c] = v[:, :128], v[:, 128:]
    pack_coarse(quads, unit)


def share_sweep(block, weight0, weight1, share, x0, r1, x1, quads):
    for k in range(16):
        x0[k] = weight0.top[k + 5, :, :128] * block[k]
    zero, low = jnp.zeros((16, 128), F32), jnp.zeros((8, 256), F32)

    def tall(v):
        return jnp.concatenate([jnp.concatenate([v, zero], axis=1), low], axis=0)

    for m in range(10):
        x = 2 * (m - 1)
        if m == 0:
            left = tall(x0[0])
        elif m == 9:
            left = tall(x0[15])
        else:
            two = x0[x] + x0[x + 1]
            flat = KEEP * (block[x] + block[x + 1]) + two
            flat = flat + x0[x - 1] if x > 0 else flat
            flat = flat + x0[x + 2] if x < 14 else flat
            left = tall(flat) + around(tall(two), 1, 1)
        v = pair_mean(left, 1)
        r1[m] = v
        x1[m] = weight1[m + 1] * v
    for c in range(6):
        pair = [m for m in (2 * c - 1, 2 * c) if 0 <= m < 10]
        two = sum(x1[m] for m in pair)
        left = KEEP * sum(r1[m] for m in pair)
        beside = two + around(two, 2, 2)
        for m in (2 * c - 2, 2 * c + 1):
            beside = beside + x1[m] if 0 <= m < 10 else beside
        v = pair_mean(left + 0.25 * beside, 2)
        quads[0, c], quads[1, c] = v[:, :128], v[:, 128:]
    gy, gz = place()[1:]
    ny, nz = sizes()[1:]
    for half in range(2):
        for start, count, first in ((20, 1, 0), (0, 5, 1)):
            row, lane = iota((count, 128), 0), iota((count, 128), 1)
            y = row // 4 + gy - (1 if count == 1 else 0)
            inside = (y >= 0) & (y < ny)
            if half == 1:
                z = jnp.where(lane < 64, gz + 1, gz - 1)
                inside = inside & (z >= 0) & (z < nz)

            def rows(c):
                v = quads[half, c, pl.ds(start, count, stride=4), :] if count > 1 else quads[half, c, pl.ds(start, 1), :]
                return jnp.where(inside, v, 0.0)

            turn = lane % 4
            v = rows(1)
            for c in range(1, 4):
                v = jnp.where(turn == c, rows(c + 1), v)
            share[pl.ds(6 * half + first, count)] = v
            v = jnp.where(turn == 3, rows(0), jnp.where(turn == 0, rows(5), 0.0))
            share[pl.ds(12 + 6 * half + first, count)] = v


def join_z_kernel(final, own, low, above, below, first, last, small):
    share, state = low[16:40], low[40:48]
    lane = iota((6, 128), 1)
    for s in (0, 12):
        main, side = pl.ds(16 + s, 6), pl.ds(22 + s, 6)
        v = share[s:s + 6] + jnp.where(lane >= 124, above[side], 0.0) + jnp.where(lane < 4, below[side], 0.0)
        small[pl.ds(s, 6)] = v
        v = share[s + 6:s + 12] + jnp.where(lane < 32, above[main], jnp.where(lane >= 96, below[main], 0.0))
        small[pl.ds(s + 6, 6)] = v
    row = iota((8, 128), 0)
    if final:
        sums = [state[j:j + 1] + state[j + 1:j + 2] + above[41 + j:42 + j] + below[40 + j:41 + j] for j in (0, 2, 4)]
    else:
        sums = [state[0:1], above[40:41]]
    v = jnp.zeros((8, 128), F32)
    for j, part in enumerate(sums):
        v = jnp.where(row == j, part, v)
    small[24:32] = v
    for k in range(5):
        first[pl.ds(16 * k, 16)] = own[k]
        last[pl.ds(16 * k, 16)] = own[11 + k]
    for ref in (first, last):
        ref[80:96] = above[:16]
        ref[96:112] = below[:16]
        ref[112:144] = small[...]


def join_x_kernel(final, own, above, below, small, sums, before, after, across, body, upper, lower, ahead, behind, stage):
    for k in range(16):
        body[pl.ds(16 * k, 16)] = own[k]
    body[256:272] = above[:16]
    body[272:288] = below[:16]
    body[288:400] = before[:112]
    body[400:512] = after[:112]
    pack_rows_kernel(body, upper, lower)
    gx = place()[0]
    for k, rows in enumerate((small[:24], after[112:136], across[:24], before[112:136])):
        stage[lax.rem(gx + k, 4)] = rows
    turn = iota((12, 128), 1) % 4
    for b in range(4):
        v = stage[b, :12]
        if b < 3:
            v = v + jnp.where(turn == 3, stage[b + 1, 12:], 0.0)
        if b > 0:
            v = v + jnp.where(turn == 0, stage[b - 1, 12:], 0.0)
        for ref in (upper, lower):
            ref[pl.ds(160 + 12 * b, 12)] = v
        for half in range(2):
            ahead[pl.ds(6 * b + 3 * half, 3)] = v[6 * half:6 * half + 3]
            behind[pl.ds(6 * b + 3 * half, 3)] = v[6 * half + 3:6 * half + 6]
    state = sums[...]
    if final:
        state = (state + before[136:144]) + (after[136:144] + across[24:32])
    for ref, start in ((upper, 208), (lower, 208), (ahead, 24), (behind, 24)):
        ref[pl.ds(start, 8)] = state


def unfold(v, c):
    turn = iota(v.shape, 1) % 4
    slab = roll(v, -c, 1)
    for j in range(1, 4):
        slab = jnp.where(turn == j, roll(v, j - c, 1), slab)
    return slab


def assemble_shares(own, up1, down1, up2, down2, out, change):
    def zeros(n):
        return jnp.zeros((n, 128), F32)

    for k in range(4):
        halves = []
        for half in range(2):
            s, t = 160 + 12 * k + 6 * half, 6 * k + 3 * half
            v = jnp.concatenate([own[s + 1:s + 6], zeros(10), own[s:s + 1]], axis=0)
            v = v + jnp.concatenate([zeros(3), up1[s:s + 6], zeros(7)], axis=0)
            v = v + jnp.concatenate([zeros(7), up2[t:t + 3], zeros(6)], axis=0)
            v = v + jnp.concatenate([down1[s + 5:s + 6], zeros(10), down1[s:s + 5]], axis=0)
            v = v + jnp.concatenate([zeros(10), down2[t:t + 3], zeros(3)], axis=0)
            halves.append(v)
        out[k] = change(k, jnp.concatenate(halves, axis=1))


def assemble_coarse(gather, t, out, change):
    gy, ny = place()[1], sizes()[1]
    for k in range(4):
        own, up1, up2, down2, down1 = [ny * k + lax.rem(gy + d + ny, ny) for d in (0, 1, 2, -2, -1)]
        v = jnp.concatenate(
            [
                jnp.concatenate([
                    gather[own, t, s:s + 4], gather[up1, t, s:s + 4], gather[up2, t, s:s + 2],
                    gather[down2, t, s + 2:s + 4], gather[down1, t, s:s + 4],
                ], axis=0)
                for s in (0, 4)
            ],
            axis=1,
        )
        out[k] = change(k, v)


def up_sweep(assemble, weight2, weight1, weight0, x0, x1, kap, u, w, a, b, rhs2, spread, middle, t1, t0):
    zero = jnp.zeros((16, 256), F32)
    for ref in (a, b):
        ref[0] = zero
        ref[5] = zero
    assemble(rhs2, lambda g, v: weight2[g] * v)
    for g in range(4):
        a[g + 1] = rhs2[g]
    turn = iota((16, 256), 1) % 4
    for sweep in range(COARSE_SWEEPS - 1):
        old, new = (a, b) if sweep % 2 == 0 else (b, a)
        ahead = [None] + [roll(old[g], -4, 1) for g in range(1, 5)] + [None]
        back = [None] + [roll(old[g], 4, 1) for g in range(1, 5)] + [None]
        for g in range(1, 5):
            v = old[g]
            up = roll(jnp.where(turn == 3, zero if g == 1 else ahead[g - 1], v), 1, 1)
            down = roll(jnp.where(turn == 0, zero if g == 4 else back[g + 1], v), -1, 1)
            beside = (up + down) + (ahead[g] + back[g]) + (roll(v, 1, 0) + roll(v, -1, 0))
            new[g] = (KEEP * v + rhs2[g - 1]) + weight2[g - 1] * (0.0625 * beside)
    last = b if COARSE_SWEEPS % 2 == 0 else a
    gx = place()[0]
    half = iota((8, 256), 0) < 4
    for c in range(6):
        g, t = (gx, 3) if c == 0 else ((gx + 2, 0) if c == 5 else (gx + 1, c - 1))
        v = unfold(last[g], t)
        spread[c] = jnp.concatenate(
            [
                jnp.where(half, jnp.broadcast_to(v[j:j + 1], (8, 256)), jnp.broadcast_to(v[k:k + 1], (8, 256)))
                for j, k in ((0, 1), (2, 3), (4, 15))
            ],
            axis=0,
        )
    for m in range(MIDS):
        t1[m] = x1[m] + spread[m // 2]
    for m in range(1, MIDS - 1):
        v = t1[m]
        beside = (t1[m - 1] + t1[m + 1]) + around(v, 2, 2)
        middle[m] = (KEEP * v + x1[m]) + weight1[m] * (0.25 * beside)
    for i in range(3, SLABS - 3):
        t0[i] = x0[i] + middle[(i - 1) // 2]
    for i in range(4, SLABS - 4):
        v = t0[i]
        beside = (t0[i - 1] + t0[i + 1]) + around(v, 1, 1)
        u[i] = (KEEP * v + x0[i]) + weight0[i] * beside
    for i in range(5, SLABS - 5):
        v = u[i]
        beside = (u[i - 1] + u[i + 1]) + around(v, 1, 1)
        w[i - 5] = (kap[i - 5] + 6.0) * v[:16, :128] - beside[:16, :128]


def lanes_of(values):
    rows = [jnp.sum(v, axis=0, keepdims=True) for v in values]
    sums = jnp.sum(jnp.concatenate(rows + [jnp.zeros((16 - len(rows), 128), F32)], axis=0), axis=1, keepdims=True)
    picked = jnp.where(iota((16, 128), 1) == MARK + iota((16, 128), 0), sums, 0.0)
    return jnp.broadcast_to(jnp.sum(picked, axis=0, keepdims=True), (8, 128))


def write_ends(w, weight0, weight1, low, high, *scratch):
    pack_near(lambda k: w[k], low.at[pl.ds(0, 16)], high.at[pl.ds(0, 16)])
    share_sweep(w, weight0, weight1, low.at[pl.ds(16, 24)], *scratch)
    high[16:40] = low[16:40]


def wide(row, k):
    return jnp.broadcast_to(row[:, MARK + k:MARK + k + 1], (16, 128))


def first_up_kernel(gather, own0, halo0s, own1, halo1, x0, x1, both, weight2, u, w, low, high, *scratch):
    (*scratch, full, y0, y1, z1, quads) = scratch
    weight0, weight1 = Joined(own0, halo0s), Joined(own1, halo1)
    row, lane = iota((16, 256), 0), iota((16, 256), 1)
    y = jnp.where(row < 10, row, row - 16) + 4 * place()[1]
    inside = inside_lanes(lane) & (y >= 0) & (y < 4 * sizes()[1])
    assemble_coarse(gather, 1, weight2, lambda s, v: jnp.where(inside, v, 0.0))
    up_sweep(lambda *a: assemble_coarse(gather, 0, *a), weight2, weight1, weight0, x0, x1, both.at[1], full, w, *scratch)
    rz = curve = jnp.zeros((16, 128), F32)
    for k in range(16):
        v = full[k + 5][:16, :128]
        u[k] = v
        rz = rz + both[0, k] * v
        curve = curve + w[k] * v
    write_ends(w, weight0, weight1, low, high, y0, y1, z1, quads)
    low[40:48] = high[40:48] = lanes_of([rz, curve])


def near_kernel(body, up1, down1, own0, halo0, own1, halo1, x0, x1, r, tall, sides):
    weight0, weight1 = Joined(own0, halo0), Joined(own1, halo1)
    here, there = units(body, 0, 32), unpack_rows(up1, down1, 0, sides)
    near_sweep(lambda i: assemble_fine(here, there, i, near_sources), weight0, weight1, x0, x1, None, r, tall)


def second_kernel(x0, x1, own, up1, down1, up2, down2, weight2, own0, halo0s, own1, halo1, both,
                  m0, n0, low, high, *scratch):
    weight0s, weight1 = Joined(own0, halo0s), Joined(own1, halo1)
    (full, *scratch, y0, y1, z1, quads) = scratch
    shares = (own, up1, down1, up2, down2)
    up_sweep(lambda *a: assemble_shares(*shares, *a), weight2, weight1, weight0s, x0, x1, both.at[1], full, n0, *scratch)
    for k in range(16):
        m0[k] = full[k + 5, :16, :128]
    write_ends(n0, weight0s, weight1, low, high, y0, y1, z1, quads)
    ahead, behind = up1[208:210] + up2[24:26], down1[208:210] + own[208:210]
    for ref in (low, high):
        ref[40:42] = ahead + behind
        ref[42:44] = ahead
        ref[44:46] = behind
        ref[46:48] = jnp.zeros((2, 128), F32)


def third_kernel(x0, x1, own, up1, down1, up2, down2, weight2, own0, halo0s, own1, halo1, both, u0, w0, m0, n0,
                 r1, u1, w1, m1, n1, first, dots, full, last, *scratch):
    weight0s, weight1 = Joined(own0, halo0s), Joined(own1, halo1)
    shares = (own, up1, down1, up2, down2)
    up_sweep(lambda *a: assemble_shares(*shares, *a), weight2, weight1, weight0s, x0, x1, both.at[1], full, last, *scratch)
    total0 = own[208:209] + up2[25:26] + down2[26:27]
    first[...] = jnp.broadcast_to(total0, (8, 128))
    alpha = wide(total0, 0) / wide(total0, 1)
    sums = [jnp.zeros((16, 128), F32)] * 12
    for k in range(16):
        vw0, vm0, vn0 = w0[k], m0[k], n0[k]
        vr1 = both[0, k] - alpha * vw0
        vu1 = u0[k] - alpha * vm0
        vw1 = vw0 - alpha * vn0
        vm1 = vm0 - alpha * full[k + 5, :16, :128]
        vn1 = vn0 - alpha * last[k]
        r1[k], u1[k], w1[k], m1[k], n1[k] = vr1, vu1, vw1, vm1, vn1
        terms = [vr1 * vu1, vr1 * vm1, vr1 * vm0, vw1 * vu1, vw1 * vm1, vw1 * vm0,
                 vw0 * vu1, vw0 * vm1, vw0 * vm0, vn1 * vm1, vn1 * vm0, vn0 * vm0]
        sums = [s + t for s, t in zip(sums, terms)]
    dots[...] = lanes_of(sums)


def finish_kernel(first, second, u0, w0, m0, n0, r1, u1, w1, m1, n1, field_out, residual_out, field, residual, sems):
    g0, d0 = [wide(first[0:1], k) for k in range(2)]
    (r1u1, r1m1, r1m0, w1u1, w1m1, w1m0, w0u1, w0m1, w0m0, n1m1, n1m0, n0m0) = [wide(second[0:1], k) for k in range(12)]
    alpha0 = g0 / d0
    beta1 = r1u1 / g0
    curve1 = w1u1 + 2.0 * beta1 * w0u1 + beta1 * beta1 * d0
    alpha1 = r1u1 / curve1
    ab = alpha1 * beta1
    su = w1u1 + beta1 * w0u1 - alpha1 * (w1m1 + beta1 * w0m1) - ab * (w1m0 + beta1 * w0m0)
    g2 = (r1u1 - alpha1 * r1m1 - ab * r1m0) - alpha1 * su
    beta2 = g2 / r1u1
    uw = (w1u1 - 2.0 * alpha1 * w1m1 - 2.0 * ab * w1m0) + (alpha1 * alpha1 * n1m1 + 2.0 * alpha1 * ab * n1m0 + ab * ab * n0m0)
    curve2 = uw + 2.0 * beta2 * su + beta2 * beta2 * curve1
    alpha2 = g2 / curve2
    mix = alpha1 + alpha2 * beta2
    cu0, cu1, cm1, cm0 = alpha0 + mix * beta1, mix + alpha2, alpha2 * alpha1, alpha2 * ab
    cw0 = mix * beta1
    copies = []
    for k in range(16):
        field[k] = (cu0 * u0[k] + cu1 * u1[k]) - (cm1 * m1[k] + cm0 * m0[k])
        residual[k] = r1[k] - (cw0 * w0[k] + cu1 * w1[k]) + (cm1 * n1[k] + cm0 * n0[k])
        if k % 4 == 3:
            part = pl.ds(k - 3, 4)
            copies.append(pltpu.make_async_copy(field.at[part], field_out.at[part], sems.at[0, k // 4]))
            copies.append(pltpu.make_async_copy(residual.at[part], residual_out.at[part], sems.at[1, k // 4]))
            copies[-2].start()
            copies[-1].start()
    for copy in copies:
        copy.wait()


def shape(*dims):
    return jax.ShapeDtypeStruct(dims, F32)


def call(kernel, outs, scratch=(), specs=None, count=0, grant=40, flops=0, out=VMEM):
    return pl.pallas_call(
        kernel,
        out_shape=outs,
        in_specs=specs or [VMEM] * count,
        out_specs=[out] * len(outs),
        scratch_shapes=list(scratch),
        compiler_params=pltpu.CompilerParams(vmem_limit_bytes=grant * 1024 * 1024),
        cost_estimate=pl.CostEstimate(flops=flops, bytes_accessed=flops, transcendentals=0) if flops else None,
    )


def shift(v, axis, distance):
    count = lax.axis_size(axis)
    return lax.ppermute(v, axis, [((i + distance) % count, i) for i in range(count)])


def fine_exchange(own, low, high):
    above, below = shift(low, "gz", 1), shift(high, "gz", -1)
    first = jnp.concatenate([own[:, :5], above[:, 4:5], below[:, 4:5]], axis=1)
    last = jnp.concatenate([own[:, 11:], above[:, 5:6], below[:, 5:6]], axis=1)
    before, after = shift(last, "gx", -1), shift(first, "gx", 1)
    body = jnp.concatenate([own, above[:, :4], below[:, :4], before, after, own[:, :2]], axis=1).reshape(-1, 128)
    upper, lower = call(pack_rows_kernel, [shape(10 * UNITS, 128)] * 2, count=1)(body)
    return body, shift(upper, "gy", 1), shift(lower, "gy", -1)


def joint_exchange(own, low, high, final):
    above, below = shift(low, "gz", 1), shift(high, "gz", -1)
    first, last, small = call(
        functools.partial(join_z_kernel, final), [shape(144, 128), shape(144, 128), shape(32, 128)], count=4
    )(own, low, above, below)
    before, after, across = shift(last, "gx", -1), shift(first, "gx", 1), shift(small, "gx", 2)
    state = small[24:] if final else small[24:] + shift(small[24:], "gz", 4)
    body, upper, lower, ahead, behind = call(
        functools.partial(join_x_kernel, final), [shape(512, 128), shape(216, 128), shape(216, 128), shape(32, 128), shape(32, 128)],
        [pltpu.VMEM((4, 24, 128), F32)], count=8,
    )(own, above, below, small, state, before, after, across)
    return body, upper, shift(upper, "gy", 1), shift(lower, "gy", -1), shift(ahead, "gy", 2), shift(behind, "gy", -2)


def gather(unit):
    count = lax.axis_size("gx") * lax.axis_size("gy")
    return lax.all_to_all(jnp.broadcast_to(unit[None], (count,) + unit.shape), ("gx", "gy"), 0, 0, tiled=True)


def total(v):
    axes = ("gx", "gy", "gz")
    count = lax.axis_size("gx") * lax.axis_size("gy") * lax.axis_size("gz")
    parts = lax.all_to_all(jnp.broadcast_to(v[None, :1], (count, 1, 128)), axes, 0, 0, tiled=True)
    return jnp.broadcast_to(parts.sum(0), (8, 128))


def local(right_side, classes, table):
    def scratch(*shapes):
        return [pltpu.VMEM(s, F32) for s in shapes]

    block, short, mids, tile = shape(*BLOCK), shape(*SHORT), shape(*MID), shape(8, 128)
    up_scratch = scratch((6, 16, 256), (6, 16, 256), (4, 16, 256), (6, 24, 256), MID, MID, SHORT, SHORT)

    both, low, high = call(
        prepare_kernel, [shape(2, *BLOCK), shape(2, 6, 16, 128), shape(2, 6, 16, 128)],
        [pltpu.VMEM(BLOCK, jnp.int32), pltpu.SMEM((CLASSES,), F32), pltpu.SemaphoreType.DMA((3,))], specs=[ANY] * 3, grant=60,
    )(right_side, classes, table)
    halos = fine_exchange(both, low, high)
    own0, own1, unit2 = call(
        own_weights_kernel, [shape(SLABS, 16, 256), shape(MIDS, 16, 256), tile],
        scratch((MIDS, 16, 256), (2, 4, 16, 128)), count=1, flops=4_000_000,
    )(halos[0])
    halo0, halo0s, halo1, x0, x1, unit = call(
        first_down_kernel, [shape(SLABS, 16, 256), shape(SLABS, 8, 256), shape(MIDS, 8, 256), short, mids, tile],
        scratch(SHORT, HALO, MID, (2, 4, 16, 128), (16 * UNITS, 128)), count=5,
    )(*halos, own0, own1)
    ends = [shape(48, 128), shape(48, 128)]
    share_scratch = scratch(BLOCK, (10, 24, 256), (10, 24, 256), (2, 6, 24, 128))
    weight2, u0, w0, low, high = call(
        first_up_kernel, [shape(4, 16, 256), block, block, *ends], up_scratch + share_scratch, count=8
    )(gather(jnp.stack([unit, unit2])), own0, halo0s, own1, halo1, x0, x1, both)

    def near(body, up1, down1):
        return call(near_kernel, [short, mids], scratch(SHORT, HALO, (512, 128)), count=7, flops=4_000_000)(
            body, up1, down1, own0, halo0, own1, halo1
        )

    body, own, up1, down1, up2, down2 = joint_exchange(w0, low, high, False)
    x0, x1 = near(body, up1, down1)
    m0, n0, low, high = call(
        second_kernel, [block, block, *ends], scratch(SHORT) + up_scratch[:-1] + share_scratch, count=13
    )(x0, x1, own, up1, down1, up2, down2, weight2, own0, halo0s, own1, halo1, both)
    body, own, up1, down1, up2, down2 = joint_exchange(n0, low, high, True)
    x0, x1 = near(body, up1, down1)
    r1, u1, w1, m1, n1, first, dots = call(
        third_kernel, [block] * 5 + [tile, tile], scratch(SHORT, BLOCK) + up_scratch[:-1], count=17
    )(x0, x1, own, up1, down1, up2, down2, weight2, own0, halo0s, own1, halo1, both, u0, w0, m0, n0)
    field, residual = call(
        finish_kernel, [block] * 2, scratch(BLOCK, BLOCK) + [pltpu.SemaphoreType.DMA((2, 4))], count=11, out=ANY
    )(
        first, total(dots), u0, w0, m0, n0, r1, u1, w1, m1, n1
    )
    return field, residual


def solution(mesh):
    in_specs = (P("gx", "gy", "gz"), P("gx", "gy", "gz"), P())
    out_specs = (P("gx", "gy", "gz"), P("gx", "gy", "gz"))
    return jax.shard_map(local, mesh=mesh, in_specs=in_specs, out_specs=out_specs, check_vma=False)
```

```python
import functools

import jax
import jax.numpy as jnp
from jax import lax
from jax.experimental import pallas as pl
from jax.experimental.pallas import tpu as pltpu
from jax.sharding import PartitionSpec as P

CLASSES = 16
COARSE_SWEEPS = 6
OMEGA = 0.8
KEEP = 1.0 - OMEGA
F32 = jnp.float32
SLABS, MIDS, UNITS = 26, 12, 40
MARK = 64
BLOCK, HALO, SHORT, MID = (16, 16, 128), (SLABS, 32, 256), (SLABS, 24, 256), (MIDS, 24, 256)
VMEM = pl.BlockSpec(memory_space=pltpu.VMEM)
ANY = pl.BlockSpec(memory_space=pl.ANY)


def iota(shape, dim):
    return lax.broadcasted_iota(jnp.int32, shape, dim)


def roll(v, shift, axis):
    shift = shift % v.shape[axis]
    return v if shift == 0 else pltpu.roll(v, shift, axis)


def around(v, rows, lanes):
    return (roll(v, rows, 0) + roll(v, -rows, 0)) + (roll(v, lanes, 1) + roll(v, -lanes, 1))


def pair_mean(v, step):
    rows = (iota(v.shape, 0) // step) % 2 == 0
    v = v + jnp.where(rows, roll(v, -step, 0), roll(v, step, 0))
    lanes = (iota(v.shape, 1) // step) % 2 == 0
    v = v + jnp.where(lanes, roll(v, -step, 1), roll(v, step, 1))
    return v * 0.125


def place():
    return tuple(lax.axis_index(axis) for axis in ("gx", "gy", "gz"))


def sizes():
    return tuple(lax.axis_size(axis) for axis in ("gx", "gy", "gz"))


def pack_fine(read, low_ref, high_ref):
    lane = iota((16, 128), 1)
    chunk = lane // 32
    for g in range(4):
        low = high = None
        for j in range(4):
            v = read(4 * g + j)
            first, last = roll(v, 32 * j, 1), roll(v, 32 * j + 32, 1)
            low = first if j == 0 else jnp.where(chunk == j, first, low)
            high = last if j == 0 else jnp.where(chunk == j, last, high)
        low_ref[g] = low
        high_ref[g] = high
    for g, slabs in ((4, (0, 1, 2, 3, 4)), (5, (15, 14, 13, 12, 11))):
        low, high = read(slabs[0]), roll(read(slabs[0]), 32, 1)
        for j in range(1, 5):
            v, here = read(slabs[j]), (lane >= 112 if j == 4 else chunk == j)
            low = jnp.where(here, roll(v, 112 if j == 4 else 32 * j, 1), low)
            high = jnp.where(here, roll(v, (32, 64, 96, 112, 0)[j], 1), high)
        low_ref[g] = low
        high_ref[g] = high


def pack_near(read, low_ref, high_ref):
    chunk = iota((16, 128), 1) // 8
    low = high = None
    for k in range(16):
        v = read(k)
        first, last = roll(v, 8 * k, 1), roll(v, 8 * k + 8, 1)
        low = first if k == 0 else jnp.where(chunk == k, first, low)
        high = last if k == 0 else jnp.where(chunk == k, last, high)
    low_ref[...] = low
    high_ref[...] = high


def prepare_kernel(rhs_in, classes_in, table_in, both, low, high, classes, table, sems):
    copies = [
        pltpu.make_async_copy(rhs_in, both.at[0], sems.at[0]),
        pltpu.make_async_copy(classes_in, classes, sems.at[1]),
        pltpu.make_async_copy(table_in, table, sems.at[2]),
    ]
    for copy in copies:
        copy.start()
    for copy in copies:
        copy.wait()
    for k in range(16):
        c = classes[k]
        v = jnp.zeros((16, 128), F32)
        for index in range(CLASSES):
            v = jnp.where(c == index, table[index], v)
        both[1, k] = v
    for t in range(2):
        pack_fine(lambda k, t=t: both[t, k], low.at[t], high.at[t])


def slab_sources(i):
    x = i - 5
    if 0 <= x < 16:
        return x, 16 + x // 4, 20 + x // 4, -32 * (x % 4), 96 - 32 * (x % 4)
    base, far = (24, -1 - x) if x < 0 else (31, x - 16)
    return base + (x + 5 if x < 0 else far), base + 5, base + 6, (0, -32, -64, -96, -112)[far], (96, 64, 32, 16, 0)[far]


def near_sources(i):
    x = i - 5
    base, above, k = (x, 16, x) if 0 <= x < 16 else ((23 + x, 23, 16 + x) if x < 0 else (x + 9, 30, x - 16))
    return base, above, above + 1, -8 * k, 120 - 8 * k


def assemble_half(refs, i, sources):
    main, above, below, up, down = sources(i)
    lane = iota((16, 128), 1)
    side = jnp.where(lane < 64, roll(refs[above][...], up, 1), roll(refs[below][...], down, 1))
    return jnp.concatenate([refs[main][...], side], axis=1)


def assemble_fine(body, sides, i, sources=slab_sources):
    return jnp.concatenate([assemble_half(body, i, sources), assemble_half(sides, i, sources)], axis=0)


class Joined:
    def __init__(self, top, bottom):
        self.top, self.bottom = top, bottom

    def __getitem__(self, i):
        return jnp.concatenate([self.top[i], self.bottom[i]], axis=0)


def pack_rows_kernel(body, upper, lower):
    for g in range(body.shape[0] // 128):
        for t in range(5):
            here = pl.ds(8 * (5 * g + t), 8)
            upper[here] = body[pl.ds(128 * g + t, 8, stride=16), :]
            lower[here] = body[pl.ds(128 * g + 11 + t, 8, stride=16), :]


def units(body, first, count):
    return [body.at[pl.ds(first + 16 * u, 16)] for u in range(count)]


def unpack_rows(upper, lower, first, sides):
    sides[...] = jnp.zeros(sides.shape, F32)
    for g in range(sides.shape[0] // 128):
        for t in range(5):
            here = pl.ds(8 * (first + 5 * g + t), 8)
            sides[pl.ds(128 * g + t, 8, stride=16), :] = upper[here]
            sides[pl.ds(128 * g + 11 + t, 8, stride=16), :] = lower[here]
    return units(sides, 0, sides.shape[0] // 16)


def squeeze(v):
    return jnp.concatenate([v[:16], jnp.where(iota((8, v.shape[1]), 0) < 4, v[16:24], v[24:])], axis=0)


def near(lane):
    return (lane < 160) | (lane >= 224)


def inside_lanes(lane):
    z = jnp.where(lane < 192, lane, lane - 256) + 128 * place()[2]
    return near(lane) & (z >= 0) & (z < 128 * sizes()[2])


def squeeze_half(v):
    return jnp.where(iota((8, v.shape[1]), 0) < 4, v[:8], v[8:])


def weigh(kap, extra, i, shift, cells, inside):
    x = cells * place()[0] + (i - shift)
    return jnp.where(inside & (x >= 0) & (x < cells * sizes()[0]), OMEGA / (kap + extra), 0.0)


def first_join_kernel(own, above, below, first, last, core, upper, lower):
    for t in range(2):
        for k in range(5):
            first[t, k] = own[t, k]
            last[t, k] = own[t, 11 + k]
        for ref, pack in ((first, 4), (last, 5)):
            ref[t, 5] = above[t, pack]
            ref[t, 6] = below[t, pack]
        for k in range(24):
            source = own[t, k] if k < 16 else (above[t, k - 16] if k < 20 else below[t, k - 20])
            core[pl.ds(16 * (24 * t + k), 16)] = source
    pack_rows_kernel(core, upper, lower)


def two_parts(core, rim, t):
    return units(core, 24 * 16 * t, 24) + units(rim, 16 * 16 * t, 16)


def two_sides(core_upper, core_lower, rim_upper, rim_lower, t, sides):
    there = unpack_rows(core_upper, core_lower, 15 * t, sides.at[pl.ds(0, 384)])
    return there + unpack_rows(rim_upper, rim_lower, 10 * t, sides.at[pl.ds(384, 256)])


def own_weights_kernel(core, rim, weight0, weight1, unit, middle, quads):
    here = two_parts(core, rim, 1)
    inside = inside_lanes(iota((16, 256), 1))
    for m in range(-1, MIDS + 1):
        pair = []
        for i in (2 * m + 1, 2 * m + 2):
            if 0 <= i < SLABS:
                kap = assemble_half(here, i, slab_sources)
                weight0[i] = weigh(kap, 6.0, i, 5, 16, inside)
                pair.append(kap)
        if 0 <= m < MIDS:
            kap1 = pair_mean(pair[0] + pair[1], 1)
            middle[m] = kap1
            weight1[m] = weigh(kap1, 1.5, m, 2, 8, inside)
    for c in range(4):
        weight2 = OMEGA / (pair_mean(middle[2 + 2 * c] + middle[3 + 2 * c], 2) + 0.375)
        quads[0, c], quads[1, c] = weight2[:, :128], weight2[:, 128:]
    pack_coarse(quads, unit)


def halo_weights(there, weight0, weight0s, weight1):
    row, lane = iota((16, 256), 0), iota((16, 256), 1)
    y = jnp.where(row < 8, row + 16, row - 16) + 16 * place()[1]
    inside = inside_lanes(lane) & (y >= 0) & (y < 16 * sizes()[1])
    y = jnp.where(iota((8, 256), 0) < 4, 1, -1) + place()[1]
    insides = inside_lanes(iota((8, 256), 1)) & (y >= 0) & (y < sizes()[1])
    for m in range(-1, MIDS + 1):
        pair = []
        for i in (2 * m + 1, 2 * m + 2):
            if 0 <= i < SLABS:
                kap = assemble_half(there, i, slab_sources)
                v = weigh(kap, 6.0, i, 5, 16, inside)
                weight0[i] = v
                weight0s[i] = squeeze_half(v)
                pair.append(squeeze_half(kap))
        if 0 <= m < MIDS:
            weight1[m] = weigh(pair_mean(pair[0] + pair[1], 1), 1.5, m, 2, 8, insides)


def pack_coarse(quads, unit):
    turn = iota((4, 128), 1) % 4
    for half in range(2):
        v = quads[half, 0, pl.ds(0, 4, stride=4), :]
        for c in range(1, 4):
            v = jnp.where(turn == c, quads[half, c, pl.ds(0, 4, stride=4), :], v)
        unit[4 * half:4 * half + 4] = v


def near_sweep(read, weight0, weight1, x0, x1, r1, r, tall):
    for i in range(SLABS):
        v = read(i)
        r[i] = squeeze(v)
        v = weight0[i] * v
        tall[i] = v
        x0[i] = squeeze(v)
    def middle_slab(m, carry):
        i = 2 * m + 1
        two = tall[i] + tall[i + 1]
        rows = squeeze(roll(two, 1, 0) + roll(two, -1, 0))
        two = x0[i] + x0[i + 1]
        lanes = roll(two, 1, 1) + roll(two, -1, 1)
        v = pair_mean(KEEP * (r[i] + r[i + 1]) + ((x0[i - 1] + x0[i + 2]) + two) + (rows + lanes), 1)
        if r1 is not None:
            r1[m] = v
        x1[m] = weight1[m] * v
        return carry

    lax.fori_loop(0, MIDS, middle_slab, 0, unroll=4)


def first_down_kernel(core, rim, core_upper, core_lower, rim_upper, rim_lower, own0, own1, halo0, halo0s, halo1, x0, x1, unit, r, tall, r1, quads, sides):
    rows = (core_upper, core_lower, rim_upper, rim_lower)
    halo_weights(two_sides(*rows, 1, sides), halo0, halo0s, halo1)
    here, there = two_parts(core, rim, 0), two_sides(*rows, 0, sides)
    weight0, weight1 = Joined(own0, halo0), Joined(own1, halo1)
    near_sweep(lambda i: assemble_fine(here, there, i), weight0, weight1, x0, x1, r1, r, tall)
    for c in range(4):
        m = 2 + 2 * c
        two = x1[m] + x1[m + 1]
        left = KEEP * (r1[m] + r1[m + 1]) + 0.25 * (((x1[m - 1] + x1[m + 2]) + two) + around(two, 2, 2))
        v = pair_mean(left, 2)[:16]
        quads[0, c], quads[1, c] = v[:, :128], v[:, 128:]
    pack_coarse(quads, unit)


def share_sweep(block, weight0, weight1, share, x0, r1, x1, quads):
    for k in range(16):
        x0[k] = weight0.top[k + 5, :, :128] * block[k]
    zero, low = jnp.zeros((16, 128), F32), jnp.zeros((8, 256), F32)

    def tall(v):
        return jnp.concatenate([jnp.concatenate([v, zero], axis=1), low], axis=0)

    for m in range(10):
        x = 2 * (m - 1)
        if m == 0:
            left = tall(x0[0])
        elif m == 9:
            left = tall(x0[15])
        else:
            two = x0[x] + x0[x + 1]
            flat = KEEP * (block[x] + block[x + 1]) + two
            flat = flat + x0[x - 1] if x > 0 else flat
            flat = flat + x0[x + 2] if x < 14 else flat
            left = tall(flat) + around(tall(two), 1, 1)
        v = pair_mean(left, 1)
        r1[m] = v
        x1[m] = weight1[m + 1] * v
    for c in range(6):
        pair = [m for m in (2 * c - 1, 2 * c) if 0 <= m < 10]
        two = sum(x1[m] for m in pair)
        left = KEEP * sum(r1[m] for m in pair)
        beside = two + around(two, 2, 2)
        for m in (2 * c - 2, 2 * c + 1):
            beside = beside + x1[m] if 0 <= m < 10 else beside
        v = pair_mean(left + 0.25 * beside, 2)
        quads[0, c], quads[1, c] = v[:, :128], v[:, 128:]
    gy, gz = place()[1:]
    ny, nz = sizes()[1:]
    for half in range(2):
        for start, count, first in ((20, 1, 0), (0, 5, 1)):
            row, lane = iota((count, 128), 0), iota((count, 128), 1)
            y = row // 4 + gy - (1 if count == 1 else 0)
            inside = (y >= 0) & (y < ny)
            if half == 1:
                z = jnp.where(lane < 64, gz + 1, gz - 1)
                inside = inside & (z >= 0) & (z < nz)

            def rows(c):
                v = quads[half, c, pl.ds(start, count, stride=4), :] if count > 1 else quads[half, c, pl.ds(start, 1), :]
                return jnp.where(inside, v, 0.0)

            turn = lane % 4
            v = rows(1)
            for c in range(1, 4):
                v = jnp.where(turn == c, rows(c + 1), v)
            share[pl.ds(6 * half + first, count)] = v
            v = jnp.where(turn == 3, rows(0), jnp.where(turn == 0, rows(5), 0.0))
            share[pl.ds(12 + 6 * half + first, count)] = v


def join_z_kernel(final, own, low, above, below, first, last, small):
    share, state = low[16:40], low[40:48]
    lane = iota((6, 128), 1)
    for s in (0, 12):
        main, side = pl.ds(16 + s, 6), pl.ds(22 + s, 6)
        v = share[s:s + 6] + jnp.where(lane >= 124, above[side], 0.0) + jnp.where(lane < 4, below[side], 0.0)
        small[pl.ds(s, 6)] = v
        v = share[s + 6:s + 12] + jnp.where(lane < 32, above[main], jnp.where(lane >= 96, below[main], 0.0))
        small[pl.ds(s + 6, 6)] = v
    row = iota((8, 128), 0)
    if final:
        sums = [state[j:j + 1] + state[j + 1:j + 2] + above[41 + j:42 + j] + below[40 + j:41 + j] for j in (0, 2, 4)]
    else:
        sums = [state[0:1], above[40:41]]
    v = jnp.zeros((8, 128), F32)
    for j, part in enumerate(sums):
        v = jnp.where(row == j, part, v)
    small[24:32] = v
    for k in range(5):
        first[pl.ds(16 * k, 16)] = own[k]
        last[pl.ds(16 * k, 16)] = own[11 + k]
    for ref in (first, last):
        ref[80:96] = above[:16]
        ref[96:112] = below[:16]
        ref[112:144] = small[...]


def join_x_kernel(final, own, above, below, small, sums, before, after, across, body, upper, lower, ahead, behind, stage):
    for k in range(16):
        body[pl.ds(16 * k, 16)] = own[k]
    body[256:272] = above[:16]
    body[272:288] = below[:16]
    body[288:400] = before[:112]
    body[400:512] = after[:112]
    pack_rows_kernel(body, upper, lower)
    gx = place()[0]
    for k, rows in enumerate((small[:24], after[112:136], across[:24], before[112:136])):
        stage[lax.rem(gx + k, 4)] = rows
    turn = iota((12, 128), 1) % 4
    for b in range(4):
        v = stage[b, :12]
        if b < 3:
            v = v + jnp.where(turn == 3, stage[b + 1, 12:], 0.0)
        if b > 0:
            v = v + jnp.where(turn == 0, stage[b - 1, 12:], 0.0)
        for ref in (upper, lower):
            ref[pl.ds(160 + 12 * b, 12)] = v
        for half in range(2):
            ahead[pl.ds(6 * b + 3 * half, 3)] = v[6 * half:6 * half + 3]
            behind[pl.ds(6 * b + 3 * half, 3)] = v[6 * half + 3:6 * half + 6]
    state = sums[...]
    if final:
        state = (state + before[136:144]) + (after[136:144] + across[24:32])
    for ref, start in ((upper, 208), (lower, 208), (ahead, 24), (behind, 24)):
        ref[pl.ds(start, 8)] = state


def unfold(v, c):
    turn = iota(v.shape, 1) % 4
    slab = roll(v, -c, 1)
    for j in range(1, 4):
        slab = jnp.where(turn == j, roll(v, j - c, 1), slab)
    return slab


def assemble_shares(own, up1, down1, up2, down2, out, change):
    def zeros(n):
        return jnp.zeros((n, 128), F32)

    for k in range(4):
        halves = []
        for half in range(2):
            s, t = 160 + 12 * k + 6 * half, 6 * k + 3 * half
            v = jnp.concatenate([own[s + 1:s + 6], zeros(10), own[s:s + 1]], axis=0)
            v = v + jnp.concatenate([zeros(3), up1[s:s + 6], zeros(7)], axis=0)
            v = v + jnp.concatenate([zeros(7), up2[t:t + 3], zeros(6)], axis=0)
            v = v + jnp.concatenate([down1[s + 5:s + 6], zeros(10), down1[s:s + 5]], axis=0)
            v = v + jnp.concatenate([zeros(10), down2[t:t + 3], zeros(3)], axis=0)
            halves.append(v)
        out[k] = change(k, jnp.concatenate(halves, axis=1))


def assemble_coarse(gather, t, out, change):
    gy, ny = place()[1], sizes()[1]
    for k in range(4):
        own, up1, up2, down2, down1 = [ny * k + lax.rem(gy + d + ny, ny) for d in (0, 1, 2, -2, -1)]
        v = jnp.concatenate(
            [
                jnp.concatenate([
                    gather[own, t, s:s + 4], gather[up1, t, s:s + 4], gather[up2, t, s:s + 2],
                    gather[down2, t, s + 2:s + 4], gather[down1, t, s:s + 4],
                ], axis=0)
                for s in (0, 4)
            ],
            axis=1,
        )
        out[k] = change(k, v)


def up_sweep(assemble, weight2, weight1, weight0, x0, x1, kap, u, w, a, b, rhs2, spread, middle, t1, t0):
    zero = jnp.zeros((16, 256), F32)
    for ref in (a, b):
        ref[0] = zero
        ref[5] = zero
    assemble(rhs2, lambda g, v: weight2[g] * v)
    for g in range(4):
        a[g + 1] = rhs2[g]
    turn = iota((16, 256), 1) % 4
    for sweep in range(COARSE_SWEEPS - 1):
        old, new = (a, b) if sweep % 2 == 0 else (b, a)
        ahead = [None] + [roll(old[g], -4, 1) for g in range(1, 5)] + [None]
        back = [None] + [roll(old[g], 4, 1) for g in range(1, 5)] + [None]
        for g in range(1, 5):
            v = old[g]
            up = roll(jnp.where(turn == 3, zero if g == 1 else ahead[g - 1], v), 1, 1)
            down = roll(jnp.where(turn == 0, zero if g == 4 else back[g + 1], v), -1, 1)
            beside = (up + down) + (ahead[g] + back[g]) + (roll(v, 1, 0) + roll(v, -1, 0))
            new[g] = (KEEP * v + rhs2[g - 1]) + weight2[g - 1] * (0.0625 * beside)
    last = b if COARSE_SWEEPS % 2 == 0 else a
    gx = place()[0]
    half = iota((8, 256), 0) < 4
    for c in range(6):
        g, t = (gx, 3) if c == 0 else ((gx + 2, 0) if c == 5 else (gx + 1, c - 1))
        v = unfold(last[g], t)
        spread[c] = jnp.concatenate(
            [
                jnp.where(half, jnp.broadcast_to(v[j:j + 1], (8, 256)), jnp.broadcast_to(v[k:k + 1], (8, 256)))
                for j, k in ((0, 1), (2, 3), (4, 15))
            ],
            axis=0,
        )
    for m in range(MIDS):
        t1[m] = x1[m] + spread[m // 2]
    for m in range(1, MIDS - 1):
        v = t1[m]
        beside = (t1[m - 1] + t1[m + 1]) + around(v, 2, 2)
        middle[m] = (KEEP * v + x1[m]) + weight1[m] * (0.25 * beside)
    for i in range(3, SLABS - 3):
        t0[i] = x0[i] + middle[(i - 1) // 2]
    for i in range(4, SLABS - 4):
        v = t0[i]
        beside = (t0[i - 1] + t0[i + 1]) + around(v, 1, 1)
        u[i] = (KEEP * v + x0[i]) + weight0[i] * beside
    for i in range(5, SLABS - 5):
        v = u[i]
        beside = (u[i - 1] + u[i + 1]) + around(v, 1, 1)
        w[i - 5] = (kap[i - 5] + 6.0) * v[:16, :128] - beside[:16, :128]


def lanes_of(values):
    rows = [jnp.sum(v, axis=0, keepdims=True) for v in values]
    sums = jnp.sum(jnp.concatenate(rows + [jnp.zeros((16 - len(rows), 128), F32)], axis=0), axis=1, keepdims=True)
    picked = jnp.where(iota((16, 128), 1) == MARK + iota((16, 128), 0), sums, 0.0)
    return jnp.broadcast_to(jnp.sum(picked, axis=0, keepdims=True), (8, 128))


def write_ends(w, weight0, weight1, low, high, *scratch):
    pack_near(lambda k: w[k], low.at[pl.ds(0, 16)], high.at[pl.ds(0, 16)])
    share_sweep(w, weight0, weight1, low.at[pl.ds(16, 24)], *scratch)
    high[16:40] = low[16:40]


def wide(row, k):
    return jnp.broadcast_to(row[:, MARK + k:MARK + k + 1], (16, 128))


def first_up_kernel(gather, own0, halo0s, own1, halo1, x0, x1, both, weight2, u, w, low, high, *scratch):
    (*scratch, full, y0, y1, z1, quads) = scratch
    weight0, weight1 = Joined(own0, halo0s), Joined(own1, halo1)
    row, lane = iota((16, 256), 0), iota((16, 256), 1)
    y = jnp.where(row < 10, row, row - 16) + 4 * place()[1]
    inside = inside_lanes(lane) & (y >= 0) & (y < 4 * sizes()[1])
    assemble_coarse(gather, 1, weight2, lambda s, v: jnp.where(inside, v, 0.0))
    up_sweep(lambda *a: assemble_coarse(gather, 0, *a), weight2, weight1, weight0, x0, x1, both.at[1], full, w, *scratch)
    rz = curve = jnp.zeros((16, 128), F32)
    for k in range(16):
        v = full[k + 5][:16, :128]
        u[k] = v
        rz = rz + both[0, k] * v
        curve = curve + w[k] * v
    write_ends(w, weight0, weight1, low, high, y0, y1, z1, quads)
    low[40:48] = high[40:48] = lanes_of([rz, curve])


def near_kernel(body, up1, down1, own0, halo0, own1, halo1, x0, x1, r, tall, sides):
    weight0, weight1 = Joined(own0, halo0), Joined(own1, halo1)
    here, there = units(body, 0, 32), unpack_rows(up1, down1, 0, sides)
    near_sweep(lambda i: assemble_fine(here, there, i, near_sources), weight0, weight1, x0, x1, None, r, tall)


def second_kernel(x0, x1, own, up1, down1, up2, down2, weight2, own0, halo0s, own1, halo1, both,
                  m0, n0, low, high, *scratch):
    weight0s, weight1 = Joined(own0, halo0s), Joined(own1, halo1)
    (full, *scratch, y0, y1, z1, quads) = scratch
    shares = (own, up1, down1, up2, down2)
    up_sweep(lambda *a: assemble_shares(*shares, *a), weight2, weight1, weight0s, x0, x1, both.at[1], full, n0, *scratch)
    for k in range(16):
        m0[k] = full[k + 5, :16, :128]
    write_ends(n0, weight0s, weight1, low, high, y0, y1, z1, quads)
    ahead, behind = up1[208:210] + up2[24:26], down1[208:210] + own[208:210]
    for ref in (low, high):
        ref[40:42] = ahead + behind
        ref[42:44] = ahead
        ref[44:46] = behind
        ref[46:48] = jnp.zeros((2, 128), F32)


def third_kernel(x0, x1, own, up1, down1, up2, down2, weight2, own0, halo0s, own1, halo1, both, u0, w0, m0, n0,
                 r1, u1, w1, m1, n1, first, dots, full, last, *scratch):
    weight0s, weight1 = Joined(own0, halo0s), Joined(own1, halo1)
    shares = (own, up1, down1, up2, down2)
    up_sweep(lambda *a: assemble_shares(*shares, *a), weight2, weight1, weight0s, x0, x1, both.at[1], full, last, *scratch)
    total0 = own[208:209] + up2[25:26] + down2[26:27]
    first[...] = jnp.broadcast_to(total0, (8, 128))
    alpha = wide(total0, 0) / wide(total0, 1)
    sums = [jnp.zeros((16, 128), F32)] * 12
    for k in range(16):
        vw0, vm0, vn0 = w0[k], m0[k], n0[k]
        vr1 = both[0, k] - alpha * vw0
        vu1 = u0[k] - alpha * vm0
        vw1 = vw0 - alpha * vn0
        vm1 = vm0 - alpha * full[k + 5, :16, :128]
        vn1 = vn0 - alpha * last[k]
        r1[k], u1[k], w1[k], m1[k], n1[k] = vr1, vu1, vw1, vm1, vn1
        terms = [vr1 * vu1, vr1 * vm1, vr1 * vm0, vw1 * vu1, vw1 * vm1, vw1 * vm0,
                 vw0 * vu1, vw0 * vm1, vw0 * vm0, vn1 * vm1, vn1 * vm0, vn0 * vm0]
        sums = [s + t for s, t in zip(sums, terms)]
    dots[...] = lanes_of(sums)


def finish_kernel(first, second, u0, w0, m0, n0, r1, u1, w1, m1, n1, field_out, residual_out, field, residual, sems):
    g0, d0 = [wide(first[0:1], k) for k in range(2)]
    (r1u1, r1m1, r1m0, w1u1, w1m1, w1m0, w0u1, w0m1, w0m0, n1m1, n1m0, n0m0) = [wide(second[0:1], k) for k in range(12)]
    alpha0 = g0 / d0
    beta1 = r1u1 / g0
    curve1 = w1u1 + 2.0 * beta1 * w0u1 + beta1 * beta1 * d0
    alpha1 = r1u1 / curve1
    ab = alpha1 * beta1
    su = w1u1 + beta1 * w0u1 - alpha1 * (w1m1 + beta1 * w0m1) - ab * (w1m0 + beta1 * w0m0)
    g2 = (r1u1 - alpha1 * r1m1 - ab * r1m0) - alpha1 * su
    beta2 = g2 / r1u1
    uw = (w1u1 - 2.0 * alpha1 * w1m1 - 2.0 * ab * w1m0) + (alpha1 * alpha1 * n1m1 + 2.0 * alpha1 * ab * n1m0 + ab * ab * n0m0)
    curve2 = uw + 2.0 * beta2 * su + beta2 * beta2 * curve1
    alpha2 = g2 / curve2
    mix = alpha1 + alpha2 * beta2
    cu0, cu1, cm1, cm0 = alpha0 + mix * beta1, mix + alpha2, alpha2 * alpha1, alpha2 * ab
    cw0 = mix * beta1
    copies = []
    for k in range(16):
        field[k] = (cu0 * u0[k] + cu1 * u1[k]) - (cm1 * m1[k] + cm0 * m0[k])
        residual[k] = r1[k] - (cw0 * w0[k] + cu1 * w1[k]) + (cm1 * n1[k] + cm0 * n0[k])
        if k % 4 == 3:
            part = pl.ds(k - 3, 4)
            copies.append(pltpu.make_async_copy(field.at[part], field_out.at[part], sems.at[0, k // 4]))
            copies.append(pltpu.make_async_copy(residual.at[part], residual_out.at[part], sems.at[1, k // 4]))
            copies[-2].start()
            copies[-1].start()
    for copy in copies:
        copy.wait()


def shape(*dims):
    return jax.ShapeDtypeStruct(dims, F32)


def call(kernel, outs, scratch=(), specs=None, count=0, grant=40, flops=0, out=VMEM):
    return pl.pallas_call(
        kernel,
        out_shape=outs,
        in_specs=specs or [VMEM] * count,
        out_specs=[out] * len(outs),
        scratch_shapes=list(scratch),
        compiler_params=pltpu.CompilerParams(vmem_limit_bytes=grant * 1024 * 1024),
        cost_estimate=pl.CostEstimate(flops=flops, bytes_accessed=flops, transcendentals=0) if flops else None,
    )


def shift(v, axis, distance):
    count = lax.axis_size(axis)
    return lax.ppermute(v, axis, [((i + distance) % count, i) for i in range(count)])


def fine_exchange(own, low, high):
    above, below = shift(low, "gz", 1), shift(high, "gz", -1)
    first, last, core, upper, lower = call(
        first_join_kernel, [shape(2, 7, 16, 128), shape(2, 7, 16, 128), shape(768, 128), shape(240, 128), shape(240, 128)], count=3
    )(own, above, below)
    core_rows = shift(upper, "gy", 1), shift(lower, "gy", -1)
    before, after = shift(last, "gx", -1), shift(first, "gx", 1)
    rim = jnp.concatenate([before, after, own[:, :2]], axis=1).reshape(-1, 128)
    upper, lower = call(pack_rows_kernel, [shape(160, 128)] * 2, count=1)(rim)
    return core, rim, *core_rows, shift(upper, "gy", 1), shift(lower, "gy", -1)


def joint_exchange(own, low, high, final):
    above, below = shift(low, "gz", 1), shift(high, "gz", -1)
    first, last, small = call(
        functools.partial(join_z_kernel, final), [shape(144, 128), shape(144, 128), shape(32, 128)], count=4
    )(own, low, above, below)
    before, after, across = shift(last, "gx", -1), shift(first, "gx", 1), shift(small, "gx", 2)
    state = small[24:] if final else small[24:] + shift(small[24:], "gz", 4)
    body, upper, lower, ahead, behind = call(
        functools.partial(join_x_kernel, final), [shape(512, 128), shape(216, 128), shape(216, 128), shape(32, 128), shape(32, 128)],
        [pltpu.VMEM((4, 24, 128), F32)], count=8,
    )(own, above, below, small, state, before, after, across)
    return body, upper, shift(upper, "gy", 1), shift(lower, "gy", -1), shift(ahead, "gy", 2), shift(behind, "gy", -2)


def gather(unit):
    count = lax.axis_size("gx") * lax.axis_size("gy")
    return lax.all_to_all(jnp.broadcast_to(unit[None], (count,) + unit.shape), ("gx", "gy"), 0, 0, tiled=True)


def total(v):
    axes = ("gx", "gy", "gz")
    count = lax.axis_size("gx") * lax.axis_size("gy") * lax.axis_size("gz")
    parts = lax.all_to_all(jnp.broadcast_to(v[None, :1], (count, 1, 128)), axes, 0, 0, tiled=True)
    return jnp.broadcast_to(parts.sum(0), (8, 128))


def local(right_side, classes, table):
    def scratch(*shapes):
        return [pltpu.VMEM(s, F32) for s in shapes]

    block, short, mids, tile = shape(*BLOCK), shape(*SHORT), shape(*MID), shape(8, 128)
    up_scratch = scratch((6, 16, 256), (6, 16, 256), (4, 16, 256), (6, 24, 256), MID, MID, SHORT, SHORT)

    both, low, high = call(
        prepare_kernel, [shape(2, *BLOCK), shape(2, 6, 16, 128), shape(2, 6, 16, 128)],
        [pltpu.VMEM(BLOCK, jnp.int32), pltpu.SMEM((CLASSES,), F32), pltpu.SemaphoreType.DMA((3,))], specs=[ANY] * 3, grant=60,
    )(right_side, classes, table)
    halos = fine_exchange(both, low, high)
    own0, own1, unit2 = call(
        own_weights_kernel, [shape(SLABS, 16, 256), shape(MIDS, 16, 256), tile],
        scratch((MIDS, 16, 256), (2, 4, 16, 128)), count=2, flops=4_000_000,
    )(*halos[:2])
    halo0, halo0s, halo1, x0, x1, unit = call(
        first_down_kernel, [shape(SLABS, 16, 256), shape(SLABS, 8, 256), shape(MIDS, 8, 256), short, mids, tile],
        scratch(SHORT, HALO, MID, (2, 4, 16, 128), (16 * UNITS, 128)), count=8,
    )(*halos, own0, own1)
    ends = [shape(48, 128), shape(48, 128)]
    share_scratch = scratch(BLOCK, (10, 24, 256), (10, 24, 256), (2, 6, 24, 128))
    weight2, u0, w0, low, high = call(
        first_up_kernel, [shape(4, 16, 256), block, block, *ends], up_scratch + share_scratch, count=8
    )(gather(jnp.stack([unit, unit2])), own0, halo0s, own1, halo1, x0, x1, both)

    def near(body, up1, down1):
        return call(near_kernel, [short, mids], scratch(SHORT, HALO, (512, 128)), count=7, flops=4_000_000)(
            body, up1, down1, own0, halo0, own1, halo1
        )

    body, own, up1, down1, up2, down2 = joint_exchange(w0, low, high, False)
    x0, x1 = near(body, up1, down1)
    m0, n0, low, high = call(
        second_kernel, [block, block, *ends], scratch(SHORT) + up_scratch[:-1] + share_scratch, count=13
    )(x0, x1, own, up1, down1, up2, down2, weight2, own0, halo0s, own1, halo1, both)
    body, own, up1, down1, up2, down2 = joint_exchange(n0, low, high, True)
    x0, x1 = near(body, up1, down1)
    r1, u1, w1, m1, n1, first, dots = call(
        third_kernel, [block] * 5 + [tile, tile], scratch(SHORT, BLOCK) + up_scratch[:-1], count=17
    )(x0, x1, own, up1, down1, up2, down2, weight2, own0, halo0s, own1, halo1, both, u0, w0, m0, n0)
    field, residual = call(
        finish_kernel, [block] * 2, scratch(BLOCK, BLOCK) + [pltpu.SemaphoreType.DMA((2, 4))], count=11, out=ANY
    )(
        first, total(dots), u0, w0, m0, n0, r1, u1, w1, m1, n1
    )
    return field, residual


def solution(mesh):
    in_specs = (P("gx", "gy", "gz"), P("gx", "gy", "gz"), P())
    out_specs = (P("gx", "gy", "gz"), P("gx", "gy", "gz"))
    return jax.shard_map(local, mesh=mesh, in_specs=in_specs, out_specs=out_specs, check_vma=False)
```

```python
import functools

import jax
import jax.numpy as jnp
from jax import lax
from jax.experimental import pallas as pl
from jax.experimental.pallas import tpu as pltpu
from jax.sharding import PartitionSpec as P

CLASSES = 16
COARSE_SWEEPS = 6
OMEGA = 0.8
KEEP = 1.0 - OMEGA
F32 = jnp.float32
SLABS, MIDS, UNITS = 26, 12, 40
MARK = 64
BLOCK, HALO, SHORT, MID = (16, 16, 128), (SLABS, 32, 256), (SLABS, 24, 256), (MIDS, 24, 256)
VMEM = pl.BlockSpec(memory_space=pltpu.VMEM)
ANY = pl.BlockSpec(memory_space=pl.ANY)


def iota(shape, dim):
    return lax.broadcasted_iota(jnp.int32, shape, dim)


def roll(v, shift, axis):
    shift = shift % v.shape[axis]
    return v if shift == 0 else pltpu.roll(v, shift, axis)


def around(v, rows, lanes):
    return (roll(v, rows, 0) + roll(v, -rows, 0)) + (roll(v, lanes, 1) + roll(v, -lanes, 1))


def pair_mean(v, step):
    rows = (iota(v.shape, 0) // step) % 2 == 0
    v = v + jnp.where(rows, roll(v, -step, 0), roll(v, step, 0))
    lanes = (iota(v.shape, 1) // step) % 2 == 0
    v = v + jnp.where(lanes, roll(v, -step, 1), roll(v, step, 1))
    return v * 0.125


def place():
    return tuple(lax.axis_index(axis) for axis in ("gx", "gy", "gz"))


def sizes():
    return tuple(lax.axis_size(axis) for axis in ("gx", "gy", "gz"))


def pack_fine(read, low_ref, high_ref):
    lane = iota((16, 128), 1)
    chunk = lane // 32
    for g in range(4):
        low = high = None
        for j in range(4):
            v = read(4 * g + j)
            first, last = roll(v, 32 * j, 1), roll(v, 32 * j + 32, 1)
            low = first if j == 0 else jnp.where(chunk == j, first, low)
            high = last if j == 0 else jnp.where(chunk == j, last, high)
        low_ref[g] = low
        high_ref[g] = high
    for g, slabs in ((4, (0, 1, 2, 3, 4)), (5, (15, 14, 13, 12, 11))):
        low, high = read(slabs[0]), roll(read(slabs[0]), 32, 1)
        for j in range(1, 5):
            v, here = read(slabs[j]), (lane >= 112 if j == 4 else chunk == j)
            low = jnp.where(here, roll(v, 112 if j == 4 else 32 * j, 1), low)
            high = jnp.where(here, roll(v, (32, 64, 96, 112, 0)[j], 1), high)
        low_ref[g] = low
        high_ref[g] = high


def pack_near(read, low_ref, high_ref):
    chunk = iota((16, 128), 1) // 8
    low = high = None
    for k in range(16):
        v = read(k)
        first, last = roll(v, 8 * k, 1), roll(v, 8 * k + 8, 1)
        low = first if k == 0 else jnp.where(chunk == k, first, low)
        high = last if k == 0 else jnp.where(chunk == k, last, high)
    low_ref[...] = low
    high_ref[...] = high


def prepare_kernel(rhs_in, classes_in, table_in, both, low, high, classes, table, sems):
    copies = [
        pltpu.make_async_copy(rhs_in, both.at[0], sems.at[0]),
        pltpu.make_async_copy(classes_in, classes, sems.at[1]),
        pltpu.make_async_copy(table_in, table, sems.at[2]),
    ]
    for copy in copies:
        copy.start()
    for copy in copies:
        copy.wait()
    for k in range(16):
        c = classes[k]
        v = jnp.zeros((16, 128), F32)
        for index in range(CLASSES):
            v = jnp.where(c == index, table[index], v)
        both[1, k] = v
    for t in range(2):
        pack_fine(lambda k, t=t: both[t, k], low.at[t], high.at[t])


def slab_sources(i):
    x = i - 5
    if 0 <= x < 16:
        return x, 16 + x // 4, 20 + x // 4, -32 * (x % 4), 96 - 32 * (x % 4)
    base, far = (24, -1 - x) if x < 0 else (31, x - 16)
    return base + (x + 5 if x < 0 else far), base + 5, base + 6, (0, -32, -64, -96, -112)[far], (96, 64, 32, 16, 0)[far]


def near_sources(i):
    x = i - 5
    base, above, k = (x, 16, x) if 0 <= x < 16 else ((23 + x, 23, 16 + x) if x < 0 else (x + 9, 30, x - 16))
    return base, above, above + 1, -8 * k, 120 - 8 * k


def assemble_half(refs, i, sources):
    main, above, below, up, down = sources(i)
    lane = iota((16, 128), 1)
    side = jnp.where(lane < 64, roll(refs[above][...], up, 1), roll(refs[below][...], down, 1))
    return jnp.concatenate([refs[main][...], side], axis=1)


def assemble_fine(body, sides, i, sources=slab_sources):
    return jnp.concatenate([assemble_half(body, i, sources), assemble_half(sides, i, sources)], axis=0)


class Joined:
    def __init__(self, top, bottom):
        self.top, self.bottom = top, bottom

    def __getitem__(self, i):
        return jnp.concatenate([self.top[i], self.bottom[i]], axis=0)


def pack_rows_kernel(body, upper, lower):
    for g in range(body.shape[0] // 128):
        for t in range(5):
            here = pl.ds(8 * (5 * g + t), 8)
            upper[here] = body[pl.ds(128 * g + t, 8, stride=16), :]
            lower[here] = body[pl.ds(128 * g + 11 + t, 8, stride=16), :]


def units(body, first, count):
    return [body.at[pl.ds(first + 16 * u, 16)] for u in range(count)]


def unpack_rows(upper, lower, first, sides):
    sides[...] = jnp.zeros(sides.shape, F32)
    for g in range(sides.shape[0] // 128):
        for t in range(5):
            here = pl.ds(8 * (first + 5 * g + t), 8)
            sides[pl.ds(128 * g + t, 8, stride=16), :] = upper[here]
            sides[pl.ds(128 * g + 11 + t, 8, stride=16), :] = lower[here]
    return units(sides, 0, sides.shape[0] // 16)


def squeeze(v):
    return jnp.concatenate([v[:16], jnp.where(iota((8, v.shape[1]), 0) < 4, v[16:24], v[24:])], axis=0)


def near(lane):
    return (lane < 160) | (lane >= 224)


def inside_lanes(lane):
    z = jnp.where(lane < 192, lane, lane - 256) + 128 * place()[2]
    return near(lane) & (z >= 0) & (z < 128 * sizes()[2])


def squeeze_half(v):
    return jnp.where(iota((8, v.shape[1]), 0) < 4, v[:8], v[8:])


def weigh(kap, extra, i, shift, cells, inside):
    x = cells * place()[0] + (i - shift)
    return jnp.where(inside & (x >= 0) & (x < cells * sizes()[0]), OMEGA / (kap + extra), 0.0)


def first_join_kernel(own, above, below, first, last, core, upper, lower):
    for t in range(2):
        for k in range(5):
            first[t, k] = own[t, k]
            last[t, k] = own[t, 11 + k]
        for ref, pack in ((first, 4), (last, 5)):
            ref[t, 5] = above[t, pack]
            ref[t, 6] = below[t, pack]
        for k in range(24):
            source = own[t, k] if k < 16 else (above[t, k - 16] if k < 20 else below[t, k - 20])
            core[pl.ds(16 * (24 * t + k), 16)] = source
    pack_rows_kernel(core, upper, lower)


def rim_join_kernel(before, after, rim, upper, lower):
    for t in range(2):
        for k in range(16):
            source = before[t, k] if k < 7 else (after[t, k - 7] if k < 14 else jnp.zeros((16, 128), F32))
            rim[pl.ds(16 * (16 * t + k), 16)] = source
    pack_rows_kernel(rim, upper, lower)


def two_parts(core, rim, t):
    return units(core, 24 * 16 * t, 24) + units(rim, 16 * 16 * t, 16)


def two_sides(core_upper, core_lower, rim_upper, rim_lower, t, sides):
    there = unpack_rows(core_upper, core_lower, 15 * t, sides.at[pl.ds(0, 384)])
    return there + unpack_rows(rim_upper, rim_lower, 10 * t, sides.at[pl.ds(384, 256)])


def own_weights_kernel(core, rim, weight0, weight1, unit, middle, quads):
    here = two_parts(core, rim, 1)
    inside = inside_lanes(iota((16, 256), 1))
    for m in range(-1, MIDS + 1):
        pair = []
        for i in (2 * m + 1, 2 * m + 2):
            if 0 <= i < SLABS:
                kap = assemble_half(here, i, slab_sources)
                weight0[i] = weigh(kap, 6.0, i, 5, 16, inside)
                pair.append(kap)
        if 0 <= m < MIDS:
            kap1 = pair_mean(pair[0] + pair[1], 1)
            middle[m] = kap1
            weight1[m] = weigh(kap1, 1.5, m, 2, 8, inside)
    for c in range(4):
        weight2 = OMEGA / (pair_mean(middle[2 + 2 * c] + middle[3 + 2 * c], 2) + 0.375)
        quads[0, c], quads[1, c] = weight2[:, :128], weight2[:, 128:]
    pack_coarse(quads, unit)


def halo_weights(there, weight0, weight0s, weight1):
    row, lane = iota((16, 256), 0), iota((16, 256), 1)
    y = jnp.where(row < 8, row + 16, row - 16) + 16 * place()[1]
    inside = inside_lanes(lane) & (y >= 0) & (y < 16 * sizes()[1])
    y = jnp.where(iota((8, 256), 0) < 4, 1, -1) + place()[1]
    insides = inside_lanes(iota((8, 256), 1)) & (y >= 0) & (y < sizes()[1])
    for m in range(-1, MIDS + 1):
        pair = []
        for i in (2 * m + 1, 2 * m + 2):
            if 0 <= i < SLABS:
                kap = assemble_half(there, i, slab_sources)
                v = weigh(kap, 6.0, i, 5, 16, inside)
                weight0[i] = v
                weight0s[i] = squeeze_half(v)
                pair.append(squeeze_half(kap))
        if 0 <= m < MIDS:
            weight1[m] = weigh(pair_mean(pair[0] + pair[1], 1), 1.5, m, 2, 8, insides)


def pack_coarse(quads, unit):
    turn = iota((4, 128), 1) % 4
    for half in range(2):
        v = quads[half, 0, pl.ds(0, 4, stride=4), :]
        for c in range(1, 4):
            v = jnp.where(turn == c, quads[half, c, pl.ds(0, 4, stride=4), :], v)
        unit[4 * half:4 * half + 4] = v


def near_sweep(read, weight0, weight1, x0, x1, r1, r, tall):
    for i in range(SLABS):
        v = read(i)
        r[i] = squeeze(v)
        v = weight0[i] * v
        tall[i] = v
        x0[i] = squeeze(v)
    def middle_slab(m, carry):
        i = 2 * m + 1
        two = tall[i] + tall[i + 1]
        rows = squeeze(roll(two, 1, 0) + roll(two, -1, 0))
        two = x0[i] + x0[i + 1]
        lanes = roll(two, 1, 1) + roll(two, -1, 1)
        v = pair_mean(KEEP * (r[i] + r[i + 1]) + ((x0[i - 1] + x0[i + 2]) + two) + (rows + lanes), 1)
        if r1 is not None:
            r1[m] = v
        x1[m] = weight1[m] * v
        return carry

    lax.fori_loop(0, MIDS, middle_slab, 0, unroll=4)


def first_down_kernel(core, rim, core_upper, core_lower, rim_upper, rim_lower, own0, own1, halo0, halo0s, halo1, x0, x1, unit, r, tall, r1, quads, sides):
    rows = (core_upper, core_lower, rim_upper, rim_lower)
    halo_weights(two_sides(*rows, 1, sides), halo0, halo0s, halo1)
    here, there = two_parts(core, rim, 0), two_sides(*rows, 0, sides)
    weight0, weight1 = Joined(own0, halo0), Joined(own1, halo1)
    near_sweep(lambda i: assemble_fine(here, there, i), weight0, weight1, x0, x1, r1, r, tall)
    for c in range(4):
        m = 2 + 2 * c
        two = x1[m] + x1[m + 1]
        left = KEEP * (r1[m] + r1[m + 1]) + 0.25 * (((x1[m - 1] + x1[m + 2]) + two) + around(two, 2, 2))
        v = pair_mean(left, 2)[:16]
        quads[0, c], quads[1, c] = v[:, :128], v[:, 128:]
    pack_coarse(quads, unit)


def share_sweep(block, weight0, weight1, share, x0, r1, x1, quads):
    for k in range(16):
        x0[k] = weight0.top[k + 5, :, :128] * block[k]
    zero, low = jnp.zeros((16, 128), F32), jnp.zeros((8, 256), F32)

    def tall(v):
        return jnp.concatenate([jnp.concatenate([v, zero], axis=1), low], axis=0)

    for m in range(10):
        x = 2 * (m - 1)
        if m == 0:
            left = tall(x0[0])
        elif m == 9:
            left = tall(x0[15])
        else:
            two = x0[x] + x0[x + 1]
            flat = KEEP * (block[x] + block[x + 1]) + two
            flat = flat + x0[x - 1] if x > 0 else flat
            flat = flat + x0[x + 2] if x < 14 else flat
            left = tall(flat) + around(tall(two), 1, 1)
        v = pair_mean(left, 1)
        r1[m] = v
        x1[m] = weight1[m + 1] * v
    for c in range(6):
        pair = [m for m in (2 * c - 1, 2 * c) if 0 <= m < 10]
        two = sum(x1[m] for m in pair)
        left = KEEP * sum(r1[m] for m in pair)
        beside = two + around(two, 2, 2)
        for m in (2 * c - 2, 2 * c + 1):
            beside = beside + x1[m] if 0 <= m < 10 else beside
        v = pair_mean(left + 0.25 * beside, 2)
        quads[0, c], quads[1, c] = v[:, :128], v[:, 128:]
    gy, gz = place()[1:]
    ny, nz = sizes()[1:]
    for half in range(2):
        for start, count, first in ((20, 1, 0), (0, 5, 1)):
            row, lane = iota((count, 128), 0), iota((count, 128), 1)
            y = row // 4 + gy - (1 if count == 1 else 0)
            inside = (y >= 0) & (y < ny)
            if half == 1:
                z = jnp.where(lane < 64, gz + 1, gz - 1)
                inside = inside & (z >= 0) & (z < nz)

            def rows(c):
                v = quads[half, c, pl.ds(start, count, stride=4), :] if count > 1 else quads[half, c, pl.ds(start, 1), :]
                return jnp.where(inside, v, 0.0)

            turn = lane % 4
            v = rows(1)
            for c in range(1, 4):
                v = jnp.where(turn == c, rows(c + 1), v)
            share[pl.ds(6 * half + first, count)] = v
            v = jnp.where(turn == 3, rows(0), jnp.where(turn == 0, rows(5), 0.0))
            share[pl.ds(12 + 6 * half + first, count)] = v


def join_z_kernel(final, own, low, above, below, first, last, small):
    share, state = low[16:40], low[40:48]
    lane = iota((6, 128), 1)
    for s in (0, 12):
        main, side = pl.ds(16 + s, 6), pl.ds(22 + s, 6)
        v = share[s:s + 6] + jnp.where(lane >= 124, above[side], 0.0) + jnp.where(lane < 4, below[side], 0.0)
        small[pl.ds(s, 6)] = v
        v = share[s + 6:s + 12] + jnp.where(lane < 32, above[main], jnp.where(lane >= 96, below[main], 0.0))
        small[pl.ds(s + 6, 6)] = v
    row = iota((8, 128), 0)
    if final:
        sums = [state[j:j + 1] + state[j + 1:j + 2] + above[41 + j:42 + j] + below[40 + j:41 + j] for j in (0, 2, 4)]
    else:
        sums = [state[0:1], above[40:41]]
    v = jnp.zeros((8, 128), F32)
    for j, part in enumerate(sums):
        v = jnp.where(row == j, part, v)
    small[24:32] = v
    for k in range(5):
        first[pl.ds(16 * k, 16)] = own[k]
        last[pl.ds(16 * k, 16)] = own[11 + k]
    for ref in (first, last):
        ref[80:96] = above[:16]
        ref[96:112] = below[:16]
        ref[112:144] = small[...]


def join_x_kernel(final, own, above, below, small, sums, before, after, across, body, upper, lower, ahead, behind, stage):
    for k in range(16):
        body[pl.ds(16 * k, 16)] = own[k]
    body[256:272] = above[:16]
    body[272:288] = below[:16]
    body[288:400] = before[:112]
    body[400:512] = after[:112]
    pack_rows_kernel(body, upper, lower)
    gx = place()[0]
    for k, rows in enumerate((small[:24], after[112:136], across[:24], before[112:136])):
        stage[lax.rem(gx + k, 4)] = rows
    turn = iota((12, 128), 1) % 4
    for b in range(4):
        v = stage[b, :12]
        if b < 3:
            v = v + jnp.where(turn == 3, stage[b + 1, 12:], 0.0)
        if b > 0:
            v = v + jnp.where(turn == 0, stage[b - 1, 12:], 0.0)
        for ref in (upper, lower):
            ref[pl.ds(160 + 12 * b, 12)] = v
        for half in range(2):
            ahead[pl.ds(6 * b + 3 * half, 3)] = v[6 * half:6 * half + 3]
            behind[pl.ds(6 * b + 3 * half, 3)] = v[6 * half + 3:6 * half + 6]
    state = sums[...]
    if final:
        state = (state + before[136:144]) + (after[136:144] + across[24:32])
    for ref, start in ((upper, 208), (lower, 208), (ahead, 24), (behind, 24)):
        ref[pl.ds(start, 8)] = state


def unfold(v, c):
    turn = iota(v.shape, 1) % 4
    slab = roll(v, -c, 1)
    for j in range(1, 4):
        slab = jnp.where(turn == j, roll(v, j - c, 1), slab)
    return slab


def assemble_shares(own, up1, down1, up2, down2, out, change):
    def zeros(n):
        return jnp.zeros((n, 128), F32)

    for k in range(4):
        halves = []
        for half in range(2):
            s, t = 160 + 12 * k + 6 * half, 6 * k + 3 * half
            v = jnp.concatenate([own[s + 1:s + 6], zeros(10), own[s:s + 1]], axis=0)
            v = v + jnp.concatenate([zeros(3), up1[s:s + 6], zeros(7)], axis=0)
            v = v + jnp.concatenate([zeros(7), up2[t:t + 3], zeros(6)], axis=0)
            v = v + jnp.concatenate([down1[s + 5:s + 6], zeros(10), down1[s:s + 5]], axis=0)
            v = v + jnp.concatenate([zeros(10), down2[t:t + 3], zeros(3)], axis=0)
            halves.append(v)
        out[k] = change(k, jnp.concatenate(halves, axis=1))


def assemble_coarse(gather, t, out, change):
    gy, ny = place()[1], sizes()[1]
    for k in range(4):
        own, up1, up2, down2, down1 = [ny * k + lax.rem(gy + d + ny, ny) for d in (0, 1, 2, -2, -1)]
        v = jnp.concatenate(
            [
                jnp.concatenate([
                    gather[own, t, s:s + 4], gather[up1, t, s:s + 4], gather[up2, t, s:s + 2],
                    gather[down2, t, s + 2:s + 4], gather[down1, t, s:s + 4],
                ], axis=0)
                for s in (0, 4)
            ],
            axis=1,
        )
        out[k] = change(k, v)


def up_sweep(assemble, weight2, weight1, weight0, x0, x1, kap, u, w, a, b, rhs2, spread, middle, t1, t0):
    zero = jnp.zeros((16, 256), F32)
    for ref in (a, b):
        ref[0] = zero
        ref[5] = zero
    assemble(rhs2, lambda g, v: weight2[g] * v)
    for g in range(4):
        a[g + 1] = rhs2[g]
    turn = iota((16, 256), 1) % 4
    for sweep in range(COARSE_SWEEPS - 1):
        old, new = (a, b) if sweep % 2 == 0 else (b, a)
        ahead = [None] + [roll(old[g], -4, 1) for g in range(1, 5)] + [None]
        back = [None] + [roll(old[g], 4, 1) for g in range(1, 5)] + [None]
        for g in range(1, 5):
            v = old[g]
            up = roll(jnp.where(turn == 3, zero if g == 1 else ahead[g - 1], v), 1, 1)
            down = roll(jnp.where(turn == 0, zero if g == 4 else back[g + 1], v), -1, 1)
            beside = (up + down) + (ahead[g] + back[g]) + (roll(v, 1, 0) + roll(v, -1, 0))
            new[g] = (KEEP * v + rhs2[g - 1]) + weight2[g - 1] * (0.0625 * beside)
    last = b if COARSE_SWEEPS % 2 == 0 else a
    gx = place()[0]
    half = iota((8, 256), 0) < 4
    for c in range(6):
        g, t = (gx, 3) if c == 0 else ((gx + 2, 0) if c == 5 else (gx + 1, c - 1))
        v = unfold(last[g], t)
        spread[c] = jnp.concatenate(
            [
                jnp.where(half, jnp.broadcast_to(v[j:j + 1], (8, 256)), jnp.broadcast_to(v[k:k + 1], (8, 256)))
                for j, k in ((0, 1), (2, 3), (4, 15))
            ],
            axis=0,
        )
    for m in range(MIDS):
        t1[m] = x1[m] + spread[m // 2]
    for m in range(1, MIDS - 1):
        v = t1[m]
        beside = (t1[m - 1] + t1[m + 1]) + around(v, 2, 2)
        middle[m] = (KEEP * v + x1[m]) + weight1[m] * (0.25 * beside)
    for i in range(3, SLABS - 3):
        t0[i] = x0[i] + middle[(i - 1) // 2]
    for i in range(4, SLABS - 4):
        v = t0[i]
        beside = (t0[i - 1] + t0[i + 1]) + around(v, 1, 1)
        u[i] = (KEEP * v + x0[i]) + weight0[i] * beside
    for i in range(5, SLABS - 5):
        v = u[i]
        beside = (u[i - 1] + u[i + 1]) + around(v, 1, 1)
        w[i - 5] = (kap[i - 5] + 6.0) * v[:16, :128] - beside[:16, :128]


def lanes_of(values):
    rows = [jnp.sum(v, axis=0, keepdims=True) for v in values]
    sums = jnp.sum(jnp.concatenate(rows + [jnp.zeros((16 - len(rows), 128), F32)], axis=0), axis=1, keepdims=True)
    picked = jnp.where(iota((16, 128), 1) == MARK + iota((16, 128), 0), sums, 0.0)
    return jnp.broadcast_to(jnp.sum(picked, axis=0, keepdims=True), (8, 128))


def write_ends(w, weight0, weight1, low, high, *scratch):
    pack_near(lambda k: w[k], low.at[pl.ds(0, 16)], high.at[pl.ds(0, 16)])
    share_sweep(w, weight0, weight1, low.at[pl.ds(16, 24)], *scratch)
    high[16:40] = low[16:40]


def wide(row, k):
    return jnp.broadcast_to(row[:, MARK + k:MARK + k + 1], (16, 128))


def first_up_kernel(gather, own0, halo0s, own1, halo1, x0, x1, both, weight2, u, w, low, high, *scratch):
    (*scratch, full, y0, y1, z1, quads) = scratch
    weight0, weight1 = Joined(own0, halo0s), Joined(own1, halo1)
    row, lane = iota((16, 256), 0), iota((16, 256), 1)
    y = jnp.where(row < 10, row, row - 16) + 4 * place()[1]
    inside = inside_lanes(lane) & (y >= 0) & (y < 4 * sizes()[1])
    assemble_coarse(gather, 1, weight2, lambda s, v: jnp.where(inside, v, 0.0))
    up_sweep(lambda *a: assemble_coarse(gather, 0, *a), weight2, weight1, weight0, x0, x1, both.at[1], full, w, *scratch)
    rz = curve = jnp.zeros((16, 128), F32)
    for k in range(16):
        v = full[k + 5][:16, :128]
        u[k] = v
        rz = rz + both[0, k] * v
        curve = curve + w[k] * v
    write_ends(w, weight0, weight1, low, high, y0, y1, z1, quads)
    low[40:48] = high[40:48] = lanes_of([rz, curve])


def near_kernel(body, up1, down1, own0, halo0, own1, halo1, x0, x1, r, tall, sides):
    weight0, weight1 = Joined(own0, halo0), Joined(own1, halo1)
    here, there = units(body, 0, 32), unpack_rows(up1, down1, 0, sides)
    near_sweep(lambda i: assemble_fine(here, there, i, near_sources), weight0, weight1, x0, x1, None, r, tall)


def second_kernel(x0, x1, own, up1, down1, up2, down2, weight2, own0, halo0s, own1, halo1, both,
                  m0, n0, low, high, *scratch):
    weight0s, weight1 = Joined(own0, halo0s), Joined(own1, halo1)
    (full, *scratch, y0, y1, z1, quads) = scratch
    shares = (own, up1, down1, up2, down2)
    up_sweep(lambda *a: assemble_shares(*shares, *a), weight2, weight1, weight0s, x0, x1, both.at[1], full, n0, *scratch)
    for k in range(16):
        m0[k] = full[k + 5, :16, :128]
    write_ends(n0, weight0s, weight1, low, high, y0, y1, z1, quads)
    ahead, behind = up1[208:210] + up2[24:26], down1[208:210] + own[208:210]
    for ref in (low, high):
        ref[40:42] = ahead + behind
        ref[42:44] = ahead
        ref[44:46] = behind
        ref[46:48] = jnp.zeros((2, 128), F32)


def third_kernel(x0, x1, own, up1, down1, up2, down2, weight2, own0, halo0s, own1, halo1, both, u0, w0, m0, n0,
                 r1, u1, w1, m1, n1, first, dots, full, last, *scratch):
    weight0s, weight1 = Joined(own0, halo0s), Joined(own1, halo1)
    shares = (own, up1, down1, up2, down2)
    up_sweep(lambda *a: assemble_shares(*shares, *a), weight2, weight1, weight0s, x0, x1, both.at[1], full, last, *scratch)
    total0 = own[208:209] + up2[25:26] + down2[26:27]
    first[...] = jnp.broadcast_to(total0, (8, 128))
    alpha = wide(total0, 0) / wide(total0, 1)
    sums = [jnp.zeros((16, 128), F32)] * 12
    for k in range(16):
        vw0, vm0, vn0 = w0[k], m0[k], n0[k]
        vr1 = both[0, k] - alpha * vw0
        vu1 = u0[k] - alpha * vm0
        vw1 = vw0 - alpha * vn0
        vm1 = vm0 - alpha * full[k + 5, :16, :128]
        vn1 = vn0 - alpha * last[k]
        r1[k], u1[k], w1[k], m1[k], n1[k] = vr1, vu1, vw1, vm1, vn1
        terms = [vr1 * vu1, vr1 * vm1, vr1 * vm0, vw1 * vu1, vw1 * vm1, vw1 * vm0,
                 vw0 * vu1, vw0 * vm1, vw0 * vm0, vn1 * vm1, vn1 * vm0, vn0 * vm0]
        sums = [s + t for s, t in zip(sums, terms)]
    dots[...] = lanes_of(sums)


def finish_kernel(first, second, u0, w0, m0, n0, r1, u1, w1, m1, n1, field_out, residual_out, field, residual, sems):
    g0, d0 = [wide(first[0:1], k) for k in range(2)]
    (r1u1, r1m1, r1m0, w1u1, w1m1, w1m0, w0u1, w0m1, w0m0, n1m1, n1m0, n0m0) = [wide(second[0:1], k) for k in range(12)]
    alpha0 = g0 / d0
    beta1 = r1u1 / g0
    curve1 = w1u1 + 2.0 * beta1 * w0u1 + beta1 * beta1 * d0
    alpha1 = r1u1 / curve1
    ab = alpha1 * beta1
    su = w1u1 + beta1 * w0u1 - alpha1 * (w1m1 + beta1 * w0m1) - ab * (w1m0 + beta1 * w0m0)
    g2 = (r1u1 - alpha1 * r1m1 - ab * r1m0) - alpha1 * su
    beta2 = g2 / r1u1
    uw = (w1u1 - 2.0 * alpha1 * w1m1 - 2.0 * ab * w1m0) + (alpha1 * alpha1 * n1m1 + 2.0 * alpha1 * ab * n1m0 + ab * ab * n0m0)
    curve2 = uw + 2.0 * beta2 * su + beta2 * beta2 * curve1
    alpha2 = g2 / curve2
    mix = alpha1 + alpha2 * beta2
    cu0, cu1, cm1, cm0 = alpha0 + mix * beta1, mix + alpha2, alpha2 * alpha1, alpha2 * ab
    cw0 = mix * beta1
    copies = []
    for k in range(16):
        field[k] = (cu0 * u0[k] + cu1 * u1[k]) - (cm1 * m1[k] + cm0 * m0[k])
        residual[k] = r1[k] - (cw0 * w0[k] + cu1 * w1[k]) + (cm1 * n1[k] + cm0 * n0[k])
        if k % 4 == 3:
            part = pl.ds(k - 3, 4)
            copies.append(pltpu.make_async_copy(field.at[part], field_out.at[part], sems.at[0, k // 4]))
            copies.append(pltpu.make_async_copy(residual.at[part], residual_out.at[part], sems.at[1, k // 4]))
            copies[-2].start()
            copies[-1].start()
    for copy in copies:
        copy.wait()


def shape(*dims):
    return jax.ShapeDtypeStruct(dims, F32)


def call(kernel, outs, scratch=(), specs=None, count=0, grant=40, flops=0, out=VMEM):
    return pl.pallas_call(
        kernel,
        out_shape=outs,
        in_specs=specs or [VMEM] * count,
        out_specs=[out] * len(outs),
        scratch_shapes=list(scratch),
        compiler_params=pltpu.CompilerParams(vmem_limit_bytes=grant * 1024 * 1024),
        cost_estimate=pl.CostEstimate(flops=flops, bytes_accessed=flops, transcendentals=0) if flops else None,
    )


def shift(v, axis, distance):
    count = lax.axis_size(axis)
    return lax.ppermute(v, axis, [((i + distance) % count, i) for i in range(count)])


def fine_exchange(own, low, high):
    above, below = shift(low, "gz", 1), shift(high, "gz", -1)
    first, last, core, upper, lower = call(
        first_join_kernel, [shape(2, 7, 16, 128), shape(2, 7, 16, 128), shape(768, 128), shape(240, 128), shape(240, 128)], count=3
    )(own, above, below)
    core_rows = shift(upper, "gy", 1), shift(lower, "gy", -1)
    before, after = shift(last, "gx", -1), shift(first, "gx", 1)
    rim, upper, lower = call(rim_join_kernel, [shape(512, 128), shape(160, 128), shape(160, 128)], count=2)(before, after)
    return core, rim, *core_rows, shift(upper, "gy", 1), shift(lower, "gy", -1)


def joint_exchange(own, low, high, final):
    above, below = shift(low, "gz", 1), shift(high, "gz", -1)
    first, last, small = call(
        functools.partial(join_z_kernel, final), [shape(144, 128), shape(144, 128), shape(32, 128)], count=4
    )(own, low, above, below)
    before, after, across = shift(last, "gx", -1), shift(first, "gx", 1), shift(small, "gx", 2)
    state = small[24:] if final else small[24:] + shift(small[24:], "gz", 4)
    body, upper, lower, ahead, behind = call(
        functools.partial(join_x_kernel, final), [shape(512, 128), shape(216, 128), shape(216, 128), shape(32, 128), shape(32, 128)],
        [pltpu.VMEM((4, 24, 128), F32)], count=8,
    )(own, above, below, small, state, before, after, across)
    return body, upper, shift(upper, "gy", 1), shift(lower, "gy", -1), shift(ahead, "gy", 2), shift(behind, "gy", -2)


def gather(unit):
    count = lax.axis_size("gx") * lax.axis_size("gy")
    return lax.all_to_all(jnp.broadcast_to(unit[None], (count,) + unit.shape), ("gx", "gy"), 0, 0, tiled=True)


def total(v):
    axes = ("gx", "gy", "gz")
    count = lax.axis_size("gx") * lax.axis_size("gy") * lax.axis_size("gz")
    parts = lax.all_to_all(jnp.broadcast_to(v[None, :1], (count, 1, 128)), axes, 0, 0, tiled=True)
    return jnp.broadcast_to(parts.sum(0), (8, 128))


def local(right_side, classes, table):
    def scratch(*shapes):
        return [pltpu.VMEM(s, F32) for s in shapes]

    block, short, mids, tile = shape(*BLOCK), shape(*SHORT), shape(*MID), shape(8, 128)
    up_scratch = scratch((6, 16, 256), (6, 16, 256), (4, 16, 256), (6, 24, 256), MID, MID, SHORT, SHORT)

    both, low, high = call(
        prepare_kernel, [shape(2, *BLOCK), shape(2, 6, 16, 128), shape(2, 6, 16, 128)],
        [pltpu.VMEM(BLOCK, jnp.int32), pltpu.SMEM((CLASSES,), F32), pltpu.SemaphoreType.DMA((3,))], specs=[ANY] * 3, grant=60,
    )(right_side, classes, table)
    halos = fine_exchange(both, low, high)
    own0, own1, unit2 = call(
        own_weights_kernel, [shape(SLABS, 16, 256), shape(MIDS, 16, 256), tile],
        scratch((MIDS, 16, 256), (2, 4, 16, 128)), count=2, flops=4_000_000,
    )(*halos[:2])
    halo0, halo0s, halo1, x0, x1, unit = call(
        first_down_kernel, [shape(SLABS, 16, 256), shape(SLABS, 8, 256), shape(MIDS, 8, 256), short, mids, tile],
        scratch(SHORT, HALO, MID, (2, 4, 16, 128), (16 * UNITS, 128)), count=8,
    )(*halos, own0, own1)
    ends = [shape(48, 128), shape(48, 128)]
    share_scratch = scratch(BLOCK, (10, 24, 256), (10, 24, 256), (2, 6, 24, 128))
    weight2, u0, w0, low, high = call(
        first_up_kernel, [shape(4, 16, 256), block, block, *ends], up_scratch + share_scratch, count=8
    )(gather(jnp.stack([unit, unit2])), own0, halo0s, own1, halo1, x0, x1, both)

    def near(body, up1, down1):
        return call(near_kernel, [short, mids], scratch(SHORT, HALO, (512, 128)), count=7, flops=4_000_000)(
            body, up1, down1, own0, halo0, own1, halo1
        )

    body, own, up1, down1, up2, down2 = joint_exchange(w0, low, high, False)
    x0, x1 = near(body, up1, down1)
    m0, n0, low, high = call(
        second_kernel, [block, block, *ends], scratch(SHORT) + up_scratch[:-1] + share_scratch, count=13
    )(x0, x1, own, up1, down1, up2, down2, weight2, own0, halo0s, own1, halo1, both)
    body, own, up1, down1, up2, down2 = joint_exchange(n0, low, high, True)
    x0, x1 = near(body, up1, down1)
    r1, u1, w1, m1, n1, first, dots = call(
        third_kernel, [block] * 5 + [tile, tile], scratch(SHORT, BLOCK) + up_scratch[:-1], count=17
    )(x0, x1, own, up1, down1, up2, down2, weight2, own0, halo0s, own1, halo1, both, u0, w0, m0, n0)
    field, residual = call(
        finish_kernel, [block] * 2, scratch(BLOCK, BLOCK) + [pltpu.SemaphoreType.DMA((2, 4))], count=11, out=ANY
    )(
        first, total(dots), u0, w0, m0, n0, r1, u1, w1, m1, n1
    )
    return field, residual


def solution(mesh):
    in_specs = (P("gx", "gy", "gz"), P("gx", "gy", "gz"), P())
    out_specs = (P("gx", "gy", "gz"), P("gx", "gy", "gz"))
    return jax.shard_map(local, mesh=mesh, in_specs=in_specs, out_specs=out_specs, check_vma=False)
```
